32 devices in a mesh: dp: 8 (over z, x), mp: 4 (over y, core).
Axes of the slice: x: 2, y: 2, z: 4, core: 2. Of those that a mesh axis runs over, the one named last changes fastest.
Arguments:
- inputs: bfloat16 [24576, 768], P(('dp', 'mp')), may hold values from -6 to 6
- cotangent: bfloat16 [24576, 768], P(('dp', 'mp')), may hold values from -6 to 6
- routes: int32 [24576, 1], P('dp'), may hold values from 0 to 7; in each aligned block of 768 rows (0 to 767, 768 to 1535, ...) at most 120 rows name the same one
- domains: int32 [24], P('dp'), may hold values from 0 to 7
- domain_counts: int32 [8], replicated, may hold values from 5 to 15
- domain_weights: float32 [8], replicated, may hold values from 0.5 to 2
- keep_mask: int32 [24], P('dp'), may hold values 0 or 1
- gain_one: float32 [768], replicated, may hold values from 0.5 to 1.5
- shift_one: float32 [768], replicated, may hold values from -1.8 to 1.8
- w_qkv: bfloat16 [768, 3, 768], P(None, None, 'mp'), may hold values from -0.21875 to 0.21875
- w_proj: bfloat16 [768, 768], P('mp'), may hold values from -0.625 to 0.625
- gain_two: float32 [768], replicated, may hold values from 0.5 to 1.5
- shift_two: float32 [768], replicated, may hold values from -1.8 to 1.8
- w_router: bfloat16 [768, 8], replicated, may hold values from -0.15625 to 0.15625
- w_in: bfloat16 [8, 768, 3072], P('dp', None, 'mp'), may hold values from -0.21875 to 0.21875
- w_out: bfloat16 [8, 3072, 768], P('dp', 'mp'), may hold values from -0.21875 to 0.21875
Outputs:
- output: bfloat16 [24576, 768], P(('dp', 'mp'))
- input_grad: bfloat16 [24576, 768], P(('dp', 'mp'))
- grad_gain_one: float32 [768], replicated
- grad_shift_one: float32 [768], replicated
- grad_w_qkv: float32 [768, 3, 768], P(None, None, 'mp')
- grad_w_proj: float32 [768, 768], P('mp')
- grad_gain_two: float32 [768], replicated
- grad_shift_two: float32 [768], replicated
- grad_router: float32 [768, 8], replicated
- grad_w_in: float32 [8, 768, 3072], P('dp', None, 'mp')
- grad_w_out: float32 [8, 3072, 768], P('dp', 'mp')
The draws below stay inside these ranges and needn't reach their ends.
Inputs may be any that keep to these rules, and one draw needn't show every extreme that they name: `routes`: within the rows of one device (aligned blocks of 768 tokens) each expert is named by at most 120 rows, a bound that some block reaches.
All inputs are finite; a program needn't handle non-finite values. No bound on the sum of `keep_mask` on one device may be relied on, other than what follows from the above.
Results may differ from the reference program's by a relative error of at most 0.015.
Values may be sent and summed in bfloat16 or wider, within the bound.
A program may use at most 192 MiB of HBM per device.

```python
import math
import jax
import jax.numpy as jnp
import numpy as np
from jax import lax

D = 768
HEADS = 12
HEAD_DIM = 64
FF = 3072
LEN = 1024
DOMAINS = 8
SEQS = 24
TOKENS = 24576
TOK_DEV = 768
EXPERTS = 8
CAP = 120
N_DP = 8
N_MP = 4


def set_ends(result, rng, least, top_value):
    index_at = [jax.random.randint(jax.random.fold_in(rng, axis), (), 0, length) for axis, length in enumerate(result.shape)]
    widest = result.shape.index(max(result.shape))
    beside = index_at[:widest] + [(index_at[widest] + 1) % result.shape[widest]] + index_at[widest + 1:]
    return result.at[tuple(index_at)].set(least).at[tuple(beside)].set(top_value)


def block_scale(stream_key, extent, cuts, low, high):
    def one(axis_at, shards_of):
        draws = jax.random.uniform(jax.random.fold_in(jax.random.fold_in(stream_key, 6), axis_at), (shards_of,), jnp.float32, low / len(cuts), high / len(cuts))
        return jnp.repeat(jnp.exp(draws), extent[axis_at] // shards_of).reshape((-1,) + (1,) * (len(extent) - axis_at - 1))

    level = one(*cuts[0])
    for cut in cuts[1:]:
        level = level * one(*cut)
    return level


def assign_block(key, own, number, rows, number_of, top, limit, skew):
    sequence = jax.random.permutation(key, number_of)
    crowded, usual = shares(number_of, rows * top, limit, skew, True), shares(number_of, rows * top, limit, skew, False)
    places = jnp.arange(number_of)

    def named(lengths, rotation):
        used = int((lengths > 0).sum())
        fixed = max(1, used // 4)
        shifted = fixed + (places - fixed + rotation * (used - fixed)) % max(1, number_of - fixed)
        return jnp.zeros((number_of,), jnp.int32).at[sequence[jnp.where(places < fixed, places, shifted)]].set(jnp.asarray(lengths, jnp.int32))

    lengths = jnp.where(number % 4 == 0, named(crowded, number // 4), named(usual, number - number // 4 - 1))
    mixed = jax.random.permutation(jax.random.fold_in(own, 3), number_of)
    source_of, sink = mixed[0:number_of // 2 * 2:2], mixed[1:number_of // 2 * 2:2]
    margin = jnp.minimum(lengths[source_of] - 1, limit - lengths[sink]) // 2
    margin = jnp.where((source_of == sequence[0]) | (sink == sequence[0]) | (lengths[sink] == 0), 0, jnp.maximum(margin, 0))
    shifted = jax.random.randint(jax.random.fold_in(own, 4), (number_of // 2,), 0, 1 << 20) % (margin + 1)
    lengths = lengths.at[source_of].add(-shifted).at[sink].add(shifted)
    items = jnp.searchsorted(jnp.cumsum(lengths), jnp.arange(rows * top), side="right").astype(jnp.int32)
    table = items.reshape(top, rows).T
    table = table[jax.random.permutation(jax.random.fold_in(own, 1), rows)]
    rotation = jax.random.randint(jax.random.fold_in(own, 2), (rows, 1), 0, top)
    return jnp.take_along_axis(table, (jnp.arange(top)[None, :] + rotation) % top, axis=1)


def shares(amount, total, bound, slope, full):
    weights = [(1 << 20) // math.isqrt(standing ** slope) + 1 for standing in range(1, amount + 1)]
    largest = bound if full else min(bound, max(-(-total // amount), total * weights[0] // sum(weights)))
    least = 1 if total - largest >= amount - 1 else 0
    counts, rest = [largest] + [least] * (amount - 1), total - largest - least * (amount - 1)
    while rest > 0:
        free = [i for i in range(1, amount) if counts[i] < largest] or [i for i in range(1, amount) if counts[i] < bound]
        pool, budget = sum([weights[i] for i in free]), rest
        for i in free:
            extra = min(bound - counts[i], max(1, budget * weights[i] // pool), rest)
            counts[i] = counts[i] + extra
            rest = rest - extra
    return np.array(counts)


def centred(own_key, shape, deviation, reach, split=(), kind=jnp.bfloat16):
    level = block_scale(own_key, shape, split, -0.22, 0.18) if split else 1.0
    drawn = jax.random.normal(own_key, shape, jnp.float32) * deviation * level
    return jnp.minimum(jnp.maximum(drawn, -reach), reach).astype(kind)


def setup_inputs(seed: int = 0) -> dict:
    keys = jax.random.split(jax.random.key(seed), 17)
    inputs = centred(keys[0], (TOKENS, D), 1.0, 6.0, ((0, 32),))
    cotangent = centred(keys[1], (TOKENS, D), 1.0, 6.0, ((0, 32),))
    routes_keys = jax.random.split(jax.random.fold_in(keys[2], 1), TOKENS // TOK_DEV)
    routes_turns = jax.random.permutation(jax.random.fold_in(keys[2], 3), TOKENS // TOK_DEV)
    routes = jax.vmap(lambda own, number: assign_block(jax.random.fold_in(keys[2], 2), own, number, TOK_DEV, EXPERTS, 1, CAP, 0))(routes_keys, routes_turns).reshape((TOKENS, 1))
    domains = set_ends(jax.random.randint(keys[3], (SEQS,), 0, DOMAINS), jax.random.fold_in(keys[3], 1), 0, DOMAINS - 1).astype(jnp.int32)
    domain_counts = set_ends(jax.random.randint(keys[4], (DOMAINS,), 5, 16), jax.random.fold_in(keys[4], 1), 5, 15).astype(jnp.int32)
    domain_weights = jnp.clip(jnp.exp(jax.random.uniform(keys[5], (DOMAINS,), jnp.float32, math.log(0.5), math.log(2.0))), 0.5, 2.0)
    keep_mask = set_ends((jax.random.randint(keys[6], (SEQS,), 0, 10) < 9).astype(jnp.int32), jax.random.fold_in(keys[6], 1), 0, 1)
    gain_one = jnp.clip(1.0 + 0.1 * jax.random.normal(keys[7], (D,), jnp.float32), 0.5, 1.5)
    shift_one = centred(keys[8], (D,), 0.3, 1.8, (), jnp.float32)
    w_qkv = centred(keys[9], (D, 3, D), D ** -0.5, 0.21875, ((2, 4),))
    w_proj = centred(keys[10], (D, D), (D // 8) ** -0.5, 0.625, ((0, 4),))
    gain_two = jnp.clip(1.0 + 0.1 * jax.random.normal(keys[11], (D,), jnp.float32), 0.5, 1.5)
    shift_two = centred(keys[12], (D,), 0.3, 1.8, (), jnp.float32)
    w_router = centred(keys[13], (D, EXPERTS), (2 * D) ** -0.5, 0.15625)
    w_in = centred(keys[14], (EXPERTS, D, FF), D ** -0.5, 0.21875, ((0, 8), (2, 4)))
    w_out = centred(keys[15], (EXPERTS, FF, D), (FF // 4) ** -0.5, 0.21875, ((0, 8), (1, 4)))
    return dict(inputs=inputs, cotangent=cotangent, routes=routes, domains=domains, domain_counts=domain_counts, domain_weights=domain_weights, keep_mask=keep_mask, gain_one=gain_one, shift_one=shift_one, w_qkv=w_qkv, w_proj=w_proj, gain_two=gain_two, shift_two=shift_two, w_router=w_router, w_in=w_in, w_out=w_out)


@jax.custom_vjp
def low(v):
    return lax.optimization_barrier(v.astype(jnp.bfloat16)).astype(jnp.float32)

@jax.custom_vjp
def low_back(v):
    return v

def low_keep(v):
    return (low(v), None)

def low_pass(kept, grad):
    return (grad,)

def back_keep(v):
    return (v, None)

def back_low(kept, grad):
    return (low(grad),)
low.defvjp(low_keep, low_pass)
low_back.defvjp(back_keep, back_low)
norm_epsilon = 1e-05
count_scale = 10.0
masked_score = -1e+30
highest = lax.Precision.HIGHEST

def layer_norm(features, gain_vec, shift_vec):
    centre = features - lax.optimization_barrier(jnp.mean(features, axis=-1, keepdims=True))
    spread = lax.optimization_barrier(jnp.mean(centre * centre, axis=-1, keepdims=True))
    return centre * lax.rsqrt(spread + norm_epsilon) * gain_vec + shift_vec

def attend_sequence(packed):
    queries = jnp.transpose(packed[:, 0], (1, 0, 2))
    keys_all = jnp.transpose(packed[:, 1], (1, 0, 2))
    values_all = jnp.transpose(packed[:, 2], (1, 0, 2))
    raw_scores = jnp.einsum('hqd,hkd->hqk', queries, keys_all, precision=highest) * HEAD_DIM ** (-0.5)
    scores = low_back(raw_scores)
    places = jnp.arange(LEN)
    scores = jnp.where(places[None, :, None] >= places[None, None, :], scores, masked_score)
    largest = lax.optimization_barrier(jnp.max(scores, axis=-1, keepdims=True))
    expo_vals = jnp.exp(scores - largest)
    attn_probs = expo_vals / lax.optimization_barrier(jnp.sum(expo_vals, axis=-1, keepdims=True))
    mixture = jnp.einsum('hqk,hkd->qhd', low(attn_probs), values_all, precision=highest)
    return mixture.reshape(LEN, HEADS * HEAD_DIM)

def expert_apply(operands):
    rows_in, weight_in, weight_out = operands
    pre_act = low_back(jnp.dot(rows_in, weight_in, precision=highest))
    activity = low(jax.nn.gelu(pre_act, approximate=True))
    return low_back(low(jnp.dot(activity, weight_out, precision=highest)))

def shard_ranks(chosen):
    onehot_int = (chosen[:, :, None] == jnp.arange(EXPERTS, dtype=jnp.int32)[None, None, :]).astype(jnp.int32)
    running = jnp.cumsum(onehot_int, axis=1)
    return lax.optimization_barrier(jnp.sum(running * onehot_int, axis=2)) - 1

def block_forward(inputs, gain_one, shift_one, w_qkv, w_proj, gain_two, shift_two, w_router, w_in, w_out, routes):
    normed_one = low(layer_norm(inputs, gain_one, shift_one))
    projected = jnp.einsum('td,dcf->tcf', normed_one, w_qkv, precision=highest)
    projected = low_back(low(projected))
    packed = projected.reshape(SEQS, LEN, 3, HEADS, HEAD_DIM)
    attended = lax.map(jax.checkpoint(attend_sequence), packed).reshape(TOKENS, D)
    attended = low_back(low(attended))
    branch = low_back(jnp.dot(attended, w_proj, precision=highest))
    hidden = inputs + branch
    normed_two = low(layer_norm(hidden, gain_two, shift_two))
    logits = low_back(jnp.dot(normed_two, w_router, precision=highest))
    chosen = routes[:, 0]
    picked = chosen[:, None] == jnp.arange(EXPERTS, dtype=jnp.int32)[None, :]
    gate_value = jax.nn.sigmoid(lax.optimization_barrier(jnp.sum(jnp.where(picked, logits, 0.0), axis=1)))
    shards = N_DP * N_MP
    rank_within = shard_ranks(chosen.reshape(shards, TOK_DEV)).reshape(TOKENS)
    source = jnp.arange(TOKENS, dtype=jnp.int32) // TOK_DEV
    slot_index = (chosen * shards + source) * CAP + rank_within
    buffer = jnp.zeros((EXPERTS * shards * CAP, D), jnp.float32).at[slot_index].set(normed_two)
    buffer = low_back(buffer)
    results = lax.map(jax.checkpoint(expert_apply), (buffer.reshape(EXPERTS, shards * CAP, D), w_in, w_out))
    returned = jnp.take(results.reshape(EXPERTS * shards * CAP, D), slot_index, axis=0)
    return hidden + gate_value[:, None] * returned

def reference(inputs, cotangent, routes, domains, domain_counts, domain_weights, keep_mask, gain_one, shift_one, w_qkv, w_proj, gain_two, shift_two, w_router, w_in, w_out):
    params = (inputs.astype(jnp.float32), gain_one.astype(jnp.float32), shift_one.astype(jnp.float32), w_qkv.astype(jnp.float32), w_proj.astype(jnp.float32), gain_two.astype(jnp.float32), shift_two.astype(jnp.float32), w_router.astype(jnp.float32), w_in.astype(jnp.float32), w_out.astype(jnp.float32))

    def forward(*operands):
        return block_forward(*operands, routes)
    output, pullback = jax.vjp(forward, *params)
    factor = keep_mask.astype(jnp.float32) * domain_weights[domains] * count_scale / domain_counts[domains].astype(jnp.float32)
    scaled = cotangent.astype(jnp.float32) * jnp.repeat(factor, LEN)[:, None]
    gradients = pullback(scaled)
    return (output.astype(jnp.bfloat16), gradients[0].astype(jnp.bfloat16), gradients[1], gradients[2], gradients[3], gradients[4], gradients[5], gradients[6], gradients[7], gradients[8], gradients[9])
```

```python
import jax
import jax.numpy as jnp
from jax import lax
from jax.experimental import pallas as pl
from jax.experimental.pallas import tpu as pltpu
from jax.sharding import PartitionSpec as P

HEAD_DIM = 64
LEN = 1024
BLOCK = 256
HALF = LEN // 2

norm_epsilon = 1e-05
count_scale = 10.0
masked_score = -1e30

f32 = jnp.float32
bf16 = jnp.bfloat16
NT = (((1,), (1,)), ((), ()))
NN = (((1,), (0,)), ((), ()))
TN = (((0,), (0,)), ((), ()))

ACROSS = [(0, 2), (2, 0), (1, 3), (3, 1)]
BESIDE = [(0, 1), (1, 0), (2, 3), (3, 2)]
LATER = [(0, 2), (1, 3)]
EARLIER = [(2, 0), (3, 1)]


def dot(left, right, dims=NN):
    return lax.dot_general(left, right, dims, preferred_element_type=f32)


def norm_forward(features, gain_vec, shift_vec):
    centre = features - jnp.mean(features, axis=-1, keepdims=True)
    inverse = lax.rsqrt(jnp.mean(centre * centre, axis=-1, keepdims=True) + norm_epsilon)
    scaled = centre * inverse
    return (scaled * gain_vec + shift_vec, scaled, inverse)


def norm_backward(d_normed, scaled, inverse, gain_vec):
    d_scaled = d_normed * gain_vec
    correction = jnp.mean(d_scaled, axis=-1, keepdims=True) + scaled * jnp.mean(
        d_scaled * scaled, axis=-1, keepdims=True
    )
    return (
        inverse * (d_scaled - correction),
        jnp.sum(d_normed * scaled, axis=0),
        jnp.sum(d_normed, axis=0),
    )


def plan(chip, run):
    second = chip == 1
    for whole, (here, there) in enumerate([(0, 2), (1, 3), (2, 0), (3, 1)]):
        run(pl.multiple_of(jnp.where(second, there, here) * BLOCK, BLOCK), whole)

    @pl.when(chip == 0)
    def _():
        run(4 * BLOCK, 0)
        run(5 * BLOCK, 1)

    @pl.when(chip == 1)
    def _():
        run(4 * BLOCK, 2)
        run(5 * BLOCK, 3)


def mask_diagonal(scores, whole):
    first = lax.broadcasted_iota(jnp.int32, (BLOCK, BLOCK), 0)
    second = lax.broadcasted_iota(jnp.int32, (BLOCK, BLOCK), 1)
    last = jnp.where(first <= second, scores[whole * BLOCK :], masked_score)
    if not whole:
        return last
    return jnp.concatenate([scores[: whole * BLOCK], last], axis=0)


def attend_kernel(chip_ref, q_ref, k_ref, v_ref, ke_ref, ve_ref, o_ref, l_ref, keys, values):
    chip = chip_ref[0]
    lane = lax.broadcasted_iota(jnp.int32, (1, 128), 1)
    row = lax.broadcasted_iota(jnp.int32, (128, 1), 0)
    keys[0:HALF] = ke_ref[...]
    keys[HALF:] = k_ref[...]
    values[:, 0:HALF] = ve_ref[...].T
    values[:, HALF:] = v_ref[...].T

    def run(first, whole):
        span = (whole + 1) * BLOCK
        start = pl.multiple_of(first + HALF - whole * BLOCK, BLOCK)
        queries = q_ref[pl.ds(first, BLOCK)] * bf16(0.125)
        near = keys[pl.ds(start, span)]
        mixed = values[:, pl.ds(start, span)]
        parts = []
        for head in range(2):
            own = jnp.where((lane // HEAD_DIM) == head, queries, bf16(0))
            scores = mask_diagonal(dot(near, own, NT), whole)
            largest = jnp.max(scores, axis=0, keepdims=True)
            expo = jnp.exp(scores - largest)
            total = jnp.sum(expo, axis=0, keepdims=True)
            parts.append(dot(mixed, expo.astype(bf16)) / total)
            l_ref[head : head + 1, pl.ds(first, BLOCK)] = largest + jnp.log(total)
        joined = jnp.where(row < HEAD_DIM, parts[0], parts[1])
        o_ref[pl.ds(first, BLOCK)] = joined.T.astype(bf16)

    plan(chip, run)


def column_block(rows, offset):
    return pl.BlockSpec((rows, 128), lambda pair: (0, offset + pair))


def attend(chip, qkv, ext):
    rows = qkv.shape[0]
    pairs = qkv.shape[1] // 384
    return pl.pallas_call(
        attend_kernel,
        grid=(pairs,),
        in_specs=[
            pl.BlockSpec(memory_space=pltpu.SMEM),
            column_block(rows, 0),
            column_block(rows, pairs),
            column_block(rows, 2 * pairs),
            column_block(HALF, 0),
            column_block(HALF, pairs),
        ],
        out_specs=[
            column_block(rows, 0),
            pl.BlockSpec((None, 8, rows), lambda pair: (pair, 0, 0)),
        ],
        out_shape=[
            jax.ShapeDtypeStruct((rows, pairs * 128), bf16),
            jax.ShapeDtypeStruct((pairs, 8, rows), f32),
        ],
        scratch_shapes=[
            pltpu.VMEM((HALF + rows, 128), bf16),
            pltpu.VMEM((128, HALF + rows), bf16),
        ],
        compiler_params=pltpu.CompilerParams(vmem_limit_bytes=48 * 2**20),
        cost_estimate=pl.CostEstimate(flops=16 * 10**9, bytes_accessed=8 * 10**6, transcendentals=8 * 10**6),
        name="attend",
    )(chip, qkv, qkv, qkv, ext, ext)


def attend_back_kernel(
    chip_ref, q_ref, k_ref, v_ref, ke_ref, ve_ref, d_ref, o_ref, l_ref,
    dq_ref, dk_ref, dv_ref, dke_ref, dve_ref, keys, values, d_keys, d_values,
):
    chip = chip_ref[0]
    lane = lax.broadcasted_iota(jnp.int32, (1, 128), 1)
    keys[0:HALF] = ke_ref[...]
    keys[HALF:] = k_ref[...]
    values[0:HALF] = ve_ref[...]
    values[HALF:] = v_ref[...]
    d_keys[...] = jnp.zeros_like(d_keys)
    d_values[...] = jnp.zeros_like(d_values)

    def run(first, whole):
        span = (whole + 1) * BLOCK
        start = pl.multiple_of(first + HALF - whole * BLOCK, BLOCK)
        queries = q_ref[pl.ds(first, BLOCK)] * bf16(0.125)
        d_mixed = d_ref[pl.ds(first, BLOCK)]
        near = keys[pl.ds(start, span)]
        near_values = values[pl.ds(start, span)]
        product = (d_mixed.astype(f32) * o_ref[pl.ds(first, BLOCK)].astype(f32)).T
        dq = dk = dv = 0.0
        for head in range(2):
            here = (lane // HEAD_DIM) == head
            own = jnp.where(here, queries, bf16(0))
            d_own = jnp.where(here, d_mixed, bf16(0))
            delta = jnp.sum(product[HEAD_DIM * head : HEAD_DIM * (head + 1)], axis=0, keepdims=True)
            scores = mask_diagonal(dot(near, own, NT), whole)
            probs = jnp.exp(scores - l_ref[head : head + 1, pl.ds(first, BLOCK)])
            d_probs = dot(near_values, d_own, NT)
            d_scores = (probs * (d_probs - delta)).astype(bf16)
            dv = dv + dot(probs.astype(bf16), d_own)
            dk = dk + dot(d_scores, own)
            dq = dq + dot(d_scores, jnp.where(here, near, bf16(0)), TN)
        dq_ref[pl.ds(first, BLOCK)] = (dq * 0.125).astype(bf16)
        d_keys[pl.ds(start, span)] += dk
        d_values[pl.ds(start, span)] += dv

    plan(chip, run)
    dk_ref[...] = d_keys[HALF:]
    dv_ref[...] = d_values[HALF:]
    dke_ref[...] = d_keys[:HALF].astype(bf16)
    dve_ref[...] = d_values[:HALF].astype(bf16)


def attend_back(chip, qkv, ext, d_mixed, mixed, log_total):
    rows = qkv.shape[0]
    pairs = qkv.shape[1] // 384
    return pl.pallas_call(
        attend_back_kernel,
        grid=(pairs,),
        in_specs=[
            pl.BlockSpec(memory_space=pltpu.SMEM),
            column_block(rows, 0),
            column_block(rows, pairs),
            column_block(rows, 2 * pairs),
            column_block(HALF, 0),
            column_block(HALF, pairs),
            column_block(rows, 0),
            column_block(rows, 0),
            pl.BlockSpec((None, 8, rows), lambda pair: (pair, 0, 0)),
        ],
        out_specs=[column_block(rows, 0)] * 3 + [column_block(HALF, 0)] * 2,
        out_shape=[
            jax.ShapeDtypeStruct((rows, pairs * 128), bf16),
            jax.ShapeDtypeStruct((rows, pairs * 128), f32),
            jax.ShapeDtypeStruct((rows, pairs * 128), f32),
            jax.ShapeDtypeStruct((HALF, pairs * 128), bf16),
            jax.ShapeDtypeStruct((HALF, pairs * 128), bf16),
        ],
        scratch_shapes=[
            pltpu.VMEM((HALF + rows, 128), bf16),
            pltpu.VMEM((HALF + rows, 128), bf16),
            pltpu.VMEM((HALF + rows, 128), f32),
            pltpu.VMEM((HALF + rows, 128), f32),
        ],
        compiler_params=pltpu.CompilerParams(vmem_limit_bytes=56 * 2**20),
        cost_estimate=pl.CostEstimate(flops=20 * 10**9, bytes_accessed=12 * 10**6, transcendentals=8 * 10**6),
        name="attend_back",
    )(chip, qkv, qkv, qkv, ext, ext, d_mixed, mixed, log_total)


def across(value):
    return lax.ppermute(value, "mp", ACROSS)


def beside(value):
    return lax.ppermute(value, "mp", BESIDE)


def in_order(first, own, other):
    return jnp.where(first, own, other), jnp.where(first, other, own)


def exchange(rows):
    return lax.all_to_all(rows, "dp", split_axis=0, concat_axis=0, tiled=True)


def gelu_parts(pre):
    scale = 0.7978845608028654
    inner = jnp.tanh(scale * (pre + 0.044715 * pre * pre * pre))
    value = 0.5 * pre * (1.0 + inner)
    slope = 0.5 * (1.0 + inner) + 0.5 * pre * (1.0 - inner * inner) * scale * (
        1.0 + 3.0 * 0.044715 * pre * pre
    )
    return value, slope


def shards(
    inputs, cotangent, routes, domains, domain_counts, domain_weights, keep_mask, gain_one, shift_one,
    w_qkv, w_proj, gain_two, shift_two, w_router, w_in, w_out,
):
    tok, width = inputs.shape
    experts = w_router.shape[1]
    cap = max(2, tok * 5 // (4 * experts))
    slots = (cap + 16) // 16 * 16
    mp_index = lax.axis_index("mp")
    chip, core = mp_index // 2, mp_index % 2
    on_first_chip, on_first_core = chip == 0, core == 0
    expert = lax.axis_index("dp")
    seq_count = routes.shape[0] // LEN

    own_routes = lax.dynamic_slice_in_dim(routes[:, 0], mp_index * tok, tok, 0)
    expert_ids = jnp.arange(experts, dtype=jnp.int32)
    picked = own_routes[:, None] == expert_ids[None, :]
    places = jnp.arange(tok, dtype=jnp.int32)
    earlier = (places[:, None] > places[None, :]).astype(bf16)
    counts = dot(earlier, picked.astype(bf16))
    rank = jnp.sum(jnp.where(picked, counts, 0.0), axis=1).astype(jnp.int32)
    own_slots = own_routes * slots + rank
    slot_ids = jnp.arange(experts * slots, dtype=jnp.int32)
    placed = own_slots[None, :] == slot_ids[:, None]
    placing = placed.astype(bf16)

    seq_ids = jnp.arange(seq_count, dtype=jnp.int32)
    domain_ids = jnp.arange(domain_weights.shape[0], dtype=jnp.int32)
    same_domain = domains[:, None] == domain_ids[None, :]
    seq_weight = jnp.sum(jnp.where(same_domain, domain_weights[None, :], 0.0), axis=1)
    seq_counts = jnp.sum(jnp.where(same_domain, domain_counts[None, :], 0), axis=1).astype(f32)
    factor = keep_mask.astype(f32) * seq_weight * count_scale / seq_counts
    row_seq = (mp_index * tok + places) // LEN
    row_factor = jnp.sum(jnp.where(row_seq[:, None] == seq_ids[None, :], factor[None, :], 0.0), axis=1)
    slot_factor = jnp.sum(jnp.where(placed, row_factor[None, :], 0.0), axis=1).reshape(experts, slots)
    high = slot_factor.astype(bf16)
    low = (slot_factor - high.astype(f32)).astype(bf16)
    cot_rows = dot(placing, cotangent).astype(bf16).reshape(experts, slots, width)
    cot_rows = cot_rows.at[:, cap, :slots].set(high).at[:, cap, width // 2 : width // 2 + slots].set(low)
    cot_rows = exchange(cot_rows)

    inputs_wide = inputs.astype(f32)
    normed_one, scaled_one, inverse_one = norm_forward(inputs_wide, gain_one, shift_one)
    normed_one = normed_one.astype(bf16)
    normed_chip = jnp.concatenate(in_order(on_first_core, normed_one, beside(normed_one)))
    w_own = jnp.transpose(w_qkv, (1, 2, 0))
    features = 2 * w_own.shape[1]
    w_heads = jnp.concatenate(in_order(on_first_chip, w_own, across(w_own)), axis=1)
    w_heads = w_heads.reshape(3 * features, width)
    qkv = dot(normed_chip, w_heads, NT).astype(bf16)
    ext = lax.ppermute(qkv[-HALF:, features:], "mp", LATER)
    chip_scalar = chip.astype(jnp.int32).reshape(1)
    mixed, log_total = attend(chip_scalar, qkv, ext)

    proj_own = jnp.concatenate(in_order(on_first_chip, w_proj, across(w_proj)))
    proj_other = beside(proj_own)
    mixed_own = lax.dynamic_slice_in_dim(mixed, core * tok, tok, 0)
    mixed_other = beside(lax.dynamic_slice_in_dim(mixed, (1 - core) * tok, tok, 0))
    hidden = inputs_wide + dot(mixed_own, proj_own) + dot(mixed_other, proj_other)
    normed_two, scaled_two, inverse_two = norm_forward(hidden, gain_two, shift_two)
    normed_two = normed_two.astype(bf16)
    expert_in = exchange(dot(placing, normed_two).astype(bf16).reshape(experts, slots, width))
    expert_in = expert_in.reshape(experts * slots, width)

    in_across, out_across = across(w_in[0]), across(w_out[0])
    weights_in = [w_in[0], in_across, beside(w_in[0]), beside(in_across)]
    weights_out = [w_out[0], out_across, beside(w_out[0]), beside(out_across)]

    cot_factor = cot_rows[:, cap, :slots].astype(f32) + cot_rows[
        :, cap, width // 2 : width // 2 + slots
    ].astype(f32)
    cot_factor = jnp.where(jnp.arange(slots)[None, :] < cap, cot_factor, 0.0).reshape(-1, 1)
    d_result = cot_rows.reshape(experts * slots, width).astype(f32) * cot_factor
    router_row = lax.dynamic_slice_in_dim(w_router.T, expert, 1, 0).astype(f32)
    gate = jax.nn.sigmoid(jnp.sum(expert_in.astype(f32) * router_row, axis=1, keepdims=True))
    d_out = (gate * d_result).astype(bf16)
    parts = [gelu_parts(dot(expert_in, w)) for w in weights_in]
    acts = [value.astype(bf16) for value, _ in parts]
    result = sum(dot(act, w) for act, w in zip(acts, weights_out))
    d_pres = [
        (dot(d_out, w, NT) * slope).astype(bf16) for (_, slope), w in zip(parts, weights_out)
    ]
    d_gate = jnp.sum(d_result * result, axis=1, keepdims=True)
    d_logit = (d_gate * gate * (1.0 - gate)).astype(bf16).astype(f32)
    d_expert_in = sum(dot(d_pre, w, NT) for d_pre, w in zip(d_pres, weights_in)) + d_logit * router_row
    returned = exchange((gate * result).astype(bf16).reshape(experts, slots, width))
    d_returned = exchange(d_expert_in.astype(bf16).reshape(experts, slots, width))
    grads_in = [dot(expert_in, d_pre, TN) for d_pre in d_pres]
    grads_out = [dot(act, d_out, TN) for act in acts]
    router_grad = jnp.sum(expert_in.astype(f32) * d_logit, axis=0)

    def collect(grads):
        here = grads[0] + beside(grads[2].astype(bf16)).astype(f32)
        there = grads[1] + beside(grads[3].astype(bf16)).astype(f32)
        return here + across(there.astype(bf16)).astype(f32)

    grad_w_in, grad_w_out = collect(grads_in), collect(grads_out)

    output = hidden + dot(placing, returned.reshape(experts * slots, width), TN)
    d_output = cotangent.astype(f32) * row_factor[:, None]
    d_norm_two = dot(placing, d_returned.reshape(experts * slots, width), TN)
    d_back_two, grad_gain_two, grad_shift_two = norm_backward(
        d_norm_two, scaled_two, inverse_two, gain_two
    )
    d_hidden = d_output + d_back_two

    d_branch = d_hidden.astype(bf16)
    d_branch = jnp.concatenate(in_order(on_first_core, d_branch, beside(d_branch)))
    grad_proj = dot(mixed, d_branch, TN)
    d_mixed = dot(d_branch, proj_own, NT).astype(bf16)
    dq, dk, dv, dk_ext, dv_ext = attend_back(chip_scalar, qkv, ext, d_mixed, mixed, log_total)
    ext_back = lax.ppermute(jnp.concatenate([dk_ext, dv_ext], axis=1), "mp", EARLIER).astype(f32)
    d_kv = jnp.concatenate([dk, dv], axis=1)
    d_kv = jnp.concatenate([d_kv[:-HALF], d_kv[-HALF:] + ext_back])
    d_qkv = jnp.concatenate([dq, d_kv.astype(bf16)], axis=1)
    grad_heads = dot(d_qkv, normed_chip, TN).reshape(3, features, width)
    d_norm_chip = dot(d_qkv, w_heads)
    d_norm_own = lax.dynamic_slice_in_dim(d_norm_chip, core * tok, tok, 0)
    d_norm_other = lax.dynamic_slice_in_dim(d_norm_chip, (1 - core) * tok, tok, 0).astype(bf16)
    d_norm_one = d_norm_own + beside(d_norm_other).astype(f32)
    d_back_one, grad_gain_one, grad_shift_one = norm_backward(
        d_norm_one, scaled_one, inverse_one, gain_one
    )
    input_grad = d_hidden + d_back_one

    def own_and_other(grads, axis):
        first, second = jnp.split(grads, 2, axis=axis)
        return in_order(on_first_chip, first, second)

    heads_own, heads_other = own_and_other(grad_heads, 1)
    proj_grad_own, proj_grad_other = own_and_other(grad_proj, 0)
    heads_sum = heads_own + across(heads_other.astype(bf16)).astype(f32)
    proj_sum = proj_grad_own + across(proj_grad_other.astype(bf16)).astype(f32)
    sums = jnp.concatenate([heads_sum.reshape(-1, width), proj_sum]).astype(bf16)
    groups = experts
    pieces = exchange(sums.reshape(groups, -1, width))
    piece = jnp.sum(pieces.astype(f32), axis=0).astype(bf16)
    sums = lax.all_gather(piece, "dp", axis=0, tiled=True).astype(f32)
    grad_w_qkv = jnp.transpose(sums[: -w_proj.shape[0]].reshape(w_own.shape), (2, 0, 1))
    grad_w_proj = sums[-w_proj.shape[0] :]
    own_expert = (expert_ids == expert)[:, None]
    small = jnp.concatenate(
        [
            jnp.stack([grad_gain_one, grad_shift_one, grad_gain_two, grad_shift_two]),
            jnp.where(own_expert, router_grad[None, :], 0.0),
        ]
    )
    small = lax.psum(small, ("dp", "mp"))
    return (
        output.astype(bf16),
        input_grad.astype(bf16),
        small[0],
        small[1],
        grad_w_qkv,
        grad_w_proj,
        small[2],
        small[3],
        small[4:].T,
        grad_w_in[None],
        grad_w_out[None],
    )


def solution(mesh):
    tokens, group = P(("dp", "mp"), None), P("dp")
    return jax.shard_map(
        shards,
        mesh=mesh,
        in_specs=(
            tokens, tokens, P("dp", None), group, P(), P(), group, P(), P(),
            P(None, None, "mp"), P("mp", None), P(), P(), P(),
            P("dp", None, "mp"), P("dp", "mp", None),
        ),
        out_specs=(
            tokens, tokens, P(), P(), P(None, None, "mp"), P("mp", None), P(), P(), P(),
            P("dp", None, "mp"), P("dp", "mp", None),
        ),
        check_vma=False,
    )
```

```python
import functools

import jax
import jax.numpy as jnp
from jax import lax
from jax.experimental import pallas as pl
from jax.experimental.pallas import tpu as pltpu
from jax.sharding import PartitionSpec as P

HEAD_DIM = 64
LEN = 1024
BLOCK = 256
HALF = LEN // 2

norm_epsilon = 1e-05
count_scale = 10.0
masked_score = -1e30

f32 = jnp.float32
bf16 = jnp.bfloat16
MESH = pl.DeviceIdType.MESH
NT = (((1,), (1,)), ((), ()))
NN = (((1,), (0,)), ((), ()))
TN = (((0,), (0,)), ((), ()))

ACROSS = [(0, 2), (2, 0), (1, 3), (3, 1)]
BESIDE = [(0, 1), (1, 0), (2, 3), (3, 2)]
LATER = [(0, 2), (1, 3)]
EARLIER = [(2, 0), (3, 1)]


def dot(left, right, dims=NN):
    return lax.dot_general(left, right, dims, preferred_element_type=f32)


def norm_forward(features, gain_vec, shift_vec):
    centre = features - jnp.mean(features, axis=-1, keepdims=True)
    inverse = lax.rsqrt(jnp.mean(centre * centre, axis=-1, keepdims=True) + norm_epsilon)
    scaled = centre * inverse
    return (scaled * gain_vec + shift_vec, scaled, inverse)


def norm_backward(d_normed, scaled, inverse, gain_vec):
    d_scaled = d_normed * gain_vec
    correction = jnp.mean(d_scaled, axis=-1, keepdims=True) + scaled * jnp.mean(
        d_scaled * scaled, axis=-1, keepdims=True
    )
    return (
        inverse * (d_scaled - correction),
        jnp.sum(d_normed * scaled, axis=0),
        jnp.sum(d_normed, axis=0),
    )


def plan(chip, run):
    second = chip == 1
    for whole, (here, there) in enumerate([(0, 2), (1, 3), (2, 0), (3, 1)]):
        run(pl.multiple_of(jnp.where(second, there, here) * BLOCK, BLOCK), whole)

    @pl.when(chip == 0)
    def _():
        run(4 * BLOCK, 0)
        run(5 * BLOCK, 1)

    @pl.when(chip == 1)
    def _():
        run(4 * BLOCK, 2)
        run(5 * BLOCK, 3)


def mask_diagonal(scores, whole):
    first = lax.broadcasted_iota(jnp.int32, (BLOCK, BLOCK), 0)
    second = lax.broadcasted_iota(jnp.int32, (BLOCK, BLOCK), 1)
    last = jnp.where(first <= second, scores[whole * BLOCK :], masked_score)
    if not whole:
        return last
    return jnp.concatenate([scores[: whole * BLOCK], last], axis=0)


def attend_kernel(chip_ref, q_ref, k_ref, v_ref, ke_ref, ve_ref, o_ref, l_ref, keys, values):
    chip = chip_ref[0]
    lane = lax.broadcasted_iota(jnp.int32, (1, 128), 1)
    row = lax.broadcasted_iota(jnp.int32, (128, 1), 0)
    keys[0:HALF] = ke_ref[...]
    keys[HALF:] = k_ref[...]
    values[:, 0:HALF] = ve_ref[...].T
    values[:, HALF:] = v_ref[...].T

    def run(first, whole):
        span = (whole + 1) * BLOCK
        start = pl.multiple_of(first + HALF - whole * BLOCK, BLOCK)
        queries = q_ref[pl.ds(first, BLOCK)] * bf16(0.125)
        near = keys[pl.ds(start, span)]
        mixed = values[:, pl.ds(start, span)]
        parts = []
        for head in range(2):
            own = jnp.where((lane // HEAD_DIM) == head, queries, bf16(0))
            scores = mask_diagonal(dot(near, own, NT), whole)
            largest = jnp.max(scores, axis=0, keepdims=True)
            expo = jnp.exp(scores - largest)
            total = jnp.sum(expo, axis=0, keepdims=True)
            parts.append(dot(mixed, expo.astype(bf16)) / total)
            l_ref[head : head + 1, pl.ds(first, BLOCK)] = largest + jnp.log(total)
        joined = jnp.where(row < HEAD_DIM, parts[0], parts[1])
        o_ref[pl.ds(first, BLOCK)] = joined.T.astype(bf16)

    plan(chip, run)


def column_block(rows, offset):
    return pl.BlockSpec((rows, 128), lambda pair: (0, offset + pair))


def attend(chip, qkv, ext):
    rows = qkv.shape[0]
    pairs = qkv.shape[1] // 384
    return pl.pallas_call(
        attend_kernel,
        grid=(pairs,),
        in_specs=[
            pl.BlockSpec(memory_space=pltpu.SMEM),
            column_block(rows, 0),
            column_block(rows, pairs),
            column_block(rows, 2 * pairs),
            column_block(HALF, 0),
            column_block(HALF, pairs),
        ],
        out_specs=[
            column_block(rows, 0),
            pl.BlockSpec((None, 8, rows), lambda pair: (pair, 0, 0)),
        ],
        out_shape=[
            jax.ShapeDtypeStruct((rows, pairs * 128), bf16),
            jax.ShapeDtypeStruct((pairs, 8, rows), f32),
        ],
        scratch_shapes=[
            pltpu.VMEM((HALF + rows, 128), bf16),
            pltpu.VMEM((128, HALF + rows), bf16),
        ],
        compiler_params=pltpu.CompilerParams(vmem_limit_bytes=48 * 2**20),
        cost_estimate=pl.CostEstimate(flops=16 * 10**9, bytes_accessed=8 * 10**6, transcendentals=8 * 10**6),
        name="attend",
    )(chip, qkv, qkv, qkv, ext, ext)


def attend_back_kernel(
    chip_ref, q_ref, k_ref, v_ref, ke_ref, ve_ref, d_ref, o_ref, l_ref,
    dq_ref, dk_ref, dv_ref, dke_ref, dve_ref, keys, values, d_keys, d_values,
):
    chip = chip_ref[0]
    lane = lax.broadcasted_iota(jnp.int32, (1, 128), 1)
    keys[0:HALF] = ke_ref[...]
    keys[HALF:] = k_ref[...]
    values[0:HALF] = ve_ref[...]
    values[HALF:] = v_ref[...]
    d_keys[...] = jnp.zeros_like(d_keys)
    d_values[...] = jnp.zeros_like(d_values)

    def run(first, whole):
        span = (whole + 1) * BLOCK
        start = pl.multiple_of(first + HALF - whole * BLOCK, BLOCK)
        queries = q_ref[pl.ds(first, BLOCK)] * bf16(0.125)
        d_mixed = d_ref[pl.ds(first, BLOCK)]
        near = keys[pl.ds(start, span)]
        near_values = values[pl.ds(start, span)]
        product = (d_mixed.astype(f32) * o_ref[pl.ds(first, BLOCK)].astype(f32)).T
        dq = dk = dv = 0.0
        for head in range(2):
            here = (lane // HEAD_DIM) == head
            own = jnp.where(here, queries, bf16(0))
            d_own = jnp.where(here, d_mixed, bf16(0))
            delta = jnp.sum(product[HEAD_DIM * head : HEAD_DIM * (head + 1)], axis=0, keepdims=True)
            scores = mask_diagonal(dot(near, own, NT), whole)
            probs = jnp.exp(scores - l_ref[head : head + 1, pl.ds(first, BLOCK)])
            d_probs = dot(near_values, d_own, NT)
            d_scores = (probs * (d_probs - delta)).astype(bf16)
            dv = dv + dot(probs.astype(bf16), d_own)
            dk = dk + dot(d_scores, own)
            dq = dq + dot(d_scores, jnp.where(here, near, bf16(0)), TN)
        dq_ref[pl.ds(first, BLOCK)] = (dq * 0.125).astype(bf16)
        d_keys[pl.ds(start, span)] += dk
        d_values[pl.ds(start, span)] += dv

    plan(chip, run)
    dk_ref[...] = d_keys[HALF:]
    dv_ref[...] = d_values[HALF:]
    dke_ref[...] = d_keys[:HALF].astype(bf16)
    dve_ref[...] = d_values[:HALF].astype(bf16)


def attend_back(chip, qkv, ext, d_mixed, mixed, log_total):
    rows = qkv.shape[0]
    pairs = qkv.shape[1] // 384
    return pl.pallas_call(
        attend_back_kernel,
        grid=(pairs,),
        in_specs=[
            pl.BlockSpec(memory_space=pltpu.SMEM),
            column_block(rows, 0),
            column_block(rows, pairs),
            column_block(rows, 2 * pairs),
            column_block(HALF, 0),
            column_block(HALF, pairs),
            column_block(rows, 0),
            column_block(rows, 0),
            pl.BlockSpec((None, 8, rows), lambda pair: (pair, 0, 0)),
        ],
        out_specs=[column_block(rows, 0)] * 3 + [column_block(HALF, 0)] * 2,
        out_shape=[
            jax.ShapeDtypeStruct((rows, pairs * 128), bf16),
            jax.ShapeDtypeStruct((rows, pairs * 128), f32),
            jax.ShapeDtypeStruct((rows, pairs * 128), f32),
            jax.ShapeDtypeStruct((HALF, pairs * 128), bf16),
            jax.ShapeDtypeStruct((HALF, pairs * 128), bf16),
        ],
        scratch_shapes=[
            pltpu.VMEM((HALF + rows, 128), bf16),
            pltpu.VMEM((HALF + rows, 128), bf16),
            pltpu.VMEM((HALF + rows, 128), f32),
            pltpu.VMEM((HALF + rows, 128), f32),
        ],
        compiler_params=pltpu.CompilerParams(vmem_limit_bytes=56 * 2**20),
        cost_estimate=pl.CostEstimate(flops=20 * 10**9, bytes_accessed=12 * 10**6, transcendentals=8 * 10**6),
        name="attend_back",
    )(chip, qkv, qkv, qkv, ext, ext, d_mixed, mixed, log_total)


def across(value):
    return lax.ppermute(value, "mp", ACROSS)


def beside(value):
    return lax.ppermute(value, "mp", BESIDE)


def in_order(first, own, other):
    return jnp.where(first, own, other), jnp.where(first, other, own)


def exchange(rows):
    return lax.all_to_all(rows, "dp", split_axis=0, concat_axis=0, tiled=True)


def gelu_parts(pre):
    scale = 0.7978845608028654
    square = pre * pre
    inner = jnp.tanh(pre * (scale + (scale * 0.044715) * square))
    half = 0.5 * (1.0 + inner)
    slope = half + (0.5 * pre) * (1.0 - inner * inner) * (scale + (3.0 * scale * 0.044715) * square)
    return pre * half, slope

STAGES = 4

def expert_kernel(
    experts, slots, steps,
    rows_ref, cot_ref, factor_ref, router_ref, w_in_ref, w_out_ref, w_in_far_ref,
    back_ref, result_ref, router_grad_ref, here_in_ref, here_out_ref, there_in_ref, there_out_ref,
    x, wi, wo, d_out, act, d_pre, total, d_x, give, g_send, g_recv,
    row_send, row_recv, back_send, back_recv, w_send, w_recv, g_send_sem, g_recv_sem, local_sem,
):
    me = lax.axis_index("dp")
    mp = lax.axis_index("mp")
    beside = {"mp": mp + 1 - 2 * (mp % 2)}
    across = {"mp": (mp + 2) % 4}
    members = experts // STAGES
    span = members * slots
    own_group, own_member = me // members, me % members

    def group_of(stage):
        return 2 * ((own_group // 2 + stage // 2) % 2) + (own_group % 2 + stage % 2) % 2

    def chunk(index):
        return pl.ds(pl.multiple_of(index * slots, 16), slots)

    def group_rows(group):
        return pl.ds(pl.multiple_of(group * span, 16), span)

    barrier = pltpu.get_barrier_semaphore()

    def greet(step, carry):
        pl.semaphore_signal(barrier, inc=1, device_id={"dp": (me + step) % experts}, device_id_type=MESH)
        return carry

    lax.fori_loop(1, experts, greet, 0)
    pl.semaphore_signal(barrier, inc=1, device_id=beside, device_id_type=MESH)
    pl.semaphore_signal(barrier, inc=1, device_id=across, device_id_type=MESH)
    pl.semaphore_wait(barrier, experts + 1)

    def remote(src, dst, send, recv, device):
        return pltpu.make_async_remote_copy(
            src_ref=src, dst_ref=dst, send_sem=send, recv_sem=recv, device_id=device, device_id_type=MESH
        )

    def row_copy(target, source):
        return remote(rows_ref.at[chunk(target)], x.at[chunk(source)], row_send.at[target], row_recv.at[source], {"dp": target})

    def back_copy(target, source):
        return remote(give.at[chunk(target)], back_ref.at[chunk(source)], back_send.at[target], back_recv.at[source], {"dp": target})

    def partners(stage):
        group = group_of(stage)
        if stage == 0:
            return [group * members + (own_member + k) % members for k in range(1, members)]
        return [group * members + (own_member + k) % members for k in range(members)]

    for stage in reversed(range(STAGES)):
        for other in partners(stage):
            row_copy(other, me).start()
    own_rows = pltpu.make_async_copy(rows_ref.at[chunk(me)], x.at[chunk(me)], local_sem.at[0])
    own_in = pltpu.make_async_copy(w_in_ref, wi.at[0], local_sem.at[1])
    own_out = pltpu.make_async_copy(w_out_ref, wo.at[0], local_sem.at[2])
    far_in = pltpu.make_async_copy(w_in_far_ref, wi.at[2], local_sem.at[3])
    near_in = remote(w_in_ref, wi.at[1], w_send.at[0], w_recv.at[0], beside)
    near_out = remote(w_out_ref, wo.at[1], w_send.at[1], w_recv.at[1], beside)
    far_near_in = remote(w_in_far_ref, wi.at[3], w_send.at[2], w_recv.at[2], beside)
    far_out = remote(w_out_ref, wo.at[2], w_send.at[3], w_recv.at[3], across)
    far_near_out = remote(wo.at[2], wo.at[3], w_send.at[4], w_recv.at[4], beside)
    for copy in (own_rows, own_in, own_out, near_in, near_out, far_in, far_out, far_near_in):
        copy.start()
    router_grad_ref[...] = jnp.zeros_like(router_grad_ref)

    def prepare(stage, rows):
        features = x[rows].astype(f32)
        gate = jax.nn.sigmoid(jnp.sum(features * router_ref[...], axis=1, keepdims=True))
        d_out[rows] = (gate * (cot_ref[rows].astype(f32) * factor_ref[rows])).astype(bf16)
        total[rows] = jnp.zeros((span, x.shape[1]), f32)
        d_x[rows] = jnp.zeros((span, x.shape[1]), f32)

    def finish(stage, rows):
        features = x[rows].astype(f32)
        gate = jax.nn.sigmoid(jnp.sum(features * router_ref[...], axis=1, keepdims=True))
        value = total[rows]
        d_gate = jnp.sum(cot_ref[rows].astype(f32) * factor_ref[rows] * value, axis=1, keepdims=True)
        d_logit = (d_gate * gate * (1.0 - gate)).astype(bf16).astype(f32)
        give[rows] = (d_x[rows] + d_logit * router_ref[...]).astype(bf16)
        result_ref[rows] = (gate * value).astype(bf16)
        router_grad_ref[...] += jnp.sum(features * d_logit, axis=0, keepdims=True)

    def stage_of(step):
        return jnp.where(step < 6, step // 2, jnp.where(step < 12, (step - 6) // 2, 3))

    def step_body(step, carry):
        stage = stage_of(step)
        part = jnp.where(step < 6, step % 2, jnp.where(step < 12, 2 + step % 2, step - 12))
        rows = group_rows(group_of(stage))

        for static, at in enumerate((0, 2, 4, 12)):
            @pl.when(step == at)
            def _():
                if static == 0:
                    own_rows.wait()
                for other in partners(static):
                    row_copy(me, other).wait_recv()
        @pl.when((step == 0) | (step == 2) | (step == 4) | (step == 12))
        def _():
            prepare(stage, rows)

        @pl.when(step == 0)
        def _():
            own_in.wait()
            own_out.wait()

        @pl.when(step == 1)
        def _():
            near_in.wait_recv()
            near_out.wait_recv()

        @pl.when(step == 6)
        def _():
            far_in.wait()
            far_out.wait_recv()
            far_near_out.start()

        @pl.when(step == 7)
        def _():
            far_near_in.wait_recv()
            far_near_out.wait_recv()

        pre = dot(x[rows], wi[part])
        value, slope = gelu_parts(pre)
        value = value.astype(bf16)
        act[part, rows] = value
        total[rows] += dot(value, wo[part])
        d_value = (dot(d_out[rows], wo[part], NT) * slope).astype(bf16)
        d_pre[part, rows] = d_value
        d_x[rows] += dot(d_value, wi[part], NT)

        @pl.when((step == 7) | (step == 9) | (step == 11) | (step == 15))
        def _():
            finish(stage, rows)

        for static, at in enumerate((7, 9, 11, 15)):
            @pl.when(step == at)
            def _():
                for other in partners(static):
                    back_copy(other, me).start()
        return carry

    lax.fori_loop(0, 16, step_body, 0)
    own_back = pltpu.make_async_copy(give.at[chunk(me)], back_ref.at[chunk(me)], local_sem.at[4])
    own_back.start()

    def grad_copy(index):
        return remote(outgoing[index], g_recv.at[index], g_send_sem.at[index], g_recv_sem.at[index], beside)

    kept = pl.ds(0, x.shape[1])
    outgoing = [g_send, act.at[3, kept], d_pre.at[3, kept], act.at[1, kept]]
    for index, part in enumerate((3, 1)):
        outgoing[2 * index][...] = dot(act[part], d_out[...], TN).astype(bf16)
        grad_copy(2 * index).start()
        outgoing[2 * index + 1][...] = dot(x[...], d_pre[part], TN).astype(bf16)
        grad_copy(2 * index + 1).start()
    grad = dot(act[2], d_out[...], TN)
    grad_copy(0).wait_recv()
    there_out_ref[...] = (grad + g_recv[0].astype(f32)).astype(bf16)
    grad = dot(x[...], d_pre[2], TN)
    grad_copy(1).wait_recv()
    there_in_ref[...] = (grad + g_recv[1].astype(f32)).astype(bf16)
    grad = dot(act[0], d_out[...], TN)
    grad_copy(2).wait_recv()
    here_out_ref[...] = grad + g_recv[2].astype(f32)
    grad = dot(x[...], d_pre[0], TN)
    grad_copy(3).wait_recv()
    here_in_ref[...] = grad + g_recv[3].astype(f32)

    own_back.wait()
    for stage in range(STAGES):
        for other in partners(stage):
            back_copy(me, other).wait_recv()
            back_copy(other, me).wait_send()
            row_copy(other, me).wait_send()
    for copy in (near_in, near_out, far_near_in, far_out, far_near_out):
        copy.wait_send()
    for index in range(4):
        grad_copy(index).wait_send()


def run_expert(rows, cot_rows, factor, router_row, w_in, w_out, w_in_far, experts):
    total, width = rows.shape
    slots = total // experts
    hidden = w_in.shape[1]
    anyspace, vmem = pl.BlockSpec(memory_space=pl.ANY), pl.BlockSpec(memory_space=pltpu.VMEM)
    dma = pltpu.SemaphoreType.DMA
    return pl.pallas_call(
        functools.partial(expert_kernel, experts, slots, 0),
        in_specs=[anyspace, vmem, vmem, vmem, anyspace, anyspace, anyspace],
        out_specs=[vmem] * 7,
        out_shape=[
            jax.ShapeDtypeStruct((total, width), bf16),
            jax.ShapeDtypeStruct((total, width), bf16),
            jax.ShapeDtypeStruct((1, width), f32),
            jax.ShapeDtypeStruct((width, hidden), f32),
            jax.ShapeDtypeStruct((hidden, width), f32),
            jax.ShapeDtypeStruct((width, hidden), bf16),
            jax.ShapeDtypeStruct((hidden, width), bf16),
        ],
        scratch_shapes=[
            pltpu.VMEM((total, width), bf16),
            pltpu.VMEM((4, width, hidden), bf16),
            pltpu.VMEM((4, hidden, width), bf16),
            pltpu.VMEM((total, width), bf16),
            pltpu.VMEM((4, total, hidden), bf16),
            pltpu.VMEM((4, total, hidden), bf16),
            pltpu.VMEM((total, width), f32),
            pltpu.VMEM((total, width), f32),
            pltpu.VMEM((total, width), bf16),
            pltpu.VMEM((width, width), bf16),
            pltpu.VMEM((4, width, width), bf16),
            dma((experts,)), dma((experts,)), dma((experts,)), dma((experts,)),
            dma((5,)), dma((5,)), dma((4,)), dma((4,)), dma((5,)),
        ],
        compiler_params=pltpu.CompilerParams(
            collective_id=1, has_side_effects=True, vmem_limit_bytes=60 * 2**20
        ),
        cost_estimate=pl.CostEstimate(flops=30 * 10**9, bytes_accessed=40 * 10**6, transcendentals=3 * 10**6),
        name="expert",
    )(rows, cot_rows, factor, router_row, w_in, w_out, w_in_far)


def shards(
    inputs, cotangent, routes, domains, domain_counts, domain_weights, keep_mask, gain_one, shift_one,
    w_qkv, w_proj, gain_two, shift_two, w_router, w_in, w_out,
):
    tok, width = inputs.shape
    experts = w_router.shape[1]
    cap = max(2, tok * 5 // (4 * experts))
    slots = (cap + 16) // 16 * 16
    mp_index = lax.axis_index("mp")
    chip, core = mp_index // 2, mp_index % 2
    on_first_chip, on_first_core = chip == 0, core == 0
    expert = lax.axis_index("dp")
    seq_count = routes.shape[0] // LEN

    own_routes = lax.dynamic_slice_in_dim(routes[:, 0], mp_index * tok, tok, 0)
    expert_ids = jnp.arange(experts, dtype=jnp.int32)
    picked = own_routes[:, None] == expert_ids[None, :]
    places = jnp.arange(tok, dtype=jnp.int32)
    earlier = (places[:, None] > places[None, :]).astype(bf16)
    counts = dot(earlier, picked.astype(bf16))
    rank = jnp.sum(jnp.where(picked, counts, 0.0), axis=1).astype(jnp.int32)
    own_slots = own_routes * slots + rank
    slot_ids = jnp.arange(experts * slots, dtype=jnp.int32)
    placed = own_slots[None, :] == slot_ids[:, None]
    placing = placed.astype(bf16)

    seq_ids = jnp.arange(seq_count, dtype=jnp.int32)
    domain_ids = jnp.arange(domain_weights.shape[0], dtype=jnp.int32)
    same_domain = domains[:, None] == domain_ids[None, :]
    seq_weight = jnp.sum(jnp.where(same_domain, domain_weights[None, :], 0.0), axis=1)
    seq_counts = jnp.sum(jnp.where(same_domain, domain_counts[None, :], 0), axis=1).astype(f32)
    factor = keep_mask.astype(f32) * seq_weight * count_scale / seq_counts
    row_seq = (mp_index * tok + places) // LEN
    row_factor = jnp.sum(jnp.where(row_seq[:, None] == seq_ids[None, :], factor[None, :], 0.0), axis=1)
    slot_factor = jnp.sum(jnp.where(placed, row_factor[None, :], 0.0), axis=1).reshape(experts, slots)
    high = slot_factor.astype(bf16)
    low = (slot_factor - high.astype(f32)).astype(bf16)
    cot_rows = dot(placing, cotangent).astype(bf16).reshape(experts, slots, width)
    cot_rows = cot_rows.at[:, cap, :slots].set(high).at[:, cap, width // 2 : width // 2 + slots].set(low)
    cot_rows = exchange(cot_rows)

    inputs_wide = inputs.astype(f32)
    normed_one, scaled_one, inverse_one = norm_forward(inputs_wide, gain_one, shift_one)
    normed_one = normed_one.astype(bf16)
    normed_chip = jnp.concatenate(in_order(on_first_core, normed_one, beside(normed_one)))
    w_own = jnp.transpose(w_qkv, (1, 2, 0))
    features = 2 * w_own.shape[1]
    w_heads = jnp.concatenate(in_order(on_first_chip, w_own, across(w_own)), axis=1)
    w_heads = w_heads.reshape(3 * features, width)
    qkv = dot(normed_chip, w_heads, NT).astype(bf16)
    ext = lax.ppermute(qkv[-HALF:, features:], "mp", LATER)
    chip_scalar = chip.astype(jnp.int32).reshape(1)
    mixed, log_total = attend(chip_scalar, qkv, ext)

    proj_own = jnp.concatenate(in_order(on_first_chip, w_proj, across(w_proj)))
    proj_other = beside(proj_own)
    mixed_own = lax.dynamic_slice_in_dim(mixed, core * tok, tok, 0)
    mixed_other = beside(lax.dynamic_slice_in_dim(mixed, (1 - core) * tok, tok, 0))
    hidden = inputs_wide + dot(mixed_own, proj_own) + dot(mixed_other, proj_other)
    normed_two, scaled_two, inverse_two = norm_forward(hidden, gain_two, shift_two)
    normed_two = normed_two.astype(bf16)
    rows = dot(placing, normed_two).astype(bf16)

    cot_factor = cot_rows[:, cap, :slots].astype(f32) + cot_rows[
        :, cap, width // 2 : width // 2 + slots
    ].astype(f32)
    cot_factor = jnp.where(jnp.arange(slots)[None, :] < cap, cot_factor, 0.0).reshape(-1, 1)
    router_row = lax.dynamic_slice_in_dim(w_router.T, expert, 1, 0).astype(f32)
    d_returned, result, router_grad, here_in, here_out, there_in, there_out = run_expert(
        rows, cot_rows.reshape(experts * slots, width), cot_factor, router_row,
        w_in[0], w_out[0], across(w_in[0]), experts,
    )
    router_grad = router_grad[0]
    grad_w_out = here_out + across(there_out).astype(f32)
    grad_w_in = here_in + across(there_in).astype(f32)
    returned = exchange(result.reshape(experts, slots, width))

    output = hidden + dot(placing, returned.reshape(experts * slots, width), TN)
    d_output = cotangent.astype(f32) * row_factor[:, None]
    d_norm_two = dot(placing, d_returned, TN)
    d_back_two, grad_gain_two, grad_shift_two = norm_backward(
        d_norm_two, scaled_two, inverse_two, gain_two
    )
    d_hidden = d_output + d_back_two

    d_branch = d_hidden.astype(bf16)
    d_branch = jnp.concatenate(in_order(on_first_core, d_branch, beside(d_branch)))
    grad_proj = dot(mixed, d_branch, TN)
    d_mixed = dot(d_branch, proj_own, NT).astype(bf16)
    dq, dk, dv, dk_ext, dv_ext = attend_back(chip_scalar, qkv, ext, d_mixed, mixed, log_total)
    ext_back = lax.ppermute(jnp.concatenate([dk_ext, dv_ext], axis=1), "mp", EARLIER).astype(f32)
    d_kv = jnp.concatenate([dk, dv], axis=1)
    d_kv = jnp.concatenate([d_kv[:-HALF], d_kv[-HALF:] + ext_back])
    d_qkv = jnp.concatenate([dq, d_kv.astype(bf16)], axis=1)
    grad_heads = dot(d_qkv, normed_chip, TN).reshape(3, features, width)
    d_norm_chip = dot(d_qkv, w_heads)
    d_norm_own = lax.dynamic_slice_in_dim(d_norm_chip, core * tok, tok, 0)
    d_norm_other = lax.dynamic_slice_in_dim(d_norm_chip, (1 - core) * tok, tok, 0).astype(bf16)
    d_norm_one = d_norm_own + beside(d_norm_other).astype(f32)
    d_back_one, grad_gain_one, grad_shift_one = norm_backward(
        d_norm_one, scaled_one, inverse_one, gain_one
    )
    input_grad = d_hidden + d_back_one

    def own_and_other(grads, axis):
        first, second = jnp.split(grads, 2, axis=axis)
        return in_order(on_first_chip, first, second)

    heads_own, heads_other = own_and_other(grad_heads, 1)
    proj_grad_own, proj_grad_other = own_and_other(grad_proj, 0)
    heads_sum = heads_own + across(heads_other.astype(bf16)).astype(f32)
    proj_sum = proj_grad_own + across(proj_grad_other.astype(bf16)).astype(f32)
    sums = jnp.concatenate([heads_sum.reshape(-1, width), proj_sum]).astype(bf16)
    groups = experts
    pieces = exchange(sums.reshape(groups, -1, width))
    piece = jnp.sum(pieces.astype(f32), axis=0).astype(bf16)
    sums = lax.all_gather(piece, "dp", axis=0, tiled=True).astype(f32)
    grad_w_qkv = jnp.transpose(sums[: -w_proj.shape[0]].reshape(w_own.shape), (2, 0, 1))
    grad_w_proj = sums[-w_proj.shape[0] :]
    own_expert = (expert_ids == expert)[:, None]
    small = jnp.concatenate(
        [
            jnp.stack([grad_gain_one, grad_shift_one, grad_gain_two, grad_shift_two]),
            jnp.where(own_expert, router_grad[None, :], 0.0),
        ]
    )
    small = lax.psum(small, ("dp", "mp"))
    return (
        output.astype(bf16),
        input_grad.astype(bf16),
        small[0],
        small[1],
        grad_w_qkv,
        grad_w_proj,
        small[2],
        small[3],
        small[4:].T,
        grad_w_in[None],
        grad_w_out[None],
    )


def solution(mesh):
    tokens, group = P(("dp", "mp"), None), P("dp")
    return jax.shard_map(
        shards,
        mesh=mesh,
        in_specs=(
            tokens, tokens, P("dp", None), group, P(), P(), group, P(), P(),
            P(None, None, "mp"), P("mp", None), P(), P(), P(),
            P("dp", None, "mp"), P("dp", "mp", None),
        ),
        out_specs=(
            tokens, tokens, P(), P(), P(None, None, "mp"), P("mp", None), P(), P(), P(),
            P("dp", None, "mp"), P("dp", "mp", None),
        ),
        check_vma=False,
    )
```

```python
import functools

import jax
import jax.numpy as jnp
from jax import lax
from jax.experimental import pallas as pl
from jax.experimental.pallas import tpu as pltpu
from jax.sharding import PartitionSpec as P

HEAD_DIM = 64
LEN = 1024
BLOCK = 256
HALF = LEN // 2

norm_epsilon = 1e-05
count_scale = 10.0
masked_score = -1e30

f32 = jnp.float32
bf16 = jnp.bfloat16
MESH = pl.DeviceIdType.MESH
NT = (((1,), (1,)), ((), ()))
NN = (((1,), (0,)), ((), ()))
TN = (((0,), (0,)), ((), ()))

ACROSS = [(0, 2), (2, 0), (1, 3), (3, 1)]
BESIDE = [(0, 1), (1, 0), (2, 3), (3, 2)]
LATER = [(0, 2), (1, 3)]


def dot(left, right, dims=NN):
    return lax.dot_general(left, right, dims, preferred_element_type=f32)


def norm_forward(features, gain_vec, shift_vec):
    centre = features - jnp.mean(features, axis=-1, keepdims=True)
    inverse = lax.rsqrt(jnp.mean(centre * centre, axis=-1, keepdims=True) + norm_epsilon)
    scaled = centre * inverse
    return (scaled * gain_vec + shift_vec, scaled, inverse)


def plan(chip, run):
    second = chip == 1
    for whole, (here, there) in enumerate([(0, 2), (1, 3), (2, 0), (3, 1)]):
        run(pl.multiple_of(jnp.where(second, there, here) * BLOCK, BLOCK), whole)

    @pl.when(chip == 0)
    def _():
        run(4 * BLOCK, 0)
        run(5 * BLOCK, 1)

    @pl.when(chip == 1)
    def _():
        run(4 * BLOCK, 2)
        run(5 * BLOCK, 3)


def mask_diagonal(scores, whole):
    first = lax.broadcasted_iota(jnp.int32, (BLOCK, BLOCK), 0)
    second = lax.broadcasted_iota(jnp.int32, (BLOCK, BLOCK), 1)
    last = jnp.where(first <= second, scores[whole * BLOCK :], masked_score)
    if not whole:
        return last
    return jnp.concatenate([scores[: whole * BLOCK], last], axis=0)


def attend_kernel(chip_ref, q_ref, k_ref, v_ref, ke_ref, ve_ref, o_ref, l_ref, keys, values):
    chip = chip_ref[0]
    lane = lax.broadcasted_iota(jnp.int32, (1, 128), 1)
    row = lax.broadcasted_iota(jnp.int32, (128, 1), 0)
    keys[0:HALF] = ke_ref[...]
    keys[HALF:] = k_ref[...]
    values[:, 0:HALF] = ve_ref[...].T
    values[:, HALF:] = v_ref[...].T

    def run(first, whole):
        span = (whole + 1) * BLOCK
        start = pl.multiple_of(first + HALF - whole * BLOCK, BLOCK)
        queries = q_ref[pl.ds(first, BLOCK)] * bf16(0.125)
        near = keys[pl.ds(start, span)]
        mixed = values[:, pl.ds(start, span)]
        parts = []
        for head in range(2):
            own = jnp.where((lane // HEAD_DIM) == head, queries, bf16(0))
            scores = mask_diagonal(dot(near, own, NT), whole)
            largest = jnp.max(scores, axis=0, keepdims=True)
            expo = jnp.exp(scores - largest)
            total = jnp.sum(expo, axis=0, keepdims=True)
            parts.append(dot(mixed, expo.astype(bf16)) / total)
            l_ref[head : head + 1, pl.ds(first, BLOCK)] = largest + jnp.log(total)
        joined = jnp.where(row < HEAD_DIM, parts[0], parts[1])
        o_ref[pl.ds(first, BLOCK)] = joined.T.astype(bf16)

    plan(chip, run)


def column_block(rows, offset):
    return pl.BlockSpec((rows, 128), lambda pair: (0, offset + pair))


def attend(chip, qkv, ext):
    rows = qkv.shape[0]
    pairs = qkv.shape[1] // 384
    return pl.pallas_call(
        attend_kernel,
        grid=(pairs,),
        in_specs=[
            pl.BlockSpec(memory_space=pltpu.SMEM),
            column_block(rows, 0),
            column_block(rows, pairs),
            column_block(rows, 2 * pairs),
            column_block(HALF, 0),
            column_block(HALF, pairs),
        ],
        out_specs=[
            column_block(rows, 0),
            pl.BlockSpec((None, 8, rows), lambda pair: (pair, 0, 0)),
        ],
        out_shape=[
            jax.ShapeDtypeStruct((rows, pairs * 128), bf16),
            jax.ShapeDtypeStruct((pairs, 8, rows), f32),
        ],
        scratch_shapes=[
            pltpu.VMEM((HALF + rows, 128), bf16),
            pltpu.VMEM((128, HALF + rows), bf16),
        ],
        compiler_params=pltpu.CompilerParams(vmem_limit_bytes=48 * 2**20),
        cost_estimate=pl.CostEstimate(flops=16 * 10**9, bytes_accessed=8 * 10**6, transcendentals=8 * 10**6),
        name="attend",
    )(chip, qkv, qkv, qkv, ext, ext)


def across(value):
    return lax.ppermute(value, "mp", ACROSS)


def beside(value):
    return lax.ppermute(value, "mp", BESIDE)


def in_order(first, own, other):
    return jnp.where(first, own, other), jnp.where(first, other, own)


def exchange(rows):
    return lax.all_to_all(rows, "dp", split_axis=0, concat_axis=0, tiled=True)


def remote(src, dst, send, recv, device):
    return pltpu.make_async_remote_copy(
        src_ref=src, dst_ref=dst, send_sem=send, recv_sem=recv, device_id=device, device_id_type=MESH
    )


def greet(devices):
    barrier = pltpu.get_barrier_semaphore()
    for device in devices:
        pl.semaphore_signal(barrier, inc=1, device_id=device, device_id_type=MESH)
    pl.semaphore_wait(barrier, len(devices))


def normalise(values):
    centre = values - jnp.mean(values, axis=-1, keepdims=True)
    inverse = lax.rsqrt(jnp.mean(centre * centre, axis=-1, keepdims=True) + norm_epsilon)
    return centre * inverse, inverse


def norm_pull(d_normed, scaled, inverse, gain):
    d_scaled = d_normed * gain
    return inverse * (
        d_scaled
        - jnp.mean(d_scaled, axis=-1, keepdims=True)
        - scaled * jnp.mean(d_scaled * scaled, axis=-1, keepdims=True)
    )


PAIRS = 3
PAIR = 2 * HEAD_DIM
STRIP = 256


def backward_kernel(
    experts, slots,
    x_ref, cot_ref, factor_ref, hidden_ref, gain_one_ref, gain_two_ref, placing_ref, d_returned_ref,
    result_ref, normed_ref, qkv_ref, ext_ref, mixed_ref, log_ref, heads_ref, proj_ref,
    output_ref, input_grad_ref, sums_ref, norms_ref,
    returned, d_hidden, d_branch, d_mixed, keys, values, d_keys, d_values, d_qkv, d_last,
    ext_send, ext_recv, grads, grads_send, grads_recv, d_norm, norm_send, norm_recv,
    row_send, row_recv, ext_sems, branch_sems, grad_sems, norm_sems, local_sem,
):
    me, mp = lax.axis_index("dp"), lax.axis_index("mp")
    chip, core = mp // 2, mp % 2
    tok = x_ref.shape[0]
    rows = 2 * tok
    beside = {"mp": mp + 1 - 2 * core}
    across = {"mp": (mp + 2) % 4}
    greet([{"dp": (me + k) % experts} for k in range(1, experts)] + [beside, across])

    def chunk(index):
        return pl.ds(pl.multiple_of(index * slots, 16), slots)

    def row_copy(target, source):
        return remote(
            result_ref.at[chunk(target)], returned.at[chunk(source)],
            row_send.at[target], row_recv.at[source], {"dp": target},
        )

    own_rows = pltpu.make_async_copy(result_ref.at[chunk(me)], returned.at[chunk(me)], local_sem)
    own_rows.start()
    others = [(me + k) % experts for k in range(1, experts)]
    for other in others:
        row_copy(other, me).start()

    norms_ref[...] = jnp.zeros_like(norms_ref)
    mine = pl.multiple_of(core * tok, tok)

    def second_norm(step, carry):
        at = pl.ds(pl.multiple_of(step * STRIP, STRIP), STRIP)
        scaled, inverse = normalise(hidden_ref[at])
        d_normed = dot(placing_ref[at], d_returned_ref[...])
        norms_ref[2:3] += jnp.sum(d_normed * scaled, axis=0, keepdims=True)
        norms_ref[3:4] += jnp.sum(d_normed, axis=0, keepdims=True)
        total = cot_ref[at].astype(f32) * factor_ref[at] + norm_pull(
            d_normed, scaled, inverse, gain_two_ref[...]
        )
        d_hidden[at] = total
        d_branch[pl.ds(pl.multiple_of(mine + step * STRIP, STRIP), STRIP)] = total.astype(bf16)
        return carry

    lax.fori_loop(0, tok // STRIP, second_norm, 0)
    branch_copy = remote(
        d_branch.at[pl.ds(mine, tok)], d_branch.at[pl.ds(mine, tok)],
        branch_sems.at[0], branch_sems.at[1], beside,
    )
    branch_copy.start()
    branch_copy.wait_recv()

    def push_branch(step, carry):
        at = pl.ds(pl.multiple_of(step * STRIP, STRIP), STRIP)
        d_mixed[at] = dot(d_branch[at], proj_ref[...], NT).astype(bf16)
        return carry

    lax.fori_loop(0, rows // STRIP, push_branch, 0)
    grads[3] = dot(mixed_ref[...], d_branch[...], TN)

    lane = lax.broadcasted_iota(jnp.int32, (1, PAIR), 1)
    second = chip == 1

    def pair_of(step):
        return (1 - chip) * (PAIRS - 1 - step) + chip * step

    def ext_copy(pair):
        return remote(ext_send.at[pair], ext_recv.at[pair], ext_sems.at[0, pair], ext_sems.at[1, pair], across)

    def attention(step, carry):
        pair = pair_of(step)

        def column(offset):
            return pl.ds(pl.multiple_of((offset * PAIRS + pair) * PAIR, PAIR), PAIR)

        keys[0:HALF] = ext_ref[:, column(0)]
        keys[HALF:] = qkv_ref[:, column(1)]
        values[0:HALF] = ext_ref[:, column(1)]
        values[HALF:] = qkv_ref[:, column(2)]
        d_keys[...] = jnp.zeros_like(d_keys)
        d_values[...] = jnp.zeros_like(d_values)

        def run(first, whole):
            span = (whole + 1) * BLOCK
            start = pl.multiple_of(first + HALF - whole * BLOCK, BLOCK)
            at = pl.ds(first, BLOCK)
            queries = qkv_ref[at, column(0)] * bf16(0.125)
            d_out = d_mixed[at, column(0)]
            near = keys[pl.ds(start, span)]
            near_values = values[pl.ds(start, span)]
            product = (d_out.astype(f32) * mixed_ref[at, column(0)].astype(f32)).T
            dq = dk = dv = 0.0
            for head in range(2):
                here = (lane // HEAD_DIM) == head
                own = jnp.where(here, queries, bf16(0))
                d_own = jnp.where(here, d_out, bf16(0))
                delta = jnp.sum(product[HEAD_DIM * head : HEAD_DIM * (head + 1)], axis=0, keepdims=True)
                scores = mask_diagonal(dot(near, own, NT), whole)
                probs = jnp.exp(scores - log_ref[pair, head : head + 1, at])
                d_probs = dot(near_values, d_own, NT)
                d_scores = (probs * (d_probs - delta)).astype(bf16)
                dv = dv + dot(probs.astype(bf16), d_own)
                dk = dk + dot(d_scores, own)
                dq = dq + dot(d_scores, jnp.where(here, near, bf16(0)), TN)
            d_qkv[at, column(0)] = (dq * 0.125).astype(bf16)
            d_keys[pl.ds(start, span)] += dk
            d_values[pl.ds(start, span)] += dv

        @pl.when(second)
        def _():
            run(0, 2)
            run(BLOCK, 3)
            ext_send[pair, :, 0:PAIR] = d_keys[0:HALF].astype(bf16)
            ext_send[pair, :, PAIR:] = d_values[0:HALF].astype(bf16)
            ext_copy(pair).start()
            run(4 * BLOCK, 2)
            run(5 * BLOCK, 3)

        @pl.when(chip == 0)
        def _():
            run(2 * BLOCK, 2)
            run(3 * BLOCK, 3)
            run(4 * BLOCK, 0)
            run(5 * BLOCK, 1)

        run(pl.multiple_of(2 * chip * BLOCK, BLOCK), 0)
        run(pl.multiple_of((2 * chip + 1) * BLOCK, BLOCK), 1)
        d_qkv[:, column(1)] = d_keys[HALF:].astype(bf16)
        d_qkv[:, column(2)] = d_values[HALF:].astype(bf16)

        @pl.when(chip == 0)
        def _():
            d_last[pair, :, 0:PAIR] = d_keys[rows:]
            d_last[pair, :, PAIR:] = d_values[rows:]

        return carry

    lax.fori_loop(0, PAIRS, attention, 0)

    other_part = pl.ds(pl.multiple_of((1 - chip) * grads_send.shape[1], 16), grads_send.shape[1])
    own_part = pl.ds(pl.multiple_of(chip * grads_send.shape[1], 16), grads_send.shape[1])

    @pl.when(chip == 0)
    def _():
        for step in range(PAIRS):
            pair = PAIRS - 1 - step
            ext_copy(pair).wait_recv()
            total = d_last[pair] + ext_recv[pair].astype(f32)
            for index in range(2):
                d_qkv[rows - HALF :, ((1 + index) * PAIRS + pair) * PAIR : ((1 + index) * PAIRS + pair + 1) * PAIR] = (
                    total[:, index * PAIR : (index + 1) * PAIR].astype(bf16)
                )

    @pl.when(second)
    def _():
        for pair in range(PAIRS):
            ext_copy(pair).wait_send()

    for index in range(3):
        grads[index] = dot(d_qkv[:, index * PAIRS * PAIR : (index + 1) * PAIRS * PAIR], normed_ref[...], TN)
    for index in range(4):
        grads_send[index] = grads[index, other_part].astype(bf16)
    grad_copy = remote(grads_send, grads_recv, grad_sems.at[0], grad_sems.at[1], across)
    grad_copy.start()

    def pull_norm(step, carry):
        at = pl.ds(pl.multiple_of(step * STRIP, STRIP), STRIP)
        d_norm[at] = dot(d_qkv[at], heads_ref[...])
        return carry

    lax.fori_loop(0, rows // STRIP, pull_norm, 0)
    norm_send[...] = d_norm[pl.ds(pl.multiple_of((1 - core) * tok, tok), tok)].astype(bf16)
    norm_copy = remote(norm_send, norm_recv, norm_sems.at[0], norm_sems.at[1], beside)
    norm_copy.start()
    own_rows.wait()
    for other in others:
        row_copy(me, other).wait_recv()

    def finish(step, carry):
        at = pl.ds(pl.multiple_of(step * STRIP, STRIP), STRIP)
        output_ref[at] = (hidden_ref[at] + dot(placing_ref[at], returned[...])).astype(bf16)
        return carry

    lax.fori_loop(0, tok // STRIP, finish, 0)
    norm_copy.wait_recv()

    def first_norm(step, carry):
        at = pl.ds(pl.multiple_of(step * STRIP, STRIP), STRIP)
        scaled, inverse = normalise(x_ref[at].astype(f32))
        d_normed = d_norm[pl.ds(pl.multiple_of(mine + step * STRIP, STRIP), STRIP)] + norm_recv[at].astype(f32)
        norms_ref[0:1] += jnp.sum(d_normed * scaled, axis=0, keepdims=True)
        norms_ref[1:2] += jnp.sum(d_normed, axis=0, keepdims=True)
        input_grad_ref[at] = (
            d_hidden[at] + norm_pull(d_normed, scaled, inverse, gain_one_ref[...])
        ).astype(bf16)
        return carry

    lax.fori_loop(0, tok // STRIP, first_norm, 0)
    grad_copy.wait_recv()
    part = grads_send.shape[1]
    for index in range(4):
        sums_ref[index * part : (index + 1) * part] = (
            grads[index, own_part] + grads_recv[index].astype(f32)
        ).astype(bf16)
    if sums_ref.shape[0] > 4 * part:
        sums_ref[4 * part :] = jnp.zeros((sums_ref.shape[0] - 4 * part, sums_ref.shape[1]), bf16)
    for other in others:
        row_copy(other, me).wait_send()
    branch_copy.wait_send()
    norm_copy.wait_send()
    grad_copy.wait_send()


def run_backward(
    x, cotangent, factor, hidden, gain_one, gain_two, placing, d_returned, result, normed_chip, qkv, ext,
    mixed, log_total, heads, proj, experts, sum_rows,
):
    tok, width = x.shape
    rows = 2 * tok
    total = d_returned.shape[0]
    part = proj.shape[0] // 2
    anyspace, vmem = pl.BlockSpec(memory_space=pl.ANY), pl.BlockSpec(memory_space=pltpu.VMEM)
    dma = pltpu.SemaphoreType.DMA
    return pl.pallas_call(
        functools.partial(backward_kernel, experts, total // experts),
        in_specs=[vmem] * 8 + [anyspace] + [vmem] * 7,
        out_specs=[vmem] * 4,
        out_shape=[
            jax.ShapeDtypeStruct((tok, width), bf16),
            jax.ShapeDtypeStruct((tok, width), bf16),
            jax.ShapeDtypeStruct((sum_rows, width), bf16),
            jax.ShapeDtypeStruct((8, width), f32),
        ],
        scratch_shapes=[
            pltpu.VMEM((total, width), bf16),
            pltpu.VMEM((tok, width), f32),
            pltpu.VMEM((rows, width), bf16),
            pltpu.VMEM((rows, PAIRS * PAIR), bf16),
            pltpu.VMEM((HALF + rows, PAIR), bf16),
            pltpu.VMEM((HALF + rows, PAIR), bf16),
            pltpu.VMEM((HALF + rows, PAIR), f32),
            pltpu.VMEM((HALF + rows, PAIR), f32),
            pltpu.VMEM((rows, 3 * PAIRS * PAIR), bf16),
            pltpu.VMEM((PAIRS, HALF, 2 * PAIR), f32),
            pltpu.VMEM((PAIRS, HALF, 2 * PAIR), bf16),
            pltpu.VMEM((PAIRS, HALF, 2 * PAIR), bf16),
            pltpu.VMEM((4, 2 * part, width), f32),
            pltpu.VMEM((4, part, width), bf16),
            pltpu.VMEM((4, part, width), bf16),
            pltpu.VMEM((rows, width), f32),
            pltpu.VMEM((tok, width), bf16),
            pltpu.VMEM((tok, width), bf16),
            dma((experts,)), dma((experts,)), dma((2, PAIRS)), dma((2,)), dma((2,)), dma((2,)), dma,
        ],
        compiler_params=pltpu.CompilerParams(
            collective_id=2, has_side_effects=True, vmem_limit_bytes=60 * 2**20
        ),
        cost_estimate=pl.CostEstimate(flops=30 * 10**9, bytes_accessed=30 * 10**6, transcendentals=8 * 10**6),
        name="backward",
    )(
        x, cotangent, factor, hidden, gain_one, gain_two, placing, d_returned, result, normed_chip, qkv, ext,
        mixed, log_total, heads, proj,
    )


def reduce_kernel(
    experts,
    sums_ref, small_ref, here_in_ref, here_out_ref, there_in_ref, there_out_ref,
    total_ref, small_total_ref, grad_in_ref, grad_out_ref,
    half_recv, half, piece_recv, small_held, small_recv, small_pieces, far_in, far_out,
    half_sems, piece_sems, gather_sems, back_sems, far_sems, small_sems, small_piece_sems,
):
    me, mp = lax.axis_index("dp"), lax.axis_index("mp")
    beside = {"mp": mp + 1 - 2 * (mp % 2)}
    across = {"mp": (mp + 2) % 4}
    side, line = me % 2, me // 2
    lines = experts // 2
    partner = {"dp": me + 1 - 2 * side}
    mates = [(line + k) % lines for k in range(1, lines)]
    greet([beside, across, partner] + [{"dp": 2 * mate + side} for mate in mates])
    half_rows = half.shape[0]
    piece_rows = half_rows // lines
    lanes = sums_ref.shape[1] // 2
    own_half = pl.multiple_of(side * half_rows, 16)
    far_half = pl.multiple_of((1 - side) * half_rows, 16)

    far_copies = [
        remote(there_out_ref, far_out, far_sems.at[0, 0], far_sems.at[1, 0], across),
        remote(there_in_ref, far_in, far_sems.at[0, 1], far_sems.at[1, 1], across),
    ]
    def columns(index):
        return pl.ds(index * lanes, lanes)

    def piece(index, base=0):
        return pl.ds(pl.multiple_of(base + index * piece_rows, 16), piece_rows)

    def half_copy(part):
        return remote(
            sums_ref.at[pl.ds(far_half, half_rows), columns(part)], half_recv.at[:, columns(part)],
            half_sems.at[0, part], half_sems.at[1, part], partner,
        )

    def piece_copy(part, target, source):
        return remote(
            half.at[piece(target), columns(part)], piece_recv.at[source, :, columns(part)],
            piece_sems.at[0, part, target], piece_sems.at[1, part, source], {"dp": 2 * target + side},
        )

    def gather_copy(part, target, source):
        block = total_ref.at[piece(source, own_half), columns(part)]
        return remote(
            block, block, gather_sems.at[0, part, target], gather_sems.at[1, part, source], {"dp": 2 * target + side}
        )

    def back_copy(part, which):
        block = total_ref.at[pl.ds(which, half_rows), columns(part)]
        return remote(block, block, back_sems.at[0, part], back_sems.at[1, part], partner)

    small_held[0] = small_ref[...]

    def small_step(index, device):
        return remote(
            small_held.at[index], small_recv.at[index], small_sems.at[0, index], small_sems.at[1, index], device
        )

    small_step(0, across).start()
    for copy in far_copies:
        copy.start()
    for part in range(2):
        half_copy(part).start()
    for index, device in enumerate((across, beside, partner)):
        if index:
            small_step(index, device).start()
        small_step(index, device).wait()
        small_held[index + 1] = small_held[index] + small_recv[index]

    def small_copy(target, source):
        return remote(
            small_held.at[3], small_pieces.at[source],
            small_piece_sems.at[0, target], small_piece_sems.at[1, source], {"dp": 2 * target + side},
        )

    for mate in mates:
        small_copy(mate, line).start()
    small_pieces[line] = small_held[3]

    for part in range(2):
        at = slice(part * lanes, (part + 1) * lanes)
        half_copy(part).wait_recv()
        half[:, at] = (
            sums_ref[pl.ds(own_half, half_rows), at].astype(f32) + half_recv[:, at].astype(f32)
        ).astype(bf16)
        for mate in mates:
            piece_copy(part, mate, line).start()
    for part in range(2):
        at = slice(part * lanes, (part + 1) * lanes)
        value = half[piece(line), at].astype(f32)
        for mate in mates:
            piece_copy(part, line, mate).wait_recv()
            value += piece_recv[mate, :, at].astype(f32)
        total_ref[piece(line, own_half), at] = value.astype(bf16)
        for mate in mates:
            gather_copy(part, mate, line).start()
    for mate in mates:
        small_copy(line, mate).wait_recv()
    small_total = small_pieces[0]
    for index in range(1, lines):
        small_total += small_pieces[index]
    small_total_ref[...] = small_total
    far_copies[0].wait_recv()
    grad_out_ref[...] = here_out_ref[...] + far_out[...].astype(f32)
    for part in range(2):
        for mate in mates:
            gather_copy(part, line, mate).wait_recv()
        back_copy(part, own_half).start()
    far_copies[1].wait_recv()
    grad_in_ref[...] = here_in_ref[...] + far_in[...].astype(f32)
    for part in range(2):
        back_copy(part, far_half).wait_recv()
        back_copy(part, own_half).wait_send()
        half_copy(part).wait_send()
        for mate in mates:
            piece_copy(part, mate, line).wait_send()
            gather_copy(part, mate, line).wait_send()
    for mate in mates:
        small_copy(mate, line).wait_send()
    for copy in far_copies:
        copy.wait_send()


def run_reduce(sums, small, here_in, here_out, there_in, there_out, experts):
    rows, width = sums.shape
    lines = experts // 2
    vmem = pl.BlockSpec(memory_space=pltpu.VMEM)
    dma = pltpu.SemaphoreType.DMA
    return pl.pallas_call(
        functools.partial(reduce_kernel, experts),
        in_specs=[vmem] * 6,
        out_specs=[vmem] * 4,
        out_shape=[
            jax.ShapeDtypeStruct((rows, width), bf16),
            jax.ShapeDtypeStruct(small.shape, f32),
            jax.ShapeDtypeStruct(here_in.shape, f32),
            jax.ShapeDtypeStruct(here_out.shape, f32),
        ],
        scratch_shapes=[
            pltpu.VMEM((rows // 2, width), bf16),
            pltpu.VMEM((rows // 2, width), bf16),
            pltpu.VMEM((lines, rows // experts, width), bf16),
            pltpu.VMEM((4,) + small.shape, f32),
            pltpu.VMEM((3,) + small.shape, f32),
            pltpu.VMEM((lines,) + small.shape, f32),
            pltpu.VMEM(there_in.shape, bf16),
            pltpu.VMEM(there_out.shape, bf16),
            dma((2, 2)), dma((2, 2, lines)), dma((2, 2, lines)), dma((2, 2)), dma((2, 2)),
            dma((2, 3)), dma((2, lines)),
        ],
        compiler_params=pltpu.CompilerParams(
            collective_id=3, has_side_effects=True, vmem_limit_bytes=48 * 2**20
        ),
        cost_estimate=pl.CostEstimate(flops=10**7, bytes_accessed=20 * 10**6, transcendentals=0),
        name="reduce",
    )(sums, small, here_in, here_out, there_in, there_out)


def gelu_parts(pre):
    scale = 0.7978845608028654
    square = pre * pre
    inner = jnp.tanh(pre * (scale + (scale * 0.044715) * square))
    half = 0.5 * (1.0 + inner)
    slope = half + (0.5 * pre) * (1.0 - inner * inner) * (scale + (3.0 * scale * 0.044715) * square)
    return pre * half, slope

STAGES = 4

def expert_kernel(
    experts, slots, steps,
    rows_ref, cot_ref, factor_ref, router_ref, w_in_ref, w_out_ref, w_in_far_ref,
    back_ref, result_ref, router_grad_ref, here_in_ref, here_out_ref, there_in_ref, there_out_ref,
    x, wi, wo, d_out, act, d_pre, total, d_x, give, g_send, g_recv,
    row_send, row_recv, back_send, back_recv, w_send, w_recv, g_send_sem, g_recv_sem, local_sem,
):
    me = lax.axis_index("dp")
    mp = lax.axis_index("mp")
    beside = {"mp": mp + 1 - 2 * (mp % 2)}
    across = {"mp": (mp + 2) % 4}
    members = experts // STAGES
    span = members * slots
    own_group, own_member = me // members, me % members

    def group_of(stage):
        return 2 * ((own_group // 2 + stage // 2) % 2) + (own_group % 2 + stage % 2) % 2

    def chunk(index):
        return pl.ds(pl.multiple_of(index * slots, 16), slots)

    def group_rows(group):
        return pl.ds(pl.multiple_of(group * span, 16), span)

    barrier = pltpu.get_barrier_semaphore()

    def greet(step, carry):
        pl.semaphore_signal(barrier, inc=1, device_id={"dp": (me + step) % experts}, device_id_type=MESH)
        return carry

    lax.fori_loop(1, experts, greet, 0)
    pl.semaphore_signal(barrier, inc=1, device_id=beside, device_id_type=MESH)
    pl.semaphore_signal(barrier, inc=1, device_id=across, device_id_type=MESH)
    pl.semaphore_wait(barrier, experts + 1)

    def remote(src, dst, send, recv, device):
        return pltpu.make_async_remote_copy(
            src_ref=src, dst_ref=dst, send_sem=send, recv_sem=recv, device_id=device, device_id_type=MESH
        )

    def row_copy(target, source):
        return remote(rows_ref.at[chunk(target)], x.at[chunk(source)], row_send.at[target], row_recv.at[source], {"dp": target})

    def back_copy(target, source):
        return remote(give.at[chunk(target)], back_ref.at[chunk(source)], back_send.at[target], back_recv.at[source], {"dp": target})

    def partners(stage):
        group = group_of(stage)
        if stage == 0:
            return [group * members + (own_member + k) % members for k in range(1, members)]
        return [group * members + (own_member + k) % members for k in range(members)]

    for stage in reversed(range(STAGES)):
        for other in partners(stage):
            row_copy(other, me).start()
    own_rows = pltpu.make_async_copy(rows_ref.at[chunk(me)], x.at[chunk(me)], local_sem.at[0])
    own_in = pltpu.make_async_copy(w_in_ref, wi.at[0], local_sem.at[1])
    own_out = pltpu.make_async_copy(w_out_ref, wo.at[0], local_sem.at[2])
    far_in = pltpu.make_async_copy(w_in_far_ref, wi.at[2], local_sem.at[3])
    near_in = remote(w_in_ref, wi.at[1], w_send.at[0], w_recv.at[0], beside)
    near_out = remote(w_out_ref, wo.at[1], w_send.at[1], w_recv.at[1], beside)
    far_near_in = remote(w_in_far_ref, wi.at[3], w_send.at[2], w_recv.at[2], beside)
    far_out = remote(w_out_ref, wo.at[2], w_send.at[3], w_recv.at[3], across)
    far_near_out = remote(wo.at[2], wo.at[3], w_send.at[4], w_recv.at[4], beside)
    for copy in (own_rows, own_in, own_out, near_in, near_out, far_in, far_out, far_near_in):
        copy.start()
    router_grad_ref[...] = jnp.zeros_like(router_grad_ref)

    def prepare(stage, rows):
        features = x[rows].astype(f32)
        gate = jax.nn.sigmoid(jnp.sum(features * router_ref[...], axis=1, keepdims=True))
        d_out[rows] = (gate * (cot_ref[rows].astype(f32) * factor_ref[rows])).astype(bf16)
        total[rows] = jnp.zeros((span, x.shape[1]), f32)
        d_x[rows] = jnp.zeros((span, x.shape[1]), f32)

    def finish(stage, rows):
        features = x[rows].astype(f32)
        gate = jax.nn.sigmoid(jnp.sum(features * router_ref[...], axis=1, keepdims=True))
        value = total[rows]
        d_gate = jnp.sum(cot_ref[rows].astype(f32) * factor_ref[rows] * value, axis=1, keepdims=True)
        d_logit = (d_gate * gate * (1.0 - gate)).astype(bf16).astype(f32)
        give[rows] = (d_x[rows] + d_logit * router_ref[...]).astype(bf16)
        result_ref[rows] = (gate * value).astype(bf16)
        router_grad_ref[...] += jnp.sum(features * d_logit, axis=0, keepdims=True)

    def stage_of(step):
        return jnp.where(
            (step < 2) | (step >= 14), 0, jnp.where(step < 6, 3, jnp.where(step < 10, 2, 1))
        )

    def step_body(step, carry):
        stage = stage_of(step)
        part = jnp.where(step < 4, step % 2, jnp.where(step < 6, step - 2, (step - 6) % 4))
        part = jnp.where(step >= 14, step - 12, part)
        rows = group_rows(group_of(stage))

        for static, at in enumerate((0, 10, 6, 2)):
            @pl.when(step == at)
            def _():
                if static == 0:
                    own_rows.wait()
                for other in partners(static):
                    row_copy(me, other).wait_recv()
        @pl.when((step == 0) | (step == 2) | (step == 6) | (step == 10))
        def _():
            prepare(stage, rows)

        @pl.when(step == 0)
        def _():
            own_in.wait()
            own_out.wait()

        @pl.when(step == 1)
        def _():
            near_in.wait_recv()
            near_out.wait_recv()

        @pl.when(step == 4)
        def _():
            far_in.wait()
            far_out.wait_recv()
            far_near_out.start()

        @pl.when(step == 5)
        def _():
            far_near_in.wait_recv()
            far_near_out.wait_recv()

        pre = dot(x[rows], wi[part])
        value, slope = gelu_parts(pre)
        value = value.astype(bf16)
        act[part, rows] = value
        total[rows] += dot(value, wo[part])
        d_value = (dot(d_out[rows], wo[part], NT) * slope).astype(bf16)
        d_pre[part, rows] = d_value
        d_x[rows] += dot(d_value, wi[part], NT)

        @pl.when((step == 5) | (step == 9) | (step == 13) | (step == 15))
        def _():
            finish(stage, rows)

        for static, at in enumerate((15, 13, 9, 5)):
            @pl.when(step == at)
            def _():
                for other in partners(static):
                    back_copy(other, me).start()
        return carry

    lax.fori_loop(0, 16, step_body, 0)
    own_back = pltpu.make_async_copy(give.at[chunk(me)], back_ref.at[chunk(me)], local_sem.at[4])
    own_back.start()

    def grad_copy(index):
        return remote(outgoing[index], g_recv.at[index], g_send_sem.at[index], g_recv_sem.at[index], beside)

    kept = pl.ds(0, x.shape[1])
    outgoing = [g_send, act.at[3, kept], d_pre.at[3, kept], act.at[1, kept]]
    for index, part in enumerate((3, 1)):
        outgoing[2 * index][...] = dot(act[part], d_out[...], TN).astype(bf16)
        grad_copy(2 * index).start()
        outgoing[2 * index + 1][...] = dot(x[...], d_pre[part], TN).astype(bf16)
        grad_copy(2 * index + 1).start()
    grad = dot(act[2], d_out[...], TN)
    grad_copy(0).wait_recv()
    there_out_ref[...] = (grad + g_recv[0].astype(f32)).astype(bf16)
    grad = dot(x[...], d_pre[2], TN)
    grad_copy(1).wait_recv()
    there_in_ref[...] = (grad + g_recv[1].astype(f32)).astype(bf16)
    grad = dot(act[0], d_out[...], TN)
    grad_copy(2).wait_recv()
    here_out_ref[...] = grad + g_recv[2].astype(f32)
    grad = dot(x[...], d_pre[0], TN)
    grad_copy(3).wait_recv()
    here_in_ref[...] = grad + g_recv[3].astype(f32)

    own_back.wait()
    for stage in range(STAGES):
        for other in partners(stage):
            back_copy(me, other).wait_recv()
            back_copy(other, me).wait_send()
            row_copy(other, me).wait_send()
    for copy in (near_in, near_out, far_near_in, far_out, far_near_out):
        copy.wait_send()
    for index in range(4):
        grad_copy(index).wait_send()


def run_expert(rows, cot_rows, factor, router_row, w_in, w_out, w_in_far, experts):
    total, width = rows.shape
    slots = total // experts
    hidden = w_in.shape[1]
    anyspace, vmem = pl.BlockSpec(memory_space=pl.ANY), pl.BlockSpec(memory_space=pltpu.VMEM)
    dma = pltpu.SemaphoreType.DMA
    return pl.pallas_call(
        functools.partial(expert_kernel, experts, slots, 0),
        in_specs=[anyspace, vmem, vmem, vmem, anyspace, anyspace, anyspace],
        out_specs=[vmem] * 7,
        out_shape=[
            jax.ShapeDtypeStruct((total, width), bf16),
            jax.ShapeDtypeStruct((total, width), bf16),
            jax.ShapeDtypeStruct((1, width), f32),
            jax.ShapeDtypeStruct((width, hidden), f32),
            jax.ShapeDtypeStruct((hidden, width), f32),
            jax.ShapeDtypeStruct((width, hidden), bf16),
            jax.ShapeDtypeStruct((hidden, width), bf16),
        ],
        scratch_shapes=[
            pltpu.VMEM((total, width), bf16),
            pltpu.VMEM((4, width, hidden), bf16),
            pltpu.VMEM((4, hidden, width), bf16),
            pltpu.VMEM((total, width), bf16),
            pltpu.VMEM((4, total, hidden), bf16),
            pltpu.VMEM((4, total, hidden), bf16),
            pltpu.VMEM((total, width), f32),
            pltpu.VMEM((total, width), f32),
            pltpu.VMEM((total, width), bf16),
            pltpu.VMEM((width, width), bf16),
            pltpu.VMEM((4, width, width), bf16),
            dma((experts,)), dma((experts,)), dma((experts,)), dma((experts,)),
            dma((5,)), dma((5,)), dma((4,)), dma((4,)), dma((5,)),
        ],
        compiler_params=pltpu.CompilerParams(
            collective_id=1, has_side_effects=True, vmem_limit_bytes=60 * 2**20
        ),
        cost_estimate=pl.CostEstimate(flops=30 * 10**9, bytes_accessed=40 * 10**6, transcendentals=3 * 10**6),
        name="expert",
    )(rows, cot_rows, factor, router_row, w_in, w_out, w_in_far)


def shards(
    inputs, cotangent, routes, domains, domain_counts, domain_weights, keep_mask, gain_one, shift_one,
    w_qkv, w_proj, gain_two, shift_two, w_router, w_in, w_out,
):
    tok, width = inputs.shape
    experts = w_router.shape[1]
    cap = max(2, tok * 5 // (4 * experts))
    slots = (cap + 16) // 16 * 16
    mp_index = lax.axis_index("mp")
    chip, core = mp_index // 2, mp_index % 2
    on_first_chip, on_first_core = chip == 0, core == 0
    expert = lax.axis_index("dp")
    seq_count = routes.shape[0] // LEN

    own_routes = lax.dynamic_slice_in_dim(routes[:, 0], mp_index * tok, tok, 0)
    expert_ids = jnp.arange(experts, dtype=jnp.int32)
    picked = own_routes[:, None] == expert_ids[None, :]
    places = jnp.arange(tok, dtype=jnp.int32)
    earlier = (places[:, None] > places[None, :]).astype(bf16)
    counts = dot(earlier, picked.astype(bf16))
    rank = jnp.sum(jnp.where(picked, counts, 0.0), axis=1).astype(jnp.int32)
    own_slots = own_routes * slots + rank
    slot_ids = jnp.arange(experts * slots, dtype=jnp.int32)
    placed = own_slots[None, :] == slot_ids[:, None]
    placing = placed.astype(bf16)

    seq_ids = jnp.arange(seq_count, dtype=jnp.int32)
    domain_ids = jnp.arange(domain_weights.shape[0], dtype=jnp.int32)
    same_domain = domains[:, None] == domain_ids[None, :]
    seq_weight = jnp.sum(jnp.where(same_domain, domain_weights[None, :], 0.0), axis=1)
    seq_counts = jnp.sum(jnp.where(same_domain, domain_counts[None, :], 0), axis=1).astype(f32)
    factor = keep_mask.astype(f32) * seq_weight * count_scale / seq_counts
    row_seq = (mp_index * tok + places) // LEN
    row_factor = jnp.sum(jnp.where(row_seq[:, None] == seq_ids[None, :], factor[None, :], 0.0), axis=1)
    slot_factor = jnp.sum(jnp.where(placed, row_factor[None, :], 0.0), axis=1).reshape(experts, slots)
    high = slot_factor.astype(bf16)
    low = (slot_factor - high.astype(f32)).astype(bf16)
    cot_rows = dot(placing, cotangent).astype(bf16).reshape(experts, slots, width)
    cot_rows = cot_rows.at[:, cap, :slots].set(high).at[:, cap, width // 2 : width // 2 + slots].set(low)
    cot_rows = exchange(cot_rows)

    inputs_wide = inputs.astype(f32)
    normed_one, scaled_one, inverse_one = norm_forward(inputs_wide, gain_one, shift_one)
    normed_one = normed_one.astype(bf16)
    normed_chip = jnp.concatenate(in_order(on_first_core, normed_one, beside(normed_one)))
    w_own = jnp.transpose(w_qkv, (1, 2, 0))
    features = 2 * w_own.shape[1]
    w_heads = jnp.concatenate(in_order(on_first_chip, w_own, across(w_own)), axis=1)
    w_heads = w_heads.reshape(3 * features, width)
    qkv = dot(normed_chip, w_heads, NT).astype(bf16)
    ext = lax.ppermute(qkv[-HALF:, features:], "mp", LATER)
    chip_scalar = chip.astype(jnp.int32).reshape(1)
    mixed, log_total = attend(chip_scalar, qkv, ext)

    proj_own = jnp.concatenate(in_order(on_first_chip, w_proj, across(w_proj)))
    proj_other = beside(proj_own)
    mixed_own = lax.dynamic_slice_in_dim(mixed, core * tok, tok, 0)
    mixed_other = beside(lax.dynamic_slice_in_dim(mixed, (1 - core) * tok, tok, 0))
    hidden = inputs_wide + dot(mixed_own, proj_own) + dot(mixed_other, proj_other)
    normed_two, scaled_two, inverse_two = norm_forward(hidden, gain_two, shift_two)
    normed_two = normed_two.astype(bf16)
    rows = dot(placing, normed_two).astype(bf16)

    cot_factor = cot_rows[:, cap, :slots].astype(f32) + cot_rows[
        :, cap, width // 2 : width // 2 + slots
    ].astype(f32)
    cot_factor = jnp.where(jnp.arange(slots)[None, :] < cap, cot_factor, 0.0).reshape(-1, 1)
    router_row = lax.dynamic_slice_in_dim(w_router.T, expert, 1, 0).astype(f32)
    d_returned, result, router_grad, here_in, here_out, there_in, there_out = run_expert(
        rows, cot_rows.reshape(experts * slots, width), cot_factor, router_row,
        w_in[0], w_out[0], across(w_in[0]), experts,
    )

    piece = (4 * w_proj.shape[0] // experts + 15) // 16 * 16
    output, input_grad, sums, norms = run_backward(
        inputs, cotangent, row_factor[:, None], hidden, gain_one[None], gain_two[None], placing.T, d_returned,
        result, normed_chip, qkv, ext, mixed, log_total, w_heads, proj_own,
        experts, experts * piece,
    )
    own_expert = (expert_ids == expert)[:, None]
    small = jnp.concatenate([norms, jnp.where(own_expert, router_grad, 0.0)])
    sums, small, grad_w_in, grad_w_out = run_reduce(
        sums, small, here_in, here_out, there_in, there_out, experts
    )
    split = 3 * w_proj.shape[0]
    grad_w_qkv = jnp.transpose(sums[:split].astype(f32).reshape(w_own.shape), (2, 0, 1))
    grad_w_proj = sums[split : split + w_proj.shape[0]].astype(f32)
    return (
        output,
        input_grad,
        small[0],
        small[1],
        grad_w_qkv,
        grad_w_proj,
        small[2],
        small[3],
        small[8:].T,
        grad_w_in[None],
        grad_w_out[None],
    )


def solution(mesh):
    tokens, group = P(("dp", "mp"), None), P("dp")
    return jax.shard_map(
        shards,
        mesh=mesh,
        in_specs=(
            tokens, tokens, P("dp", None), group, P(), P(), group, P(), P(),
            P(None, None, "mp"), P("mp", None), P(), P(), P(),
            P("dp", None, "mp"), P("dp", "mp", None),
        ),
        out_specs=(
            tokens, tokens, P(), P(), P(None, None, "mp"), P("mp", None), P(), P(), P(),
            P("dp", None, "mp"), P("dp", "mp", None),
        ),
        check_vma=False,
    )
```

```python
import functools

import jax
import jax.numpy as jnp
from jax import lax
from jax.experimental import pallas as pl
from jax.experimental.pallas import tpu as pltpu
from jax.sharding import PartitionSpec as P

HEAD_DIM = 64
LEN = 1024
BLOCK = 256
HALF = LEN // 2

norm_epsilon = 1e-05
count_scale = 10.0
masked_score = -1e30

f32 = jnp.float32
bf16 = jnp.bfloat16
MESH = pl.DeviceIdType.MESH
NT = (((1,), (1,)), ((), ()))
NN = (((1,), (0,)), ((), ()))
TN = (((0,), (0,)), ((), ()))


def dot(left, right, dims=NN):
    return lax.dot_general(left, right, dims, preferred_element_type=f32)


def mask_diagonal(scores, whole):
    first = lax.broadcasted_iota(jnp.int32, (BLOCK, BLOCK), 0)
    second = lax.broadcasted_iota(jnp.int32, (BLOCK, BLOCK), 1)
    last = jnp.where(first <= second, scores[whole * BLOCK :], masked_score)
    if not whole:
        return last
    return jnp.concatenate([scores[: whole * BLOCK], last], axis=0)


def remote(src, dst, send, recv, device):
    return pltpu.make_async_remote_copy(
        src_ref=src, dst_ref=dst, send_sem=send, recv_sem=recv, device_id=device, device_id_type=MESH
    )


def greet(devices):
    barrier = pltpu.get_barrier_semaphore()
    for device in devices:
        pl.semaphore_signal(barrier, inc=1, device_id=device, device_id_type=MESH)
    pl.semaphore_wait(barrier, len(devices))


def normalise(values):
    centre = values - jnp.mean(values, axis=-1, keepdims=True)
    inverse = lax.rsqrt(jnp.mean(centre * centre, axis=-1, keepdims=True) + norm_epsilon)
    return centre * inverse, inverse


def norm_pull(d_normed, scaled, inverse, gain):
    d_scaled = d_normed * gain
    return inverse * (
        d_scaled
        - jnp.mean(d_scaled, axis=-1, keepdims=True)
        - scaled * jnp.mean(d_scaled * scaled, axis=-1, keepdims=True)
    )


PAIRS = 3
PAIR = 2 * HEAD_DIM
STRIP = 256


def pick_sequence(positions, factor_ref):
    value = jnp.full(positions.shape, factor_ref[0], f32)
    for index in range(1, factor_ref.shape[0]):
        value = jnp.where(positions >= index * LEN, factor_ref[index], value)
    return value


def forward_kernel(
    experts, slots, cap,
    x_ref, cot_ref, routes_ref, factor_ref, gain_one_ref, shift_one_ref, gain_two_ref, shift_two_ref,
    w_ref, proj_ref, w_in_ref,
    normed_out, qkv_out, ext_out, mixed_out, log_out, heads_out, proj_out, hidden_out, rows_out, cot_out,
    placing_t_out, w_in_far_out,
    normed, qkv, ext, mixed, logs, heads, proj, hidden, rows, placing, placing_t, cot_send, mixed_far, normed_two,
    keys, values,
    w_sems, pass_sems, proj_sems, w_in_sems, normed_sems, ext_sems, mixed_sems, row_send, row_recv, local_sems,
    save_sems,
):
    me, mp = lax.axis_index("dp"), lax.axis_index("mp")
    chip, core = mp // 2, mp % 2
    tok, width = x_ref.shape
    part = proj_ref.shape[0]
    total = experts * slots
    beside = {"mp": mp + 1 - 2 * core}
    across = {"mp": (mp + 2) % 4}
    side = me % 2
    partner = {"dp": me + 1 - 2 * side}
    second = chip == 1
    others = [(me + k) % experts for k in range(1, experts)]
    greet([{"dp": other} for other in others] + [beside, across])

    own_part = pl.ds(pl.multiple_of(chip * part, 16), part)
    other_part = pl.ds(pl.multiple_of((1 - chip) * part, 16), part)
    half = pl.ds(pl.multiple_of(side * (width // 2), 128), width // 2)

    def w_copy(index):
        if index == 3:
            source, target = proj_ref.at[:, half], proj.at[0, own_part, half]
        else:
            source, target = w_ref.at[index, :, half], heads.at[index, own_part, half]
        return remote(source, target, w_sems.at[0, index], w_sems.at[1, index], across)

    def w_pass(index):
        block = proj.at[0, other_part, half] if index == 3 else heads.at[index, other_part, half]
        return remote(block, block, pass_sems.at[0, index], pass_sems.at[1, index], partner)

    proj_pass = remote(proj.at[0], proj.at[1], proj_sems.at[0], proj_sems.at[1], beside)
    w_in_copy = remote(w_in_ref, w_in_far_out, w_in_sems.at[0], w_in_sems.at[1], across)
    for index in range(4):
        w_copy(index).start()
    w_local = pltpu.make_async_copy(w_ref, heads.at[:, own_part], local_sems.at[0])
    proj_local = pltpu.make_async_copy(proj_ref, proj.at[0, own_part], local_sems.at[1])
    w_local.start()
    proj_local.start()

    mine = pl.multiple_of(core * tok, tok)

    def first_norm(step, carry):
        at = pl.ds(pl.multiple_of(step * STRIP, STRIP), STRIP)
        scaled, _ = normalise(x_ref[at].astype(f32))
        normed[pl.ds(pl.multiple_of(HALF + mine + step * STRIP, STRIP), STRIP)] = (
            scaled * gain_one_ref[...][None, :] + shift_one_ref[...][None, :]
        ).astype(bf16)
        return carry

    lax.fori_loop(0, tok // STRIP, first_norm, 0)
    own_normed = normed.at[pl.ds(pl.multiple_of(HALF + mine, STRIP), tok)]
    normed_copy = remote(own_normed, own_normed, normed_sems.at[0], normed_sems.at[1], beside)
    normed_copy.start()

    wide = max(16, experts)
    own_routes = routes_ref[:, pl.ds(pl.multiple_of(mp * tok, tok), tok)]
    picked = own_routes == lax.broadcasted_iota(jnp.int32, (wide, tok), 0)
    earlier = lax.broadcasted_iota(jnp.int32, (tok, tok), 0) < lax.broadcasted_iota(jnp.int32, (tok, tok), 1)
    counts = dot(jnp.where(picked, 1.0, 0.0).astype(bf16), jnp.where(earlier, 1.0, 0.0).astype(bf16))
    rank = jnp.sum(jnp.where(picked, counts, 0.0), axis=0, keepdims=True)
    slot_of = own_routes.astype(f32) * slots + rank
    for strip in range(total // STRIP):
        ids = lax.broadcasted_iota(jnp.int32, (STRIP, tok), 0) + strip * STRIP
        placing[strip * STRIP : (strip + 1) * STRIP] = jnp.where(ids.astype(f32) == slot_of, 1.0, 0.0).astype(bf16)

    positions = mp * tok + lax.broadcasted_iota(jnp.int32, (1, tok), 1)
    factors = pick_sequence(positions, factor_ref)
    high = factors.astype(bf16)
    low = (factors - high.astype(f32)).astype(bf16)
    which = lax.broadcasted_iota(jnp.int32, (16, tok), 0)
    both = jnp.where(which == 0, high, jnp.where(which == 1, low, bf16(0)))
    spread = dot(both, placing[...], NT)

    def place_cot(step, carry):
        at = pl.ds(pl.multiple_of(step * STRIP, STRIP), STRIP)
        cot_send[at] = dot(placing[at], cot_ref[...]).astype(bf16)
        return carry

    lax.fori_loop(0, total // STRIP, place_cot, 0)
    spare = lax.broadcasted_iota(jnp.int32, (16, slots), 0) == cap - (slots - 16)
    for expert in range(experts):
        at = slice((expert + 1) * slots - 16, (expert + 1) * slots)
        here = slice(expert * slots, (expert + 1) * slots)
        for term, column in ((0, 0), (1, width // 2)):
            cot_send[at, column : column + slots] = jnp.where(
                spare, spread[term : term + 1, here], cot_send[at, column : column + slots].astype(f32)
            ).astype(bf16)

    def chunk(index):
        return pl.ds(pl.multiple_of(index * slots, 16), slots)

    def row_copy(target, source):
        return remote(
            cot_send.at[chunk(target)], cot_out.at[chunk(source)],
            row_send.at[target], row_recv.at[source], {"dp": target},
        )

    own_rows = pltpu.make_async_copy(cot_send.at[chunk(me)], cot_out.at[chunk(me)], local_sems.at[2])
    own_rows.start()
    for other in others:
        row_copy(other, me).start()
    for strip in range(total // STRIP):
        at = slice(strip * STRIP, (strip + 1) * STRIP)
        placing_t[:, at] = placing[at].T

    saves = []

    def save(source, target):
        copy = pltpu.make_async_copy(source, target, save_sems.at[len(saves)])
        copy.start()
        saves.append(copy)

    save(placing_t, placing_t_out)

    def pair_of(step):
        return (1 - chip) * step + chip * (PAIRS - 1 - step)

    def column(offset, pair):
        return pl.ds(pl.multiple_of((offset * PAIRS + pair) * PAIR, PAIR), PAIR)

    def project(step):
        pair = pair_of(step)
        weights = jnp.concatenate([heads[index, column(0, pair)] for index in range(3)])

        def strip_of(strip, carry):
            at = pl.ds(pl.multiple_of(strip * 512, 512), 512)
            value = dot(normed[pl.ds(pl.multiple_of(HALF + strip * 512, 512), 512)], weights, NT).astype(bf16)
            for index in range(3):
                qkv[at, column(index, pair)] = value[:, index * PAIR : (index + 1) * PAIR]
            return carry

        lax.fori_loop(0, 2 * tok // 512, strip_of, 0)

    lane = lax.broadcasted_iota(jnp.int32, (1, PAIR), 1)
    row = lax.broadcasted_iota(jnp.int32, (PAIR, 1), 0)

    def attend_block(pair, first, whole):
        span = (whole + 1) * BLOCK
        start = pl.multiple_of(first + HALF - whole * BLOCK, BLOCK)
        at = pl.ds(first, BLOCK)
        queries = qkv[at, column(0, pair)] * bf16(0.125)
        near = keys[pl.ds(start, span)]
        near_values = values[:, pl.ds(start, span)]
        parts = []
        for head in range(2):
            own = jnp.where((lane // HEAD_DIM) == head, queries, bf16(0))
            scores = mask_diagonal(dot(near, own, NT), whole)
            largest = jnp.max(scores, axis=0, keepdims=True)
            expo = jnp.exp(scores - largest)
            summed = jnp.sum(expo, axis=0, keepdims=True)
            parts.append(dot(near_values, expo.astype(bf16)) / summed)
            logs[pair, head : head + 1, at] = largest + jnp.log(summed)
        mixed[at, column(0, pair)] = jnp.where(row < HEAD_DIM, parts[0], parts[1]).T.astype(bf16)

    quarter = HALF // 2
    ext_rows = pl.ds(pl.multiple_of(core * quarter, quarter), quarter)
    ext_copy = remote(
        normed.at[pl.ds(pl.multiple_of(2 * tok + core * quarter, quarter), quarter)], normed.at[ext_rows],
        ext_sems.at[0, 0], ext_sems.at[1, 0], across,
    )
    ext_pass = remote(normed.at[ext_rows], normed.at[ext_rows], ext_sems.at[0, 1], ext_sems.at[1, 1], beside)
    w_local.wait()
    normed_copy.wait_recv()

    @pl.when(chip == 0)
    def _():
        ext_copy.start()

    w_in_copy.start()
    project(0)
    for index in range(4):
        w_copy(index).wait_recv()
        w_pass(index).start()

    def attention(step, carry):
        pair = pair_of(step)

        @pl.when(step == 1)
        def _():
            for index in range(3):
                w_pass(index).wait_recv()
            project(1)
            project(2)

        keys[HALF:] = qkv[:, column(1, pair)]
        values[:, HALF:] = qkv[:, column(2, pair)].T
        for whole in range(4):
            attend_block(pair, pl.multiple_of((2 * chip + whole) * BLOCK, BLOCK), whole)

        @pl.when(chip == 0)
        def _():
            attend_block(pair, 4 * BLOCK, 0)
            attend_block(pair, 5 * BLOCK, 1)

        return carry

    lax.fori_loop(0, PAIRS, attention, 0)
    save(qkv, qkv_out)
    save(heads, heads_out)
    proj_local.wait()
    w_pass(3).wait_recv()
    proj_pass.start()
    save(proj.at[0], proj_out)

    @pl.when(second)
    def _():
        ext_copy.wait_recv()
        ext_pass.start()
        ext_pass.wait_recv()
        for index in range(2):
            ext[:, index * PAIRS * PAIR : (index + 1) * PAIRS * PAIR] = dot(
                normed[0:HALF], heads[1 + index], NT
            ).astype(bf16)

        def late(pair, carry):
            keys[0:HALF] = ext[:, column(0, pair)]
            keys[HALF : 2 * HALF] = qkv[0:HALF, column(1, pair)]
            values[:, 0:HALF] = ext[:, column(1, pair)].T
            values[:, HALF : 2 * HALF] = qkv[0:HALF, column(2, pair)].T
            attend_block(pair, 0, 2)
            attend_block(pair, BLOCK, 3)
            return carry

        lax.fori_loop(0, PAIRS, late, 0)

    @pl.when(chip == 0)
    def _():
        ext_copy.wait_send()
        ext[...] = jnp.zeros_like(ext)
        normed[0:HALF] = jnp.zeros((HALF, width), bf16)

    @pl.when(second)
    def _():
        ext_pass.wait_send()

    save(normed, normed_out)
    save(ext, ext_out)
    save(mixed, mixed_out)
    save(logs, log_out)
    mixed_copy = remote(
        mixed.at[pl.ds(pl.multiple_of((1 - core) * tok, tok), tok)], mixed_far,
        mixed_sems.at[0], mixed_sems.at[1], beside,
    )
    mixed_copy.start()
    proj_pass.wait_recv()
    mixed_copy.wait_recv()

    def second_norm(step, carry):
        at = pl.ds(pl.multiple_of(step * STRIP, STRIP), STRIP)
        value = x_ref[at].astype(f32) + (
            dot(mixed[pl.ds(pl.multiple_of(mine + step * STRIP, STRIP), STRIP)], proj[0])
            + dot(mixed_far[at], proj[1])
        )
        hidden[at] = value
        scaled, _ = normalise(value)
        normed_two[at] = (scaled * gain_two_ref[...][None, :] + shift_two_ref[...][None, :]).astype(bf16)
        return carry

    lax.fori_loop(0, tok // STRIP, second_norm, 0)
    save(hidden, hidden_out)

    def place_rows(step, carry):
        at = pl.ds(pl.multiple_of(step * STRIP, STRIP), STRIP)
        rows[at] = dot(placing[at], normed_two[...]).astype(bf16)
        return carry

    lax.fori_loop(0, total // STRIP, place_rows, 0)
    save(rows, rows_out)
    own_rows.wait()
    for other in others:
        row_copy(me, other).wait_recv()
        row_copy(other, me).wait_send()
    for index in range(4):
        w_copy(index).wait_send()
        w_pass(index).wait_send()
    for copy in (proj_pass, normed_copy, mixed_copy):
        copy.wait_send()
    for copy in saves:
        copy.wait()
    w_in_copy.wait()


def run_forward(
    x, cotangent, routes, factor, gain_one, shift_one, gain_two, shift_two, w_heads, w_proj, w_in, experts, cap, slots
):
    tok, width = x.shape
    rows = 2 * tok
    total = experts * slots
    part = w_proj.shape[0]
    anyspace, vmem = pl.BlockSpec(memory_space=pl.ANY), pl.BlockSpec(memory_space=pltpu.VMEM)
    smem = pl.BlockSpec(memory_space=pltpu.SMEM)
    dma = pltpu.SemaphoreType.DMA
    kept = [
        ((HALF + rows, width), bf16),
        ((rows, 3 * PAIRS * PAIR), bf16),
        ((HALF, 2 * PAIRS * PAIR), bf16),
        ((rows, PAIRS * PAIR), bf16),
        ((PAIRS, 8, rows), f32),
        ((3, 2 * part, width), bf16),
    ]
    late = [((tok, width), f32), ((total, width), bf16)]
    return pl.pallas_call(
        functools.partial(forward_kernel, experts, slots, cap),
        in_specs=[vmem, vmem, vmem, smem] + [vmem] * 4 + [anyspace] * 3,
        out_specs=[anyspace] * 12,
        out_shape=[
            jax.ShapeDtypeStruct(*item)
            for item in kept
            + [((2 * part, width), bf16)]
            + late
            + [((total, width), bf16), ((tok, total), bf16), (w_in.shape, bf16)]
        ],
        scratch_shapes=[pltpu.VMEM(*item) for item in kept + [((2, 2 * part, width), bf16)] + late]
        + [
            pltpu.VMEM((total, tok), bf16),
            pltpu.VMEM((tok, total), bf16),
            pltpu.VMEM((total, width), bf16),
            pltpu.VMEM((tok, PAIRS * PAIR), bf16),
            pltpu.VMEM((tok, width), bf16),
            pltpu.VMEM((HALF + rows, PAIR), bf16),
            pltpu.VMEM((PAIR, HALF + rows), bf16),
            dma((2, 4)), dma((2, 4)), dma((2,)), dma((2,)), dma((2,)), dma((2, 2)), dma((2,)),
            dma((experts,)), dma((experts,)), dma((3,)), dma((10,)),
        ],
        compiler_params=pltpu.CompilerParams(
            collective_id=4, has_side_effects=True, vmem_limit_bytes=56 * 2**20
        ),
        cost_estimate=pl.CostEstimate(flops=30 * 10**9, bytes_accessed=30 * 10**6, transcendentals=8 * 10**6),
        name="forward",
    )(x, cotangent, routes, factor, gain_one, shift_one, gain_two, shift_two, w_heads, w_proj, w_in)


def backward_kernel(
    experts, slots,
    x_ref, cot_ref, factor_ref, hidden_ref, gain_one_ref, gain_two_ref, placing_ref, d_returned_ref,
    result_ref, normed_ref, qkv_ref, ext_ref, mixed_ref, log_ref, heads_ref, proj_ref, router_ref,
    there_in_ref, there_out_ref,
    output_ref, input_grad_ref, total_ref, small_ref, far_in_ref, far_out_ref,
    returned, d_hidden, d_branch, d_mixed, keys, values, d_keys, d_values, d_qkv, d_ext,
    grads_own, grads_send, grads_recv, d_norm, norm_recv, ext_recv,
    held, half_recv, piece_recv, small_held, small_recv,
    row_send, row_recv, branch_sems, norm_sems, ext_sems, far_sems, grad_sems,
    half_sems, piece_sems, gather_sems, back_sems, small_sems, local_sems,
):
    me, mp = lax.axis_index("dp"), lax.axis_index("mp")
    chip, core = mp // 2, mp % 2
    tok, width = x_ref.shape
    rows = 2 * tok
    part = grads_own.shape[1]
    all_heads = PAIRS * PAIR
    beside = {"mp": mp + 1 - 2 * core}
    across = {"mp": (mp + 2) % 4}
    second = chip == 1
    others = [(me + k) % experts for k in range(1, experts)]
    greet([{"dp": other} for other in others] + [beside, across])

    def chunk(index):
        return pl.ds(pl.multiple_of(index * slots, 16), slots)

    def row_copy(target, source):
        return remote(
            result_ref.at[chunk(target)], returned.at[chunk(source)],
            row_send.at[target], row_recv.at[source], {"dp": target},
        )

    def far_copy(index):
        source, target = ((there_out_ref, far_out_ref), (there_in_ref, far_in_ref))[index]
        return remote(source, target, far_sems.at[0, index], far_sems.at[1, index], across)

    far_copy(0).start()
    own_rows = pltpu.make_async_copy(result_ref.at[chunk(me)], returned.at[chunk(me)], local_sems.at[0])
    own_rows.start()
    for other in others:
        row_copy(other, me).start()

    cot_copy = pltpu.make_async_copy(cot_ref, grads_send, local_sems.at[1])
    cot_copy.start()
    cot_copy.wait()
    small_held[...] = jnp.zeros_like(small_held)
    mine = pl.multiple_of(core * tok, tok)

    def second_norm(step, carry):
        at = pl.ds(pl.multiple_of(step * STRIP, STRIP), STRIP)
        scaled, inverse = normalise(hidden_ref[at])
        d_normed = dot(placing_ref[at], d_returned_ref[...])
        small_held[0, 2:3] += jnp.sum(d_normed * scaled, axis=0, keepdims=True)
        small_held[0, 3:4] += jnp.sum(d_normed, axis=0, keepdims=True)
        positions = mp * tok + step * STRIP + lax.broadcasted_iota(jnp.int32, (STRIP, 1), 0)
        total = grads_send[at].astype(f32) * pick_sequence(positions, factor_ref) + norm_pull(
            d_normed, scaled, inverse, gain_two_ref[...][None, :]
        )
        d_hidden[at] = total
        d_branch[pl.ds(pl.multiple_of(mine + step * STRIP, STRIP), STRIP)] = total.astype(bf16)
        return carry

    lax.fori_loop(0, tok // STRIP, second_norm, 0)
    own_branch = d_branch.at[pl.ds(mine, tok)]
    branch_copy = remote(own_branch, own_branch, branch_sems.at[0], branch_sems.at[1], beside)
    branch_copy.start()
    branch_copy.wait()

    def push_branch(step, carry):
        at = pl.ds(pl.multiple_of(step * STRIP, STRIP), STRIP)
        d_mixed[at] = dot(d_branch[at], proj_ref[...], NT).astype(bf16)
        return carry

    lax.fori_loop(0, rows // STRIP, push_branch, 0)

    side, line = me % 2, me // 2
    lines = experts // 2
    partner = {"dp": me + 1 - 2 * side}
    mates = [(line + k) % lines for k in range(1, lines)]
    piece_rows = held.shape[1] // lines
    own_columns = pl.ds(pl.multiple_of(side * (width // 2), 128), width // 2)
    other_columns = pl.ds(pl.multiple_of((1 - side) * (width // 2), 128), width // 2)

    def piece(index):
        return pl.ds(pl.multiple_of(index * piece_rows, 16), piece_rows)

    def sent(index):
        return slice(index * part, (index + 1) * part)

    def grad_copy(index):
        return remote(
            grads_send.at[sent(index)], grads_recv.at[index], grad_sems.at[0, index], grad_sems.at[1, index], across
        )

    def half_copy(index):
        return remote(
            held.at[index, :, other_columns], half_recv.at[index],
            half_sems.at[0, index], half_sems.at[1, index], partner,
        )

    def piece_copy(index, target, source):
        return remote(
            held.at[index, piece(target), own_columns], piece_recv.at[index, source],
            piece_sems.at[0, index, target], piece_sems.at[1, index, source], {"dp": 2 * target + side},
        )

    def gather_copy(index, target, source):
        block = total_ref.at[index, piece(source), own_columns]
        return remote(
            block, block,
            gather_sems.at[0, index, target], gather_sems.at[1, index, source], {"dp": 2 * target + side},
        )

    def back_copy(index):
        block = total_ref.at[index, :, own_columns]
        return remote(block, block, back_sems.at[0, index], back_sems.at[1, index], partner)

    def send_grad(index, grad):
        for own in range(2):

            @pl.when(chip == own)
            def _():
                grads_own[index] = grad[own * part : (own + 1) * part]
                grads_send[sent(index)] = grad[(1 - own) * part : (2 - own) * part].astype(bf16)

        grad_copy(index).start()

    chunks = held.shape[0]
    parts = 4 // chunks

    def stage_one(index):
        if index >= chunks:
            return
        for at in range(parts):
            number = index * parts + at
            grad_copy(number).wait_recv()
            held[index, at * part : (at + 1) * part] = (
                grads_own[number] + grads_recv[number].astype(f32)
            ).astype(bf16)
        if held.shape[1] > parts * part:
            held[index, parts * part :] = jnp.zeros((held.shape[1] - parts * part, width), bf16)
        half_copy(index).start()

    def stage_two(index):
        if index >= chunks:
            return
        half_copy(index).wait_recv()
        held[index, :, own_columns] = (
            held[index, :, own_columns].astype(f32) + half_recv[index].astype(f32)
        ).astype(bf16)
        for mate in mates:
            piece_copy(index, mate, line).start()

    def stage_three(index):
        if index >= chunks:
            return
        value = held[index, piece(line), own_columns].astype(f32)
        for mate in mates:
            piece_copy(index, line, mate).wait_recv()
            value += piece_recv[index, mate].astype(f32)
        total_ref[index, piece(line), own_columns] = value.astype(bf16)
        for mate in mates:
            gather_copy(index, mate, line).start()

    def stage_four(index):
        if index >= chunks:
            return
        for mate in mates:
            gather_copy(index, line, mate).wait_recv()
        back_copy(index).start()

    send_grad(0, dot(mixed_ref[...], d_branch[...], TN))

    lane = lax.broadcasted_iota(jnp.int32, (1, PAIR), 1)

    def attention(pair, carry):
        def column(offset):
            return pl.ds(pl.multiple_of((offset * PAIRS + pair) * PAIR, PAIR), PAIR)

        keys[0:HALF] = ext_ref[:, column(0)]
        keys[HALF:] = qkv_ref[:, column(1)]
        values[0:HALF] = ext_ref[:, column(1)]
        values[HALF:] = qkv_ref[:, column(2)]
        d_keys[...] = jnp.zeros_like(d_keys)
        d_values[...] = jnp.zeros_like(d_values)

        def run(first, whole):
            span = (whole + 1) * BLOCK
            start = pl.multiple_of(first + HALF - whole * BLOCK, BLOCK)
            at = pl.ds(first, BLOCK)
            queries = qkv_ref[at, column(0)] * bf16(0.125)
            d_out = d_mixed[at, column(0)]
            near = keys[pl.ds(start, span)]
            near_values = values[pl.ds(start, span)]
            product = (d_out.astype(f32) * mixed_ref[at, column(0)].astype(f32)).T
            dq = dk = dv = 0.0
            for head in range(2):
                here = (lane // HEAD_DIM) == head
                own = jnp.where(here, queries, bf16(0))
                d_own = jnp.where(here, d_out, bf16(0))
                delta = jnp.sum(product[HEAD_DIM * head : HEAD_DIM * (head + 1)], axis=0, keepdims=True)
                scores = mask_diagonal(dot(near, own, NT), whole)
                probs = jnp.exp(scores - log_ref[pair, head : head + 1, at])
                d_probs = dot(near_values, d_own, NT)
                d_scores = (probs * (d_probs - delta)).astype(bf16)
                dv = dv + dot(probs.astype(bf16), d_own)
                dk = dk + dot(d_scores, own)
                dq = dq + dot(d_scores, jnp.where(here, near, bf16(0)), TN)
            d_qkv[at, column(0)] = (dq * 0.125).astype(bf16)
            d_keys[pl.ds(start, span)] += dk
            d_values[pl.ds(start, span)] += dv

        for whole in range(4):
            run(pl.multiple_of((2 * chip + whole) * BLOCK, BLOCK), whole)

        @pl.when(second)
        def _():
            run(0, 2)
            run(BLOCK, 3)

        @pl.when(chip == 0)
        def _():
            run(4 * BLOCK, 0)
            run(5 * BLOCK, 1)

        d_qkv[:, column(1)] = d_keys[HALF:].astype(bf16)
        d_qkv[:, column(2)] = d_values[HALF:].astype(bf16)
        d_ext[:, column(0)] = d_keys[0:HALF].astype(bf16)
        d_ext[:, column(1)] = d_values[0:HALF].astype(bf16)
        return carry

    lax.fori_loop(0, PAIRS, attention, 0)

    norm_send, ext_part = d_branch.at[0:tok], d_branch.at[tok : tok + HALF]

    ext_beside = remote(ext_part, ext_recv, ext_sems.at[0, 0], ext_sems.at[1, 0], beside)
    ext_across = remote(ext_part, ext_recv, ext_sems.at[0, 1], ext_sems.at[1, 1], across)

    @pl.when(second)
    def _():
        ext_part[...] = dot(d_ext[...], heads_ref[1:3].reshape(2 * all_heads, width)).astype(bf16)

    @pl.when(mp == 2)
    def _():
        ext_beside.start()

    send_grad(1, dot(d_qkv[:, 0:all_heads], normed_ref[HALF:], TN))

    @pl.when(mp == 3)
    def _():
        ext_beside.wait_recv()
        ext_part[...] = (ext_part[...].astype(f32) + ext_recv[...].astype(f32)).astype(bf16)
        ext_across.start()

    for index in (1, 2):
        at = slice(index * all_heads, (index + 1) * all_heads)
        send_grad(
            1 + index,
            dot(d_qkv[:, at], normed_ref[HALF:], TN)
            + dot(d_ext[:, (index - 1) * all_heads : index * all_heads], normed_ref[0:HALF], TN),
        )
    stage_one(0)

    weights = heads_ref[...].reshape(3 * all_heads, width)

    def push_norm(step, carry):
        at = pl.ds(pl.multiple_of((1 - core) * tok + step * STRIP, STRIP), STRIP)
        norm_send[pl.ds(pl.multiple_of(step * STRIP, STRIP), STRIP)] = dot(d_qkv[at], weights).astype(bf16)
        return carry

    def pull_norm(step, carry):
        at = pl.ds(pl.multiple_of(mine + step * STRIP, STRIP), STRIP)
        d_norm[pl.ds(pl.multiple_of(step * STRIP, STRIP), STRIP)] = dot(d_qkv[at], weights)
        return carry

    lax.fori_loop(0, tok // STRIP, push_norm, 0)
    norm_copy = remote(norm_send, norm_recv, norm_sems.at[0], norm_sems.at[1], beside)
    norm_copy.start()
    lax.fori_loop(0, tok // STRIP, pull_norm, 0)
    stage_two(0)
    own_rows.wait()
    for other in others:
        row_copy(me, other).wait_recv()

    def finish(step, carry):
        at = pl.ds(pl.multiple_of(step * STRIP, STRIP), STRIP)
        output_ref[at] = (hidden_ref[at] + dot(placing_ref[at], returned[...])).astype(bf16)
        return carry

    lax.fori_loop(0, tok // STRIP, finish, 0)
    stage_three(0)
    norm_copy.wait_recv()

    @pl.when(mp == 1)
    def _():
        ext_across.wait_recv()
        d_norm[tok - HALF :] += ext_recv[...].astype(f32)

    def first_norm(step, carry):
        at = pl.ds(pl.multiple_of(step * STRIP, STRIP), STRIP)
        scaled, inverse = normalise(x_ref[at].astype(f32))
        d_normed = d_norm[at] + norm_recv[at].astype(f32)
        small_held[0, 0:1] += jnp.sum(d_normed * scaled, axis=0, keepdims=True)
        small_held[0, 1:2] += jnp.sum(d_normed, axis=0, keepdims=True)
        input_grad_ref[at] = (
            d_hidden[at] + norm_pull(d_normed, scaled, inverse, gain_one_ref[...][None, :])
        ).astype(bf16)
        return carry

    lax.fori_loop(0, tok // STRIP, first_norm, 0)

    small_rows = lax.broadcasted_iota(jnp.int32, small_ref.shape, 0)
    small_held[0] = jnp.where(small_rows == 8 + me, router_ref[...], small_held[0])

    small_devices = [across, beside, partner]
    stride = 1
    while stride < lines:
        mate = line + stride * (1 - 2 * (line // stride % 2))
        small_devices.append({"dp": 2 * mate + side})
        stride *= 2

    def small_step(index):
        return remote(
            small_held.at[index], small_recv.at[index],
            small_sems.at[0, index], small_sems.at[1, index], small_devices[index],
        )

    def small_sum(index):
        small_step(index).wait_recv()
        small_held[index + 1] = small_held[index] + small_recv[index]

    small_step(0).start()
    far_copy(1).start()
    stage_one(1)
    stage_four(0)
    stage_two(1)
    stage_one(2)
    small_sum(0)
    small_step(1).start()
    stage_three(1)
    stage_two(2)
    stage_one(3)
    small_sum(1)
    small_step(2).start()
    stage_four(1)
    stage_three(2)
    stage_two(3)
    small_sum(2)
    small_step(3).start()
    stage_four(2)
    small_sum(3)
    for index in range(4, len(small_devices)):
        small_step(index).start()
        if index == 4:
            stage_three(3)
        small_sum(index)
    small_ref[...] = small_held[len(small_devices)]
    stage_four(3)
    for index in range(chunks):
        other = total_ref.at[index, :, other_columns]
        remote(other, other, back_sems.at[0, index], back_sems.at[1, index], partner).wait_recv()

    for other in others:
        row_copy(other, me).wait_send()
    for mate in mates:
        for index in range(chunks):
            piece_copy(index, mate, line).wait_send()
            gather_copy(index, mate, line).wait_send()
    for index in range(4):
        grad_copy(index).wait_send()
    for index in range(chunks):
        half_copy(index).wait_send()
        back_copy(index).wait_send()
    for index in range(len(small_devices)):
        small_step(index).wait_send()
    norm_copy.wait_send()

    @pl.when(mp == 2)
    def _():
        ext_beside.wait_send()

    @pl.when(mp == 3)
    def _():
        ext_across.wait_send()

    for index in range(2):
        far_copy(index).wait()


def run_backward(
    x, cotangent, factor, hidden, gain_one, gain_two, placing, d_returned, result, normed, qkv, ext,
    mixed, log_total, heads, proj, router_grad, there_in, there_out, experts,
):
    tok, width = x.shape
    rows = 2 * tok
    total = d_returned.shape[0]
    part = proj.shape[0] // 2
    lines = experts // 2
    steps = 3 + (lines - 1).bit_length()
    chunks = 4 if part % (16 * lines) == 0 else 2
    padded = (4 // chunks * part + 16 * lines - 1) // (16 * lines) * (16 * lines)
    small = (8 + max(8, experts), width)
    anyspace, vmem = pl.BlockSpec(memory_space=pl.ANY), pl.BlockSpec(memory_space=pltpu.VMEM)
    smem = pl.BlockSpec(memory_space=pltpu.SMEM)
    dma = pltpu.SemaphoreType.DMA
    return pl.pallas_call(
        functools.partial(backward_kernel, experts, total // experts),
        in_specs=[vmem, anyspace, smem] + [vmem] * 5 + [anyspace] + [vmem] * 8 + [anyspace] * 2,
        out_specs=[vmem] * 4 + [anyspace] * 2,
        out_shape=[
            jax.ShapeDtypeStruct((tok, width), bf16),
            jax.ShapeDtypeStruct((tok, width), bf16),
            jax.ShapeDtypeStruct((chunks, padded, width), bf16),
            jax.ShapeDtypeStruct(small, f32),
            jax.ShapeDtypeStruct(there_in.shape, bf16),
            jax.ShapeDtypeStruct(there_out.shape, bf16),
        ],
        scratch_shapes=[
            pltpu.VMEM((total, width), bf16),
            pltpu.VMEM((tok, width), f32),
            pltpu.VMEM((rows, width), bf16),
            pltpu.VMEM((rows, PAIRS * PAIR), bf16),
            pltpu.VMEM((HALF + rows, PAIR), bf16),
            pltpu.VMEM((HALF + rows, PAIR), bf16),
            pltpu.VMEM((HALF + rows, PAIR), f32),
            pltpu.VMEM((HALF + rows, PAIR), f32),
            pltpu.VMEM((rows, 3 * PAIRS * PAIR), bf16),
            pltpu.VMEM((HALF, 2 * PAIRS * PAIR), bf16),
            pltpu.VMEM((4, part, width), f32),
            pltpu.VMEM((4 * part, width), bf16),
            pltpu.VMEM((4, part, width), bf16),
            pltpu.VMEM((tok, width), f32),
            pltpu.VMEM((tok, width), bf16),
            pltpu.VMEM((HALF, width), bf16),
            pltpu.VMEM((chunks, padded, width), bf16),
            pltpu.VMEM((chunks, padded, width // 2), bf16),
            pltpu.VMEM((chunks, lines, padded // lines, width // 2), bf16),
            pltpu.VMEM((steps + 1,) + small, f32),
            pltpu.VMEM((steps,) + small, f32),
            dma((experts,)), dma((experts,)), dma((2,)), dma((2,)), dma((2, 2)), dma((2, 2)), dma((2, 4)),
            dma((2, chunks)), dma((2, chunks, lines)), dma((2, chunks, lines)), dma((2, chunks)),
            dma((2, steps)), dma((2,)),
        ],
        compiler_params=pltpu.CompilerParams(
            collective_id=2, has_side_effects=True, vmem_limit_bytes=62 * 2**20
        ),
        cost_estimate=pl.CostEstimate(flops=30 * 10**9, bytes_accessed=30 * 10**6, transcendentals=8 * 10**6),
        name="backward",
    )(
        x, cotangent, factor, hidden, gain_one, gain_two, placing, d_returned, result, normed, qkv, ext,
        mixed, log_total, heads, proj, router_grad, there_in, there_out,
    )


def gelu_parts(pre):
    scale = 0.7978845608028654
    square = pre * pre
    inner = jnp.tanh(pre * (scale + (scale * 0.044715) * square))
    half = 0.5 * (1.0 + inner)
    slope = half + (0.5 * pre) * (1.0 - inner * inner) * (scale + (3.0 * scale * 0.044715) * square)
    return pre * half, slope

STAGES = 4

def expert_kernel(
    experts, slots, cap,
    rows_ref, cot_ref, router_ref, w_in_ref, w_out_ref, w_in_far_ref,
    back_ref, result_ref, router_grad_ref, here_in_ref, here_out_ref, there_in_ref, there_out_ref,
    router, factor, x, wi, wo, d_out, act, d_pre, total, d_x, give, g_send, g_recv,
    row_send, row_recv, back_send, back_recv, w_send, w_recv, g_send_sem, g_recv_sem, local_sem,
):
    me = lax.axis_index("dp")
    mp = lax.axis_index("mp")
    beside = {"mp": mp + 1 - 2 * (mp % 2)}
    across = {"mp": (mp + 2) % 4}
    members = experts // STAGES
    span = members * slots
    own_group, own_member = me // members, me % members

    def group_of(stage):
        return 2 * ((own_group // 2 + stage // 2) % 2) + (own_group % 2 + stage % 2) % 2

    def chunk(index):
        return pl.ds(pl.multiple_of(index * slots, 16), slots)

    def group_rows(group):
        return pl.ds(pl.multiple_of(group * span, 16), span)

    barrier = pltpu.get_barrier_semaphore()

    def greet(step, carry):
        pl.semaphore_signal(barrier, inc=1, device_id={"dp": (me + step) % experts}, device_id_type=MESH)
        return carry

    lax.fori_loop(1, experts, greet, 0)
    pl.semaphore_signal(barrier, inc=1, device_id=beside, device_id_type=MESH)
    pl.semaphore_signal(barrier, inc=1, device_id=across, device_id_type=MESH)
    pl.semaphore_wait(barrier, experts + 1)

    def remote(src, dst, send, recv, device):
        return pltpu.make_async_remote_copy(
            src_ref=src, dst_ref=dst, send_sem=send, recv_sem=recv, device_id=device, device_id_type=MESH
        )

    def row_copy(target, source):
        return remote(rows_ref.at[chunk(target)], x.at[chunk(source)], row_send.at[target], row_recv.at[source], {"dp": target})

    def back_copy(target, source):
        return remote(give.at[chunk(target)], back_ref.at[chunk(source)], back_send.at[target], back_recv.at[source], {"dp": target})

    def partners(stage):
        group = group_of(stage)
        if stage == 0:
            return [group * members + (own_member + k) % members for k in range(1, members)]
        return [group * members + (own_member + k) % members for k in range(members)]

    for stage in reversed(range(STAGES)):
        for other in partners(stage):
            row_copy(other, me).start()
    own_rows = pltpu.make_async_copy(rows_ref.at[chunk(me)], x.at[chunk(me)], local_sem.at[0])
    own_in = pltpu.make_async_copy(w_in_ref, wi.at[0], local_sem.at[1])
    own_out = pltpu.make_async_copy(w_out_ref, wo.at[0], local_sem.at[2])
    far_in = pltpu.make_async_copy(w_in_far_ref, wi.at[2], local_sem.at[3])
    near_in = remote(w_in_ref, wi.at[1], w_send.at[0], w_recv.at[0], beside)
    near_out = remote(w_out_ref, wo.at[1], w_send.at[1], w_recv.at[1], beside)
    far_near_in = remote(w_in_far_ref, wi.at[3], w_send.at[2], w_recv.at[2], beside)
    far_out = remote(w_out_ref, wo.at[2], w_send.at[3], w_recv.at[3], across)
    far_near_out = remote(wo.at[2], wo.at[3], w_send.at[4], w_recv.at[4], beside)
    for copy in (own_rows, own_in, own_out, near_in, near_out, far_in, far_out, far_near_in):
        copy.start()
    router_grad_ref[...] = jnp.zeros_like(router_grad_ref)
    router[...] = router_ref[...].astype(f32)

    diagonal = lax.broadcasted_iota(jnp.int32, (slots, slots), 0) == lax.broadcasted_iota(
        jnp.int32, (slots, slots), 1
    )

    def prepare(stage, rows):
        for member in range(members):
            index = group_of(stage) * members + member
            spare = cot_ref[pl.ds(pl.multiple_of((index + 1) * slots - 16, 16), 16)].astype(f32)
            spare = spare[cap - slots + 16 : cap - slots + 17]
            value = spare[:, 0:slots] + spare[:, x.shape[1] // 2 : x.shape[1] // 2 + slots]
            factor[chunk(index)] = jnp.sum(jnp.where(diagonal, value, 0.0), axis=1, keepdims=True)
        features = x[rows].astype(f32)
        gate = jax.nn.sigmoid(jnp.sum(features * router[pl.ds(me, 1)], axis=1, keepdims=True))
        d_out[rows] = (gate * (cot_ref[rows].astype(f32) * factor[rows])).astype(bf16)
        total[rows] = jnp.zeros((span, x.shape[1]), f32)
        d_x[rows] = jnp.zeros((span, x.shape[1]), f32)

    def finish(stage, rows):
        features = x[rows].astype(f32)
        gate = jax.nn.sigmoid(jnp.sum(features * router[pl.ds(me, 1)], axis=1, keepdims=True))
        value = total[rows]
        d_gate = jnp.sum(cot_ref[rows].astype(f32) * factor[rows] * value, axis=1, keepdims=True)
        d_logit = (d_gate * gate * (1.0 - gate)).astype(bf16).astype(f32)
        give[rows] = (d_x[rows] + d_logit * router[pl.ds(me, 1)]).astype(bf16)
        result_ref[rows] = (gate * value).astype(bf16)
        router_grad_ref[...] += jnp.sum(features * d_logit, axis=0, keepdims=True)

    def stage_of(step):
        return jnp.where(
            (step < 2) | (step >= 14), 0, jnp.where(step < 6, 3, jnp.where(step < 10, 2, 1))
        )

    def step_body(step, carry):
        stage = stage_of(step)
        part = jnp.where(step < 4, step % 2, jnp.where(step < 6, step - 2, (step - 6) % 4))
        part = jnp.where(step >= 14, step - 12, part)
        rows = group_rows(group_of(stage))

        for static, at in enumerate((0, 10, 6, 2)):
            @pl.when(step == at)
            def _():
                if static == 0:
                    own_rows.wait()
                for other in partners(static):
                    row_copy(me, other).wait_recv()
        @pl.when((step == 0) | (step == 2) | (step == 6) | (step == 10))
        def _():
            prepare(stage, rows)

        @pl.when(step == 0)
        def _():
            own_in.wait()
            own_out.wait()

        @pl.when(step == 1)
        def _():
            near_in.wait_recv()
            near_out.wait_recv()

        @pl.when(step == 4)
        def _():
            far_in.wait()
            far_out.wait_recv()
            far_near_out.start()

        @pl.when(step == 5)
        def _():
            far_near_in.wait_recv()
            far_near_out.wait_recv()

        pre = dot(x[rows], wi[part])
        value, slope = gelu_parts(pre)
        value = value.astype(bf16)
        act[part, rows] = value
        total[rows] += dot(value, wo[part])
        d_value = (dot(d_out[rows], wo[part], NT) * slope).astype(bf16)
        d_pre[part, rows] = d_value
        d_x[rows] += dot(d_value, wi[part], NT)

        @pl.when((step == 5) | (step == 9) | (step == 13) | (step == 15))
        def _():
            finish(stage, rows)

        for static, at in enumerate((15, 13, 9, 5)):
            @pl.when(step == at)
            def _():
                for other in partners(static):
                    back_copy(other, me).start()
        return carry

    lax.fori_loop(0, 16, step_body, 0)
    own_back = pltpu.make_async_copy(give.at[chunk(me)], back_ref.at[chunk(me)], local_sem.at[4])
    own_back.start()

    def grad_copy(index):
        return remote(outgoing[index], g_recv.at[index], g_send_sem.at[index], g_recv_sem.at[index], beside)

    kept = pl.ds(0, x.shape[1])
    outgoing = [g_send, act.at[3, kept], d_pre.at[3, kept], act.at[1, kept]]
    for index, part in enumerate((3, 1)):
        outgoing[2 * index][...] = dot(act[part], d_out[...], TN).astype(bf16)
        grad_copy(2 * index).start()
        outgoing[2 * index + 1][...] = dot(x[...], d_pre[part], TN).astype(bf16)
        grad_copy(2 * index + 1).start()
    grad = dot(act[2], d_out[...], TN)
    grad_copy(0).wait_recv()
    there_out_ref[...] = (grad + g_recv[0].astype(f32)).astype(bf16)
    grad = dot(x[...], d_pre[2], TN)
    grad_copy(1).wait_recv()
    there_in_ref[...] = (grad + g_recv[1].astype(f32)).astype(bf16)
    grad = dot(act[0], d_out[...], TN)
    grad_copy(2).wait_recv()
    here_out_ref[...] = grad + g_recv[2].astype(f32)
    grad = dot(x[...], d_pre[0], TN)
    grad_copy(3).wait_recv()
    here_in_ref[...] = grad + g_recv[3].astype(f32)

    own_back.wait()
    for stage in range(STAGES):
        for other in partners(stage):
            back_copy(me, other).wait_recv()
            back_copy(other, me).wait_send()
            row_copy(other, me).wait_send()
    for copy in (near_in, near_out, far_near_in, far_out, far_near_out):
        copy.wait_send()
    for index in range(4):
        grad_copy(index).wait_send()


def run_expert(rows, cot_rows, router, w_in, w_out, w_in_far, experts, cap):
    total, width = rows.shape
    slots = total // experts
    hidden = w_in.shape[1]
    anyspace, vmem = pl.BlockSpec(memory_space=pl.ANY), pl.BlockSpec(memory_space=pltpu.VMEM)
    dma = pltpu.SemaphoreType.DMA
    return pl.pallas_call(
        functools.partial(expert_kernel, experts, slots, cap),
        in_specs=[anyspace, vmem, vmem, anyspace, anyspace, anyspace],
        out_specs=[vmem] * 7,
        out_shape=[
            jax.ShapeDtypeStruct((total, width), bf16),
            jax.ShapeDtypeStruct((total, width), bf16),
            jax.ShapeDtypeStruct((1, width), f32),
            jax.ShapeDtypeStruct((width, hidden), f32),
            jax.ShapeDtypeStruct((hidden, width), f32),
            jax.ShapeDtypeStruct((width, hidden), bf16),
            jax.ShapeDtypeStruct((hidden, width), bf16),
        ],
        scratch_shapes=[
            pltpu.VMEM(router.shape, f32),
            pltpu.VMEM((total, 1), f32),
            pltpu.VMEM((total, width), bf16),
            pltpu.VMEM((4, width, hidden), bf16),
            pltpu.VMEM((4, hidden, width), bf16),
            pltpu.VMEM((total, width), bf16),
            pltpu.VMEM((4, total, hidden), bf16),
            pltpu.VMEM((4, total, hidden), bf16),
            pltpu.VMEM((total, width), f32),
            pltpu.VMEM((total, width), f32),
            pltpu.VMEM((total, width), bf16),
            pltpu.VMEM((width, width), bf16),
            pltpu.VMEM((4, width, width), bf16),
            dma((experts,)), dma((experts,)), dma((experts,)), dma((experts,)),
            dma((5,)), dma((5,)), dma((4,)), dma((4,)), dma((5,)),
        ],
        compiler_params=pltpu.CompilerParams(
            collective_id=1, has_side_effects=True, vmem_limit_bytes=60 * 2**20
        ),
        cost_estimate=pl.CostEstimate(flops=30 * 10**9, bytes_accessed=40 * 10**6, transcendentals=3 * 10**6),
        name="expert",
    )(rows, cot_rows, router, w_in, w_out, w_in_far)


def shards(
    inputs, cotangent, routes, domains, domain_counts, domain_weights, keep_mask, gain_one, shift_one,
    w_qkv, w_proj, gain_two, shift_two, w_router, w_in, w_out,
):
    tok, width = inputs.shape
    experts = w_router.shape[1]
    cap = max(2, tok * 5 // (4 * experts))
    slots = (cap + 16) // 16 * 16
    domain_ids = jnp.arange(domain_weights.shape[0], dtype=jnp.int32)
    same_domain = domains[:, None] == domain_ids[None, :]
    seq_weight = jnp.sum(jnp.where(same_domain, domain_weights[None, :], 0.0), axis=1)
    seq_counts = jnp.sum(jnp.where(same_domain, domain_counts[None, :], 0), axis=1).astype(f32)
    factor = keep_mask.astype(f32) * seq_weight * count_scale / seq_counts

    w_own = jnp.transpose(w_qkv, (1, 2, 0))
    normed, qkv, ext, mixed, log_total, heads, proj, hidden, rows, cot_rows, placing_t, w_in_far = run_forward(
        inputs, cotangent, routes.reshape(1, -1), factor, gain_one, shift_one, gain_two,
        shift_two, w_own, w_proj, w_in[0], experts, cap, slots,
    )
    d_returned, result, router_grad, here_in, here_out, there_in, there_out = run_expert(
        rows, cot_rows, w_router.T, w_in[0], w_out[0], w_in_far, experts, cap
    )
    output, input_grad, sums, small, far_in, far_out = run_backward(
        inputs, cotangent, factor, hidden, gain_one, gain_two, placing_t, d_returned, result,
        normed, qkv, ext, mixed, log_total, heads, proj, router_grad, there_in, there_out, experts,
    )
    part = w_proj.shape[0]
    sums = sums[:, : 4 * part // sums.shape[0]].reshape(4, part, -1)
    return (
        output,
        input_grad,
        small[0],
        small[1],
        jnp.transpose(sums[1:].astype(f32), (2, 0, 1)),
        sums[0].astype(f32),
        small[2],
        small[3],
        small[8 : 8 + experts].T,
        (here_in + far_in.astype(f32))[None],
        (here_out + far_out.astype(f32))[None],
    )


def solution(mesh):
    tokens, group = P(("dp", "mp"), None), P("dp")
    return jax.shard_map(
        shards,
        mesh=mesh,
        in_specs=(
            tokens, tokens, P("dp", None), group, P(), P(), group, P(), P(),
            P(None, None, "mp"), P("mp", None), P(), P(), P(),
            P("dp", None, "mp"), P("dp", "mp", None),
        ),
        out_specs=(
            tokens, tokens, P(), P(), P(None, None, "mp"), P("mp", None), P(), P(), P(),
            P("dp", None, "mp"), P("dp", "mp", None),
        ),
        check_vma=False,
    )
```

```python
import functools

import jax
import jax.numpy as jnp
from jax import lax
from jax.experimental import pallas as pl
from jax.experimental.pallas import tpu as pltpu
from jax.sharding import PartitionSpec as P

HEAD_DIM = 64
LEN = 1024
BLOCK = 256
HALF = LEN // 2

norm_epsilon = 1e-05
count_scale = 10.0
masked_score = -1e30

f32 = jnp.float32
bf16 = jnp.bfloat16
MESH = pl.DeviceIdType.MESH
NT = (((1,), (1,)), ((), ()))
NN = (((1,), (0,)), ((), ()))
TN = (((0,), (0,)), ((), ()))


def dot(left, right, dims=NN):
    return lax.dot_general(left, right, dims, preferred_element_type=f32)


def mask_diagonal(scores, whole):
    first = lax.broadcasted_iota(jnp.int32, (BLOCK, BLOCK), 0)
    second = lax.broadcasted_iota(jnp.int32, (BLOCK, BLOCK), 1)
    last = jnp.where(first <= second, scores[whole * BLOCK :], masked_score)
    if not whole:
        return last
    return jnp.concatenate([scores[: whole * BLOCK], last], axis=0)


def remote(src, dst, send, recv, device):
    return pltpu.make_async_remote_copy(
        src_ref=src, dst_ref=dst, send_sem=send, recv_sem=recv, device_id=device, device_id_type=MESH
    )


def greet(devices):
    barrier = pltpu.get_barrier_semaphore()
    for device in devices:
        pl.semaphore_signal(barrier, inc=1, device_id=device, device_id_type=MESH)
    pl.semaphore_wait(barrier, len(devices))


def normalise(values):
    centre = values - jnp.mean(values, axis=-1, keepdims=True)
    inverse = lax.rsqrt(jnp.mean(centre * centre, axis=-1, keepdims=True) + norm_epsilon)
    return centre * inverse, inverse


def norm_pull(d_normed, scaled, inverse, gain):
    d_scaled = d_normed * gain
    return inverse * (
        d_scaled
        - jnp.mean(d_scaled, axis=-1, keepdims=True)
        - scaled * jnp.mean(d_scaled * scaled, axis=-1, keepdims=True)
    )


PAIRS = 3
PAIR = 2 * HEAD_DIM
STRIP = 256


def pick_sequence(positions, factor_ref):
    value = jnp.full(positions.shape, factor_ref[0], f32)
    for index in range(1, factor_ref.shape[0]):
        value = jnp.where(positions >= index * LEN, factor_ref[index], value)
    return value


def forward_kernel(
    experts, slots, cap,
    x_ref, cot_ref, routes_ref, factor_ref, gain_one_ref, shift_one_ref, gain_two_ref, shift_two_ref,
    w_ref, proj_ref, w_in_ref,
    normed_out, qkv_out, ext_out, mixed_out, log_out, heads_out, proj_out, hidden_out, rows_out, cot_out,
    placing_t_out, w_in_far_out,
    normed, qkv, ext, mixed, logs, heads, proj, hidden, rows, placing, placing_t, cot_send, mixed_far, normed_two,
    keys, values,
    w_sems, pass_sems, proj_sems, w_in_sems, normed_sems, ext_sems, mixed_sems, row_send, row_recv, local_sems,
    save_sems,
):
    me, mp = lax.axis_index("dp"), lax.axis_index("mp")
    chip, core = mp // 2, mp % 2
    tok, width = x_ref.shape
    part = proj_ref.shape[0]
    total = experts * slots
    beside = {"mp": mp + 1 - 2 * core}
    across = {"mp": (mp + 2) % 4}
    side = me % 2
    partner = {"dp": me + 1 - 2 * side}
    second = chip == 1
    others = [(me + k) % experts for k in range(1, experts)]
    greet([{"dp": other} for other in others] + [beside, across])

    own_part = pl.ds(pl.multiple_of(chip * part, 16), part)
    other_part = pl.ds(pl.multiple_of((1 - chip) * part, 16), part)
    half = pl.ds(pl.multiple_of(side * (width // 2), 128), width // 2)

    def w_copy(index):
        if index == 3:
            source, target = proj_ref.at[:, half], proj.at[0, own_part, half]
        else:
            source, target = w_ref.at[index, :, half], heads.at[index, own_part, half]
        return remote(source, target, w_sems.at[0, index], w_sems.at[1, index], across)

    def w_pass(index):
        block = proj.at[0, other_part, half] if index == 3 else heads.at[index, other_part, half]
        return remote(block, block, pass_sems.at[0, index], pass_sems.at[1, index], partner)

    proj_pass = remote(proj.at[0], proj.at[1], proj_sems.at[0], proj_sems.at[1], beside)
    w_in_copy = remote(w_in_ref, w_in_far_out, w_in_sems.at[0], w_in_sems.at[1], across)
    for index in range(4):
        w_copy(index).start()
    w_local = pltpu.make_async_copy(w_ref, heads.at[:, own_part], local_sems.at[0])
    proj_local = pltpu.make_async_copy(proj_ref, proj.at[0, own_part], local_sems.at[1])
    w_local.start()
    proj_local.start()

    mine = pl.multiple_of(core * tok, tok)

    def first_norm(step, carry):
        at = pl.ds(pl.multiple_of(step * STRIP, STRIP), STRIP)
        scaled, _ = normalise(x_ref[at].astype(f32))
        normed[pl.ds(pl.multiple_of(HALF + mine + step * STRIP, STRIP), STRIP)] = (
            scaled * gain_one_ref[...][None, :] + shift_one_ref[...][None, :]
        ).astype(bf16)
        return carry

    lax.fori_loop(0, tok // STRIP, first_norm, 0)
    own_normed = normed.at[pl.ds(pl.multiple_of(HALF + mine, STRIP), tok)]
    normed_copy = remote(own_normed, own_normed, normed_sems.at[0], normed_sems.at[1], beside)
    normed_copy.start()

    wide = max(16, experts)
    own_routes = routes_ref[:, pl.ds(pl.multiple_of(mp * tok, tok), tok)]
    picked = own_routes == lax.broadcasted_iota(jnp.int32, (wide, tok), 0)
    earlier = lax.broadcasted_iota(jnp.int32, (tok, tok), 0) < lax.broadcasted_iota(jnp.int32, (tok, tok), 1)
    counts = dot(jnp.where(picked, 1.0, 0.0).astype(bf16), jnp.where(earlier, 1.0, 0.0).astype(bf16))
    rank = jnp.sum(jnp.where(picked, counts, 0.0), axis=0, keepdims=True)
    slot_of = own_routes.astype(f32) * slots + rank
    for strip in range(total // STRIP):
        ids = lax.broadcasted_iota(jnp.int32, (STRIP, tok), 0) + strip * STRIP
        placing[strip * STRIP : (strip + 1) * STRIP] = jnp.where(ids.astype(f32) == slot_of, 1.0, 0.0).astype(bf16)

    positions = mp * tok + lax.broadcasted_iota(jnp.int32, (1, tok), 1)
    factors = pick_sequence(positions, factor_ref)
    high = factors.astype(bf16)
    low = (factors - high.astype(f32)).astype(bf16)
    which = lax.broadcasted_iota(jnp.int32, (16, tok), 0)
    both = jnp.where(which == 0, high, jnp.where(which == 1, low, bf16(0)))
    spread = dot(both, placing[...], NT)

    def place_cot(step, carry):
        at = pl.ds(pl.multiple_of(step * STRIP, STRIP), STRIP)
        cot_send[at] = dot(placing[at], cot_ref[...]).astype(bf16)
        return carry

    lax.fori_loop(0, total // STRIP, place_cot, 0)
    spare = lax.broadcasted_iota(jnp.int32, (16, slots), 0) == cap - (slots - 16)
    for expert in range(experts):
        at = slice((expert + 1) * slots - 16, (expert + 1) * slots)
        here = slice(expert * slots, (expert + 1) * slots)
        for term, column in ((0, 0), (1, width // 2)):
            cot_send[at, column : column + slots] = jnp.where(
                spare, spread[term : term + 1, here], cot_send[at, column : column + slots].astype(f32)
            ).astype(bf16)

    def chunk(index):
        return pl.ds(pl.multiple_of(index * slots, 16), slots)

    def row_copy(target, source):
        return remote(
            cot_send.at[chunk(target)], cot_out.at[chunk(source)],
            row_send.at[target], row_recv.at[source], {"dp": target},
        )

    own_rows = pltpu.make_async_copy(cot_send.at[chunk(me)], cot_out.at[chunk(me)], local_sems.at[2])
    own_rows.start()
    same_side = [(me + k) % experts for k in range(2, experts, 2)]
    for other in same_side:
        row_copy(other, me).start()
    for strip in range(total // STRIP):
        at = slice(strip * STRIP, (strip + 1) * STRIP)
        placing_t[:, at] = placing[at].T

    saves = []

    def save(source, target):
        copy = pltpu.make_async_copy(source, target, save_sems.at[len(saves)])
        copy.start()
        saves.append(copy)

    save(placing_t, placing_t_out)

    def pair_of(step):
        return (1 - chip) * step + chip * (PAIRS - 1 - step)

    def column(offset, pair):
        return pl.ds(pl.multiple_of((offset * PAIRS + pair) * PAIR, PAIR), PAIR)

    def project(step):
        pair = pair_of(step)
        weights = jnp.concatenate([heads[index, column(0, pair)] for index in range(3)])

        def strip_of(strip, carry):
            at = pl.ds(pl.multiple_of(strip * 512, 512), 512)
            value = dot(normed[pl.ds(pl.multiple_of(HALF + strip * 512, 512), 512)], weights, NT).astype(bf16)
            for index in range(3):
                qkv[at, column(index, pair)] = value[:, index * PAIR : (index + 1) * PAIR]
            return carry

        lax.fori_loop(0, 2 * tok // 512, strip_of, 0)

    lane = lax.broadcasted_iota(jnp.int32, (1, PAIR), 1)
    row = lax.broadcasted_iota(jnp.int32, (PAIR, 1), 0)

    def attend_block(pair, first, whole):
        span = (whole + 1) * BLOCK
        start = pl.multiple_of(first + HALF - whole * BLOCK, BLOCK)
        at = pl.ds(first, BLOCK)
        queries = qkv[at, column(0, pair)] * bf16(0.125)
        near = keys[pl.ds(start, span)]
        near_values = values[:, pl.ds(start, span)]
        parts = []
        for head in range(2):
            own = jnp.where((lane // HEAD_DIM) == head, queries, bf16(0))
            scores = mask_diagonal(dot(near, own, NT), whole)
            largest = jnp.max(scores, axis=0, keepdims=True)
            expo = jnp.exp(scores - largest)
            summed = jnp.sum(expo, axis=0, keepdims=True)
            parts.append(dot(near_values, expo.astype(bf16)) / summed)
            logs[pair, head : head + 1, at] = largest + jnp.log(summed)
        mixed[at, column(0, pair)] = jnp.where(row < HEAD_DIM, parts[0], parts[1]).T.astype(bf16)

    quarter = HALF // 2
    ext_rows = pl.ds(pl.multiple_of(core * quarter, quarter), quarter)
    ext_copy = remote(
        normed.at[pl.ds(pl.multiple_of(2 * tok + core * quarter, quarter), quarter)], normed.at[ext_rows],
        ext_sems.at[0, 0], ext_sems.at[1, 0], across,
    )
    ext_pass = remote(normed.at[ext_rows], normed.at[ext_rows], ext_sems.at[0, 1], ext_sems.at[1, 1], beside)
    w_local.wait()
    normed_copy.wait_recv()

    @pl.when(chip == 0)
    def _():
        ext_copy.start()

    w_in_copy.start()
    project(0)
    for index in range(4):
        w_copy(index).wait_recv()
        w_pass(index).start()

    def attention(step, carry):
        pair = pair_of(step)

        @pl.when(step == 1)
        def _():
            for index in range(3):
                w_pass(index).wait_recv()
            for other in [(me + k) % experts for k in range(1, experts, 2)]:
                row_copy(other, me).start()
            project(1)
            project(2)

        keys[HALF:] = qkv[:, column(1, pair)]
        values[:, HALF:] = qkv[:, column(2, pair)].T
        for whole in range(4):
            attend_block(pair, pl.multiple_of((2 * chip + whole) * BLOCK, BLOCK), whole)

        @pl.when(chip == 0)
        def _():
            attend_block(pair, 4 * BLOCK, 0)
            attend_block(pair, 5 * BLOCK, 1)

        return carry

    lax.fori_loop(0, PAIRS, attention, 0)
    save(qkv, qkv_out)
    save(heads, heads_out)
    proj_local.wait()
    w_pass(3).wait_recv()
    proj_pass.start()
    save(proj.at[0], proj_out)

    @pl.when(second)
    def _():
        ext_copy.wait_recv()
        ext_pass.start()
        ext_pass.wait_recv()
        for index in range(2):
            ext[:, index * PAIRS * PAIR : (index + 1) * PAIRS * PAIR] = dot(
                normed[0:HALF], heads[1 + index], NT
            ).astype(bf16)

        def late(pair, carry):
            keys[0:HALF] = ext[:, column(0, pair)]
            keys[HALF : 2 * HALF] = qkv[0:HALF, column(1, pair)]
            values[:, 0:HALF] = ext[:, column(1, pair)].T
            values[:, HALF : 2 * HALF] = qkv[0:HALF, column(2, pair)].T
            attend_block(pair, 0, 2)
            attend_block(pair, BLOCK, 3)
            return carry

        lax.fori_loop(0, PAIRS, late, 0)

    @pl.when(chip == 0)
    def _():
        ext_copy.wait_send()
        ext[...] = jnp.zeros_like(ext)
        normed[0:HALF] = jnp.zeros((HALF, width), bf16)

    @pl.when(second)
    def _():
        ext_pass.wait_send()

    save(normed, normed_out)
    save(ext, ext_out)
    save(mixed, mixed_out)
    save(logs, log_out)
    mixed_copy = remote(
        mixed.at[pl.ds(pl.multiple_of((1 - core) * tok, tok), tok)], mixed_far,
        mixed_sems.at[0], mixed_sems.at[1], beside,
    )
    mixed_copy.start()
    proj_pass.wait_recv()
    mixed_copy.wait_recv()

    def second_norm(step, carry):
        at = pl.ds(pl.multiple_of(step * STRIP, STRIP), STRIP)
        value = x_ref[at].astype(f32) + (
            dot(mixed[pl.ds(pl.multiple_of(mine + step * STRIP, STRIP), STRIP)], proj[0])
            + dot(mixed_far[at], proj[1])
        )
        hidden[at] = value
        scaled, _ = normalise(value)
        normed_two[at] = (scaled * gain_two_ref[...][None, :] + shift_two_ref[...][None, :]).astype(bf16)
        return carry

    lax.fori_loop(0, tok // STRIP, second_norm, 0)
    save(hidden, hidden_out)

    def place_rows(step, carry):
        at = pl.ds(pl.multiple_of(step * STRIP, STRIP), STRIP)
        rows[at] = dot(placing[at], normed_two[...]).astype(bf16)
        return carry

    lax.fori_loop(0, total // STRIP, place_rows, 0)
    save(rows, rows_out)
    own_rows.wait()
    for other in others:
        row_copy(me, other).wait_recv()
        row_copy(other, me).wait_send()
    for index in range(4):
        w_copy(index).wait_send()
        w_pass(index).wait_send()
    for copy in (proj_pass, normed_copy, mixed_copy):
        copy.wait_send()
    for copy in saves:
        copy.wait()
    w_in_copy.wait()


def run_forward(
    x, cotangent, routes, factor, gain_one, shift_one, gain_two, shift_two, w_heads, w_proj, w_in, experts, cap, slots
):
    tok, width = x.shape
    rows = 2 * tok
    total = experts * slots
    part = w_proj.shape[0]
    anyspace, vmem = pl.BlockSpec(memory_space=pl.ANY), pl.BlockSpec(memory_space=pltpu.VMEM)
    smem = pl.BlockSpec(memory_space=pltpu.SMEM)
    dma = pltpu.SemaphoreType.DMA
    kept = [
        ((HALF + rows, width), bf16),
        ((rows, 3 * PAIRS * PAIR), bf16),
        ((HALF, 2 * PAIRS * PAIR), bf16),
        ((rows, PAIRS * PAIR), bf16),
        ((PAIRS, 8, rows), f32),
        ((3, 2 * part, width), bf16),
    ]
    late = [((tok, width), f32), ((total, width), bf16)]
    return pl.pallas_call(
        functools.partial(forward_kernel, experts, slots, cap),
        in_specs=[vmem, vmem, vmem, smem] + [vmem] * 4 + [anyspace] * 3,
        out_specs=[anyspace] * 12,
        out_shape=[
            jax.ShapeDtypeStruct(*item)
            for item in kept
            + [((2 * part, width), bf16)]
            + late
            + [((total, width), bf16), ((tok, total), bf16), (w_in.shape, bf16)]
        ],
        scratch_shapes=[pltpu.VMEM(*item) for item in kept + [((2, 2 * part, width), bf16)] + late]
        + [
            pltpu.VMEM((total, tok), bf16),
            pltpu.VMEM((tok, total), bf16),
            pltpu.VMEM((total, width), bf16),
            pltpu.VMEM((tok, PAIRS * PAIR), bf16),
            pltpu.VMEM((tok, width), bf16),
            pltpu.VMEM((HALF + rows, PAIR), bf16),
            pltpu.VMEM((PAIR, HALF + rows), bf16),
            dma((2, 4)), dma((2, 4)), dma((2,)), dma((2,)), dma((2,)), dma((2, 2)), dma((2,)),
            dma((experts,)), dma((experts,)), dma((3,)), dma((10,)),
        ],
        compiler_params=pltpu.CompilerParams(
            collective_id=4, has_side_effects=True, vmem_limit_bytes=56 * 2**20
        ),
        cost_estimate=pl.CostEstimate(flops=30 * 10**9, bytes_accessed=30 * 10**6, transcendentals=8 * 10**6),
        name="forward",
    )(x, cotangent, routes, factor, gain_one, shift_one, gain_two, shift_two, w_heads, w_proj, w_in)


def backward_kernel(
    experts, slots,
    factor_ref, hidden_ref, gain_one_ref, gain_two_ref, placing_ref, d_returned_ref, router_ref,
    cot_any, result_ref, there_in_ref, there_out_ref, mixed_any, proj_any, qkv_any, ext_any, log_any, normed_any, heads_any, x_any,
    output_ref, input_grad_ref, total_ref, small_ref, far_in_ref, far_out_ref,
    mixed_ref, proj_ref, qkv_ref, ext_ref, log_ref, normed_ref, heads_ref, x_ref, saved,
    returned, d_hidden, d_branch, d_mixed, keys, values, d_keys, d_values, d_qkv, d_ext,
    grads_own, grads_send, grads_recv, d_norm, norm_recv, ext_recv,
    held, half_recv, piece_recv, small, small_groups,
    row_send, row_recv, branch_sems, norm_sems, ext_sems, far_sems, grad_sems,
    half_sems, piece_sems, gather_sems, back_sems, small_sems, load_sems, local_sems,
):
    me, mp = lax.axis_index("dp"), lax.axis_index("mp")
    chip, core = mp // 2, mp % 2
    tok, width = hidden_ref.shape
    rows = 2 * tok
    part = grads_own.shape[1]
    all_heads = PAIRS * PAIR
    beside = {"mp": mp + 1 - 2 * core}
    across = {"mp": (mp + 2) % 4}
    second = chip == 1
    others = [(me + k) % experts for k in range(1, experts)]
    diagonal = {"mp": 3 - mp}
    greet([{"dp": other} for other in others] + [beside, across, diagonal])

    def chunk(index):
        return pl.ds(pl.multiple_of(index * slots, 16), slots)

    def row_copy(target, source):
        return remote(
            result_ref.at[chunk(target)], returned.at[chunk(source)],
            row_send.at[target], row_recv.at[source], {"dp": target},
        )

    cot_copy = pltpu.make_async_copy(cot_any, grads_send, local_sems.at[1])
    cot_copy.start()
    loads = [
        pltpu.make_async_copy(source, target, load_sems.at[index])
        for index, (source, target) in enumerate(
            (
                (mixed_any, mixed_ref), (proj_any, proj_ref), (qkv_any, qkv_ref), (ext_any, ext_ref),
                (log_any, log_ref), (normed_any, normed_ref), (heads_any, heads_ref), (x_any, x_ref),
            )
        )
    ]
    for load in loads:
        load.start()
    far_half = there_in_ref.shape[0] // 2
    far_copies = [remote(there_out_ref, far_out_ref, far_sems.at[0, 0], far_sems.at[1, 0], across)] + [
        remote(
            there_in_ref.at[pl.ds(index * far_half, far_half)], far_in_ref.at[pl.ds(index * far_half, far_half)],
            far_sems.at[0, 1 + index], far_sems.at[1, 1 + index], across,
        )
        for index in range(2)
    ]
    far_copies[0].start()
    own_rows = pltpu.make_async_copy(result_ref.at[chunk(me)], returned.at[chunk(me)], local_sems.at[0])
    own_rows.start()
    for other in others:
        row_copy(other, me).start()

    cot_copy.wait()
    small[...] = jnp.zeros_like(small)
    mine = pl.multiple_of(core * tok, tok)

    def second_norm(step, carry):
        at = pl.ds(pl.multiple_of(step * STRIP, STRIP), STRIP)
        scaled, inverse = normalise(hidden_ref[at])
        d_normed = dot(placing_ref[at], d_returned_ref[...])
        small[2:3] += jnp.sum(d_normed * scaled, axis=0, keepdims=True)
        small[3:4] += jnp.sum(d_normed, axis=0, keepdims=True)
        positions = mp * tok + step * STRIP + lax.broadcasted_iota(jnp.int32, (STRIP, 1), 0)
        total = grads_send[at].astype(f32) * pick_sequence(positions, factor_ref) + norm_pull(
            d_normed, scaled, inverse, gain_two_ref[...][None, :]
        )
        d_hidden[at] = total
        d_branch[pl.ds(pl.multiple_of(mine + step * STRIP, STRIP), STRIP)] = total.astype(bf16)
        return carry

    lax.fori_loop(0, tok // STRIP, second_norm, 0)
    own_branch = d_branch.at[pl.ds(mine, tok)]
    branch_copy = remote(own_branch, own_branch, branch_sems.at[0], branch_sems.at[1], beside)
    branch_copy.start()
    branch_copy.wait()

    for load in loads[:2]:
        load.wait()

    def push_branch(step, carry):
        at = pl.ds(pl.multiple_of(step * STRIP, STRIP), STRIP)
        d_mixed[at] = dot(d_branch[at], proj_ref[...], NT).astype(bf16)
        return carry

    lax.fori_loop(0, rows // STRIP, push_branch, 0)

    side, line = me % 2, me // 2
    lines = experts // 2
    partner = {"dp": me + 1 - 2 * side}
    mates = [(line + k) % lines for k in range(1, lines)]
    piece_rows = held.shape[1] // lines
    own_columns = pl.ds(pl.multiple_of(side * (width // 2), 128), width // 2)
    other_columns = pl.ds(pl.multiple_of((1 - side) * (width // 2), 128), width // 2)

    def piece(index):
        return pl.ds(pl.multiple_of(index * piece_rows, 16), piece_rows)

    def sent(index):
        return slice(index * part, (index + 1) * part)

    def grad_copy(index):
        return remote(
            grads_send.at[sent(index)], grads_recv.at[index], grad_sems.at[0, index], grad_sems.at[1, index], across
        )

    def half_copy(index):
        return remote(
            held.at[index, :, other_columns], half_recv.at[index],
            half_sems.at[0, index], half_sems.at[1, index], partner,
        )

    def piece_copy(index, target, source):
        return remote(
            held.at[index, piece(target), own_columns], piece_recv.at[index, source],
            piece_sems.at[0, index, target], piece_sems.at[1, index, source], {"dp": 2 * target + side},
        )

    def gather_copy(index, target, source):
        block = total_ref.at[index, piece(source), own_columns]
        return remote(
            block, block,
            gather_sems.at[0, index, target], gather_sems.at[1, index, source], {"dp": 2 * target + side},
        )

    def back_copy(index):
        block = total_ref.at[index, :, own_columns]
        return remote(block, block, back_sems.at[0, index], back_sems.at[1, index], partner)

    def send_grad(index, grad):
        for own in range(2):

            @pl.when(chip == own)
            def _():
                grads_own[index] = grad[own * part : (own + 1) * part]
                grads_send[sent(index)] = grad[(1 - own) * part : (2 - own) * part].astype(bf16)

        grad_copy(index).start()

    chunks = held.shape[0]
    parts = 4 // chunks

    def stage_one(index):
        if index >= chunks:
            return
        for at in range(parts):
            number = index * parts + at
            grad_copy(number).wait_recv()
            held[index, at * part : (at + 1) * part] = (
                grads_own[number] + grads_recv[number].astype(f32)
            ).astype(bf16)
        if held.shape[1] > parts * part:
            held[index, parts * part :] = jnp.zeros((held.shape[1] - parts * part, width), bf16)
        half_copy(index).start()

    def stage_two(index):
        if index >= chunks:
            return
        half_copy(index).wait_recv()
        held[index, :, own_columns] = (
            held[index, :, own_columns].astype(f32) + half_recv[index].astype(f32)
        ).astype(bf16)
        for mate in mates:
            piece_copy(index, mate, line).start()

    def stage_three(index):
        if index >= chunks:
            return
        value = held[index, piece(line), own_columns].astype(f32)
        for mate in mates:
            piece_copy(index, line, mate).wait_recv()
            value += piece_recv[index, mate].astype(f32)
        total_ref[index, piece(line), own_columns] = value.astype(bf16)
        for mate in mates:
            gather_copy(index, mate, line).start()

    def stage_four(index):
        if index >= chunks:
            return
        for mate in mates:
            gather_copy(index, line, mate).wait_recv()
        back_copy(index).start()

    send_grad(0, dot(mixed_ref[...], d_branch[...], TN))

    lane = lax.broadcasted_iota(jnp.int32, (1, PAIR), 1)

    def column(offset, pair):
        return pl.ds(pl.multiple_of((offset * PAIRS + pair) * PAIR, PAIR), PAIR)

    def attend_blocks(pair, blocks):
        for first, whole in blocks:
            span = (whole + 1) * BLOCK
            start = pl.multiple_of(first + HALF - whole * BLOCK, BLOCK)
            at = pl.ds(first, BLOCK)
            queries = qkv_ref[at, column(0, pair)] * bf16(0.125)
            d_out = d_mixed[at, column(0, pair)]
            near = keys[pl.ds(start, span)]
            near_values = values[pl.ds(start, span)]
            product = (d_out.astype(f32) * mixed_ref[at, column(0, pair)].astype(f32)).T
            dq = dk = dv = 0.0
            for head in range(2):
                here = (lane // HEAD_DIM) == head
                own = jnp.where(here, queries, bf16(0))
                d_own = jnp.where(here, d_out, bf16(0))
                delta = jnp.sum(product[HEAD_DIM * head : HEAD_DIM * (head + 1)], axis=0, keepdims=True)
                scores = mask_diagonal(dot(near, own, NT), whole)
                probs = jnp.exp(scores - log_ref[pair, head : head + 1, at])
                d_probs = dot(near_values, d_own, NT)
                d_scores = (probs * (d_probs - delta)).astype(bf16)
                dv = dv + dot(probs.astype(bf16), d_own)
                dk = dk + dot(d_scores, own)
                dq = dq + dot(d_scores, jnp.where(here, near, bf16(0)), TN)
            d_qkv[at, column(0, pair)] = (dq * 0.125).astype(bf16)
            d_keys[pl.ds(start, span)] += dk
            d_values[pl.ds(start, span)] += dv

    ext_part, norm_send = d_branch.at[tok : tok + HALF], d_branch.at[0:tok]
    ext_beside = remote(ext_part, ext_recv, ext_sems.at[0, 0], ext_sems.at[1, 0], beside)
    ext_across = remote(ext_part, ext_recv, ext_sems.at[0, 1], ext_sems.at[1, 1], across)
    for load in loads[2:5]:
        load.wait()

    @pl.when(second)
    def _():
        def early(pair, carry):
            keys[0:HALF] = ext_ref[:, column(0, pair)]
            keys[HALF : 2 * HALF] = qkv_ref[0:HALF, column(1, pair)]
            values[0:HALF] = ext_ref[:, column(1, pair)]
            values[HALF : 2 * HALF] = qkv_ref[0:HALF, column(2, pair)]
            d_keys[0 : 2 * HALF] = jnp.zeros((2 * HALF, PAIR), f32)
            d_values[0 : 2 * HALF] = jnp.zeros((2 * HALF, PAIR), f32)
            attend_blocks(pair, [(0, 2), (BLOCK, 3)])
            d_ext[:, column(0, pair)] = d_keys[0:HALF].astype(bf16)
            d_ext[:, column(1, pair)] = d_values[0:HALF].astype(bf16)
            saved[pair, :, 0:PAIR] = d_keys[HALF : 2 * HALF]
            saved[pair, :, PAIR:] = d_values[HALF : 2 * HALF]
            return carry

        lax.fori_loop(0, PAIRS, early, 0)

    for load in loads[5:7]:
        load.wait()

    @pl.when(second)
    def _():
        ext_part[...] = dot(d_ext[...], heads_ref[1:3].reshape(2 * all_heads, width)).astype(bf16)

    @pl.when(chip == 0)
    def _():
        d_ext[...] = jnp.zeros_like(d_ext)
        saved[...] = jnp.zeros_like(saved)

    @pl.when(mp == 2)
    def _():
        ext_beside.start()

    def attention(pair, carry):
        keys[HALF:] = qkv_ref[:, column(1, pair)]
        values[HALF:] = qkv_ref[:, column(2, pair)]
        d_keys[HALF : 2 * HALF] = saved[pair, :, 0:PAIR]
        d_keys[2 * HALF :] = jnp.zeros((rows - HALF, PAIR), f32)
        d_values[HALF : 2 * HALF] = saved[pair, :, PAIR:]
        d_values[2 * HALF :] = jnp.zeros((rows - HALF, PAIR), f32)
        attend_blocks(pair, [(pl.multiple_of((2 * chip + whole) * BLOCK, BLOCK), whole) for whole in range(4)])

        @pl.when(chip == 0)
        def _():
            attend_blocks(pair, [(4 * BLOCK, 0), (5 * BLOCK, 1)])

        @pl.when((mp == 3) & (pair == 0))
        def _():
            ext_beside.wait_recv()
            ext_part[...] = (ext_part[...].astype(f32) + ext_recv[...].astype(f32)).astype(bf16)
            ext_across.start()

        d_qkv[:, column(1, pair)] = d_keys[HALF:].astype(bf16)
        d_qkv[:, column(2, pair)] = d_values[HALF:].astype(bf16)
        return carry

    lax.fori_loop(0, PAIRS, attention, 0)

    send_grad(1, dot(d_qkv[:, 0:all_heads], normed_ref[HALF:], TN))

    for index in (1, 2):
        at = slice(index * all_heads, (index + 1) * all_heads)
        send_grad(
            1 + index,
            dot(d_qkv[:, at], normed_ref[HALF:], TN)
            + dot(d_ext[:, (index - 1) * all_heads : index * all_heads], normed_ref[0:HALF], TN),
        )
    far_copies[1].start()
    stage_one(0)

    weights = heads_ref[...].reshape(3 * all_heads, width)

    def push_norm(step, carry):
        at = pl.ds(pl.multiple_of((1 - core) * tok + step * STRIP, STRIP), STRIP)
        norm_send[pl.ds(pl.multiple_of(step * STRIP, STRIP), STRIP)] = dot(d_qkv[at], weights).astype(bf16)
        return carry

    def pull_norm(step, carry):
        at = pl.ds(pl.multiple_of(mine + step * STRIP, STRIP), STRIP)
        d_norm[pl.ds(pl.multiple_of(step * STRIP, STRIP), STRIP)] = dot(d_qkv[at], weights)
        return carry

    lax.fori_loop(0, tok // STRIP, push_norm, 0)
    norm_copy = remote(norm_send, norm_recv, norm_sems.at[0], norm_sems.at[1], beside)
    norm_copy.start()
    lax.fori_loop(0, tok // STRIP, pull_norm, 0)
    stage_two(0)
    stage_one(1)
    own_rows.wait()
    for other in others:
        row_copy(me, other).wait_recv()

    def finish(step, carry):
        at = pl.ds(pl.multiple_of(step * STRIP, STRIP), STRIP)
        output_ref[at] = (hidden_ref[at] + dot(placing_ref[at], returned[...])).astype(bf16)
        return carry

    lax.fori_loop(0, tok // STRIP, finish, 0)
    stage_three(0)
    stage_two(1)
    stage_one(2)
    norm_copy.wait_recv()
    loads[7].wait()

    @pl.when(mp == 1)
    def _():
        ext_across.wait_recv()
        d_norm[tok - HALF :] += ext_recv[...].astype(f32)

    def first_norm(step, carry):
        at = pl.ds(pl.multiple_of(step * STRIP, STRIP), STRIP)
        scaled, inverse = normalise(x_ref[at].astype(f32))
        d_normed = d_norm[at] + norm_recv[at].astype(f32)
        small[0:1] += jnp.sum(d_normed * scaled, axis=0, keepdims=True)
        small[1:2] += jnp.sum(d_normed, axis=0, keepdims=True)
        input_grad_ref[at] = (
            d_hidden[at] + norm_pull(d_normed, scaled, inverse, gain_one_ref[...][None, :])
        ).astype(bf16)
        return carry

    lax.fori_loop(0, tok // STRIP, first_norm, 0)

    small_rows = lax.broadcasted_iota(jnp.int32, small.shape, 0)
    small[...] = jnp.where(small_rows == 8 + me, router_ref[...], small[...])
    rounds = [("mp", mp, mp - mp % 4, 1, 4)]
    stride = 1
    while stride < experts:
        rounds.append(("dp", me, me - me // stride % 8 * stride, stride, 8))
        stride *= 8

    def small_copies(number, receiving):
        axis, place, base, step, size = rounds[number]
        own = (place - base) // step
        copies = []
        for k in range(1, size):
            other = (own + k) % size
            source, target = (other, own) if receiving else (own, other)
            copies.append(
                remote(
                    small_groups.at[number, own], small_groups.at[number, source],
                    small_sems.at[0, number, target], small_sems.at[1, number, source],
                    {axis: base + other * step},
                )
            )
        return copies

    def small_start(number):
        axis, place, base, step, size = rounds[number]
        small_groups[number, (place - base) // step] = small[...]
        for copy in small_copies(number, False):
            copy.start()

    def small_finish(number):
        for copy in small_copies(number, True):
            copy.wait_recv()
        value = small_groups[number, 0]
        for index in range(1, rounds[number][4]):
            value += small_groups[number, index]
        small[...] = value

    small_start(0)
    far_copies[2].start()
    stage_four(0)
    stage_three(1)
    stage_two(2)
    stage_one(3)
    stage_four(1)
    stage_three(2)
    stage_two(3)
    stage_four(2)
    stage_three(3)
    for number in range(len(rounds)):
        small_finish(number)
        if number + 1 < len(rounds):
            small_start(number + 1)
            if number == 0:
                stage_four(3)
    small_ref[...] = small[...]
    for index in range(chunks):
        other = total_ref.at[index, :, other_columns]
        remote(other, other, back_sems.at[0, index], back_sems.at[1, index], partner).wait_recv()

    for other in others:
        row_copy(other, me).wait_send()
    for mate in mates:
        for index in range(chunks):
            piece_copy(index, mate, line).wait_send()
            gather_copy(index, mate, line).wait_send()
    for index in range(4):
        grad_copy(index).wait_send()
    for index in range(chunks):
        half_copy(index).wait_send()
        back_copy(index).wait_send()
    for number in range(len(rounds)):
        for copy in small_copies(number, False):
            copy.wait_send()
    norm_copy.wait_send()

    @pl.when(mp == 2)
    def _():
        ext_beside.wait_send()

    @pl.when(mp == 3)
    def _():
        ext_across.wait_send()

    for copy in far_copies:
        copy.wait()


def run_backward(
    x, cotangent, factor, hidden, gain_one, gain_two, placing, d_returned, result, normed, qkv, ext,
    mixed, log_total, heads, proj, router_grad, there_in, there_out, experts,
):
    tok, width = x.shape
    rows = 2 * tok
    total = d_returned.shape[0]
    part = proj.shape[0] // 2
    lines = experts // 2
    steps = 2 if experts <= 8 else 3
    chunks = 4 if part % (16 * lines) == 0 else 2
    padded = (4 // chunks * part + 16 * lines - 1) // (16 * lines) * (16 * lines)
    small = (8 + max(8, experts), width)
    anyspace, vmem = pl.BlockSpec(memory_space=pl.ANY), pl.BlockSpec(memory_space=pltpu.VMEM)
    smem = pl.BlockSpec(memory_space=pltpu.SMEM)
    dma = pltpu.SemaphoreType.DMA
    return pl.pallas_call(
        functools.partial(backward_kernel, experts, total // experts),
        in_specs=[smem] + [vmem] * 6 + [anyspace] * 12,
        out_specs=[vmem] * 4 + [anyspace] * 2,
        out_shape=[
            jax.ShapeDtypeStruct((tok, width), bf16),
            jax.ShapeDtypeStruct((tok, width), bf16),
            jax.ShapeDtypeStruct((chunks, padded, width), bf16),
            jax.ShapeDtypeStruct(small, f32),
            jax.ShapeDtypeStruct(there_in.shape, bf16),
            jax.ShapeDtypeStruct(there_out.shape, bf16),
        ],
        scratch_shapes=[
            pltpu.VMEM(item.shape, item.dtype) for item in (mixed, proj, qkv, ext, log_total, normed, heads, x)
        ]
        + [
            pltpu.VMEM((PAIRS, HALF, 2 * PAIR), f32),
            pltpu.VMEM((total, width), bf16),
            pltpu.VMEM((tok, width), f32),
            pltpu.VMEM((rows, width), bf16),
            pltpu.VMEM((rows, PAIRS * PAIR), bf16),
            pltpu.VMEM((HALF + rows, PAIR), bf16),
            pltpu.VMEM((HALF + rows, PAIR), bf16),
            pltpu.VMEM((HALF + rows, PAIR), f32),
            pltpu.VMEM((HALF + rows, PAIR), f32),
            pltpu.VMEM((rows, 3 * PAIRS * PAIR), bf16),
            pltpu.VMEM((HALF, 2 * PAIRS * PAIR), bf16),
            pltpu.VMEM((4, part, width), f32),
            pltpu.VMEM((4 * part, width), bf16),
            pltpu.VMEM((4, part, width), bf16),
            pltpu.VMEM((tok, width), f32),
            pltpu.VMEM((tok, width), bf16),
            pltpu.VMEM((HALF, width), bf16),
            pltpu.VMEM((chunks, padded, width), bf16),
            pltpu.VMEM((chunks, padded, width // 2), bf16),
            pltpu.VMEM((chunks, lines, padded // lines, width // 2), bf16),
            pltpu.VMEM(small, f32),
            pltpu.VMEM((steps, 8) + small, f32),
            dma((experts,)), dma((experts,)), dma((2,)), dma((2,)), dma((2, 2)), dma((2, 3)), dma((2, 4)),
            dma((2, chunks)), dma((2, chunks, lines)), dma((2, chunks, lines)), dma((2, chunks)),
            dma((2, steps, 8)), dma((8,)), dma((2,)),
        ],
        compiler_params=pltpu.CompilerParams(
            collective_id=2, has_side_effects=True, vmem_limit_bytes=62 * 2**20
        ),
        cost_estimate=pl.CostEstimate(flops=30 * 10**9, bytes_accessed=30 * 10**6, transcendentals=8 * 10**6),
        name="backward",
    )(
        factor, hidden, gain_one, gain_two, placing, d_returned, router_grad,
        cotangent, result, there_in, there_out, mixed, proj, qkv, ext, log_total, normed, heads, x,
    )


def gelu_parts(pre):
    scale = 0.7978845608028654
    square = pre * pre
    inner = jnp.tanh(pre * (scale + (scale * 0.044715) * square))
    half = 0.5 * (1.0 + inner)
    slope = half + (0.5 * pre) * (1.0 - inner * inner) * (scale + (3.0 * scale * 0.044715) * square)
    return pre * half, slope

STAGES = 4

def expert_kernel(
    experts, slots, cap,
    rows_ref, cot_ref, router_ref, w_in_ref, w_out_ref, w_in_far_ref,
    back_ref, result_out, router_grad_ref, here_in_ref, here_out, there_in_ref, there_out_ref,
    result, here_out_held, router, factor, x, wi, wo, d_out, act, d_pre, total, d_x, give, g_send, g_recv,
    row_send, row_recv, back_send, back_recv, w_send, w_recv, g_send_sem, g_recv_sem, save_sems, local_sem,
):
    me = lax.axis_index("dp")
    mp = lax.axis_index("mp")
    beside = {"mp": mp + 1 - 2 * (mp % 2)}
    across = {"mp": (mp + 2) % 4}
    members = experts // STAGES
    span = members * slots
    own_group, own_member = me // members, me % members

    def group_of(stage):
        return 2 * ((own_group // 2 + stage // 2) % 2) + (own_group % 2 + stage % 2) % 2

    def chunk(index):
        return pl.ds(pl.multiple_of(index * slots, 16), slots)

    def group_rows(group):
        return pl.ds(pl.multiple_of(group * span, 16), span)

    barrier = pltpu.get_barrier_semaphore()

    def greet(step, carry):
        pl.semaphore_signal(barrier, inc=1, device_id={"dp": (me + step) % experts}, device_id_type=MESH)
        return carry

    lax.fori_loop(1, experts, greet, 0)
    pl.semaphore_signal(barrier, inc=1, device_id=beside, device_id_type=MESH)
    pl.semaphore_signal(barrier, inc=1, device_id=across, device_id_type=MESH)
    pl.semaphore_wait(barrier, experts + 1)

    def remote(src, dst, send, recv, device):
        return pltpu.make_async_remote_copy(
            src_ref=src, dst_ref=dst, send_sem=send, recv_sem=recv, device_id=device, device_id_type=MESH
        )

    def row_copy(target, source):
        return remote(rows_ref.at[chunk(target)], x.at[chunk(source)], row_send.at[target], row_recv.at[source], {"dp": target})

    def back_copy(target, source):
        return remote(give.at[chunk(target)], back_ref.at[chunk(source)], back_send.at[target], back_recv.at[source], {"dp": target})

    def partners(stage):
        group = group_of(stage)
        if stage == 0:
            return [group * members + (own_member + k) % members for k in range(1, members)]
        return [group * members + (own_member + k) % members for k in range(members)]

    for stage in (0, 1, 3, 2):
        for other in partners(stage):
            row_copy(other, me).start()
    own_rows = pltpu.make_async_copy(rows_ref.at[chunk(me)], x.at[chunk(me)], local_sem.at[0])
    own_in = pltpu.make_async_copy(w_in_ref, wi.at[0], local_sem.at[1])
    own_out = pltpu.make_async_copy(w_out_ref, wo.at[0], local_sem.at[2])
    far_in = pltpu.make_async_copy(w_in_far_ref, wi.at[2], local_sem.at[3])
    near_in = remote(w_in_ref, wi.at[1], w_send.at[0], w_recv.at[0], beside)
    near_out = remote(w_out_ref, wo.at[1], w_send.at[1], w_recv.at[1], beside)
    far_near_in = remote(w_in_far_ref, wi.at[3], w_send.at[2], w_recv.at[2], beside)
    far_out = remote(w_out_ref, wo.at[2], w_send.at[3], w_recv.at[3], across)
    far_near_out = remote(wo.at[2], wo.at[3], w_send.at[4], w_recv.at[4], beside)
    for copy in (own_rows, own_in, own_out, near_in, near_out, far_in, far_out, far_near_in):
        copy.start()
    router_grad_ref[...] = jnp.zeros_like(router_grad_ref)
    router[...] = router_ref[...].astype(f32)

    diagonal = lax.broadcasted_iota(jnp.int32, (slots, slots), 0) == lax.broadcasted_iota(
        jnp.int32, (slots, slots), 1
    )

    def prepare(stage, rows):
        for member in range(members):
            index = group_of(stage) * members + member
            spare = cot_ref[pl.ds(pl.multiple_of((index + 1) * slots - 16, 16), 16)].astype(f32)
            spare = spare[cap - slots + 16 : cap - slots + 17]
            value = spare[:, 0:slots] + spare[:, x.shape[1] // 2 : x.shape[1] // 2 + slots]
            factor[chunk(index)] = jnp.sum(jnp.where(diagonal, value, 0.0), axis=1, keepdims=True)
        features = x[rows].astype(f32)
        gate = jax.nn.sigmoid(jnp.sum(features * router[pl.ds(me, 1)], axis=1, keepdims=True))
        d_out[rows] = (gate * (cot_ref[rows].astype(f32) * factor[rows])).astype(bf16)
        total[rows] = jnp.zeros((span, x.shape[1]), f32)
        d_x[rows] = jnp.zeros((span, x.shape[1]), f32)

    def finish(stage, rows):
        features = x[rows].astype(f32)
        gate = jax.nn.sigmoid(jnp.sum(features * router[pl.ds(me, 1)], axis=1, keepdims=True))
        value = total[rows]
        d_gate = jnp.sum(cot_ref[rows].astype(f32) * factor[rows] * value, axis=1, keepdims=True)
        d_logit = (d_gate * gate * (1.0 - gate)).astype(bf16).astype(f32)
        give[rows] = (d_x[rows] + d_logit * router[pl.ds(me, 1)]).astype(bf16)
        result[rows] = (gate * value).astype(bf16)
        router_grad_ref[...] += jnp.sum(features * d_logit, axis=0, keepdims=True)

    def stage_of(step):
        near = jnp.where(step < 2, 0, jnp.where(step < 4, 1, 3))
        return jnp.where(step < 8, near, jnp.where(step < 12, 2, jnp.where(step < 14, 1, 0)))

    def step_body(step, carry):
        stage = stage_of(step)
        part = jnp.where(step < 6, step % 2, jnp.where((step < 8) | (step >= 12), 2 + step % 2, step - 8))
        rows = group_rows(group_of(stage))

        for static, at in enumerate((0, 2, 8, 4)):
            @pl.when(step == at)
            def _():
                if static == 0:
                    own_rows.wait()
                for other in partners(static):
                    row_copy(me, other).wait_recv()
        @pl.when((step == 0) | (step == 2) | (step == 4) | (step == 8))
        def _():
            prepare(stage, rows)

        @pl.when(step == 0)
        def _():
            own_in.wait()
            own_out.wait()

        @pl.when(step == 1)
        def _():
            near_in.wait_recv()
            near_out.wait_recv()

        @pl.when(step == 6)
        def _():
            far_in.wait()
            far_out.wait_recv()
            far_near_out.start()

        @pl.when(step == 7)
        def _():
            far_near_in.wait_recv()
            far_near_out.wait_recv()

        pre = dot(x[rows], wi[part])
        value, slope = gelu_parts(pre)
        value = value.astype(bf16)
        act[part, rows] = value
        total[rows] += dot(value, wo[part])
        d_value = (dot(d_out[rows], wo[part], NT) * slope).astype(bf16)
        d_pre[part, rows] = d_value
        d_x[rows] += dot(d_value, wi[part], NT)

        @pl.when((step == 7) | (step == 11) | (step == 13) | (step == 15))
        def _():
            finish(stage, rows)

        for static, at in enumerate((15, 13, 11, 7)):
            @pl.when(step == at)
            def _():
                for other in partners(static):
                    back_copy(other, me).start()
        return carry

    lax.fori_loop(0, 16, step_body, 0)
    own_back = pltpu.make_async_copy(give.at[chunk(me)], back_ref.at[chunk(me)], local_sem.at[4])
    own_back.start()
    result_save = pltpu.make_async_copy(result, result_out, save_sems.at[0])
    result_save.start()

    kept = pl.ds(0, x.shape[1])
    outgoing = [g_send, act.at[3, kept], d_pre.at[3, kept], act.at[1, kept]]

    def grad_copy(index):
        return remote(outgoing[index], g_recv.at[index], g_send_sem.at[index], g_recv_sem.at[index], beside)

    outgoing[0][...] = dot(act[3], d_out[...], TN).astype(bf16)
    grad_copy(0).start()
    outgoing[1][...] = dot(x[...], d_pre[3], TN).astype(bf16)
    grad_copy(1).start()
    outgoing[2][...] = dot(act[1], d_out[...], TN).astype(bf16)
    grad_copy(2).start()
    outgoing[3][...] = dot(x[...], d_pre[1], TN).astype(bf16)
    grad_copy(3).start()
    total[kept] = dot(act[2], d_out[...], TN)
    d_x[kept] = dot(x[...], d_pre[2], TN)
    here_out_held[...] = dot(act[0], d_out[...], TN)
    here_in_ref[...] = dot(x[...], d_pre[0], TN)
    grad_copy(0).wait_recv()
    there_out_ref[...] = (total[kept] + g_recv[0].astype(f32)).astype(bf16)
    grad_copy(1).wait_recv()
    there_in_ref[...] = (d_x[kept] + g_recv[1].astype(f32)).astype(bf16)
    grad_copy(2).wait_recv()
    here_out_held[...] += g_recv[2].astype(f32)
    here_save = pltpu.make_async_copy(here_out_held, here_out, save_sems.at[1])
    here_save.start()
    grad_copy(3).wait_recv()
    here_in_ref[...] += g_recv[3].astype(f32)

    result_save.wait()
    here_save.wait()
    own_back.wait()
    for stage in range(STAGES):
        for other in partners(stage):
            back_copy(me, other).wait_recv()
            back_copy(other, me).wait_send()
            row_copy(other, me).wait_send()
    for copy in (near_in, near_out, far_near_in, far_out, far_near_out):
        copy.wait_send()
    for index in range(4):
        grad_copy(index).wait_send()


def run_expert(rows, cot_rows, router, w_in, w_out, w_in_far, experts, cap):
    total, width = rows.shape
    slots = total // experts
    hidden = w_in.shape[1]
    anyspace, vmem = pl.BlockSpec(memory_space=pl.ANY), pl.BlockSpec(memory_space=pltpu.VMEM)
    dma = pltpu.SemaphoreType.DMA
    return pl.pallas_call(
        functools.partial(expert_kernel, experts, slots, cap),
        in_specs=[anyspace, vmem, vmem, anyspace, anyspace, anyspace],
        out_specs=[anyspace, anyspace, vmem, vmem, anyspace, vmem, vmem],
        out_shape=[
            jax.ShapeDtypeStruct((total, width), bf16),
            jax.ShapeDtypeStruct((total, width), bf16),
            jax.ShapeDtypeStruct((1, width), f32),
            jax.ShapeDtypeStruct((width, hidden), f32),
            jax.ShapeDtypeStruct((hidden, width), f32),
            jax.ShapeDtypeStruct((width, hidden), bf16),
            jax.ShapeDtypeStruct((hidden, width), bf16),
        ],
        scratch_shapes=[
            pltpu.VMEM((total, width), bf16),
            pltpu.VMEM((hidden, width), f32),
            pltpu.VMEM(router.shape, f32),
            pltpu.VMEM((total, 1), f32),
            pltpu.VMEM((total, width), bf16),
            pltpu.VMEM((4, width, hidden), bf16),
            pltpu.VMEM((4, hidden, width), bf16),
            pltpu.VMEM((total, width), bf16),
            pltpu.VMEM((4, total, hidden), bf16),
            pltpu.VMEM((4, total, hidden), bf16),
            pltpu.VMEM((total, width), f32),
            pltpu.VMEM((total, width), f32),
            pltpu.VMEM((total, width), bf16),
            pltpu.VMEM((width, width), bf16),
            pltpu.VMEM((4, width, width), bf16),
            dma((experts,)), dma((experts,)), dma((experts,)), dma((experts,)),
            dma((5,)), dma((5,)), dma((4,)), dma((4,)), dma((2,)), dma((5,)),
        ],
        compiler_params=pltpu.CompilerParams(
            collective_id=1, has_side_effects=True, vmem_limit_bytes=60 * 2**20
        ),
        cost_estimate=pl.CostEstimate(flops=30 * 10**9, bytes_accessed=40 * 10**6, transcendentals=3 * 10**6),
        name="expert",
    )(rows, cot_rows, router, w_in, w_out, w_in_far)


def shards(
    inputs, cotangent, routes, domains, domain_counts, domain_weights, keep_mask, gain_one, shift_one,
    w_qkv, w_proj, gain_two, shift_two, w_router, w_in, w_out,
):
    tok, width = inputs.shape
    experts = w_router.shape[1]
    cap = max(2, tok * 5 // (4 * experts))
    slots = (cap + 16) // 16 * 16
    domain_ids = jnp.arange(domain_weights.shape[0], dtype=jnp.int32)
    same_domain = domains[:, None] == domain_ids[None, :]
    seq_weight = jnp.sum(jnp.where(same_domain, domain_weights[None, :], 0.0), axis=1)
    seq_counts = jnp.sum(jnp.where(same_domain, domain_counts[None, :], 0), axis=1).astype(f32)
    factor = keep_mask.astype(f32) * seq_weight * count_scale / seq_counts

    w_own = jnp.transpose(w_qkv, (1, 2, 0))
    normed, qkv, ext, mixed, log_total, heads, proj, hidden, rows, cot_rows, placing_t, w_in_far = run_forward(
        inputs, cotangent, routes.reshape(1, -1), factor, gain_one, shift_one, gain_two,
        shift_two, w_own, w_proj, w_in[0], experts, cap, slots,
    )
    d_returned, result, router_grad, here_in, here_out, there_in, there_out = run_expert(
        rows, cot_rows, w_router.T, w_in[0], w_out[0], w_in_far, experts, cap
    )
    output, input_grad, sums, small, far_in, far_out = run_backward(
        inputs, cotangent, factor, hidden, gain_one, gain_two, placing_t, d_returned, result,
        normed, qkv, ext, mixed, log_total, heads, proj, router_grad, there_in, there_out, experts,
    )
    part = w_proj.shape[0]
    sums = sums[:, : 4 * part // sums.shape[0]].reshape(4, part, -1)
    return (
        output,
        input_grad,
        small[0],
        small[1],
        jnp.transpose(sums[1:].astype(f32), (2, 0, 1)),
        sums[0].astype(f32),
        small[2],
        small[3],
        small[8 : 8 + experts].T,
        (here_in + far_in.astype(f32))[None],
        (here_out + far_out.astype(f32))[None],
    )


def solution(mesh):
    tokens, group = P(("dp", "mp"), None), P("dp")
    return jax.shard_map(
        shards,
        mesh=mesh,
        in_specs=(
            tokens, tokens, P("dp", None), group, P(), P(), group, P(), P(),
            P(None, None, "mp"), P("mp", None), P(), P(), P(),
            P("dp", None, "mp"), P("dp", "mp", None),
        ),
        out_specs=(
            tokens, tokens, P(), P(), P(None, None, "mp"), P("mp", None), P(), P(), P(),
            P("dp", None, "mp"), P("dp", "mp", None),
        ),
        check_vma=False,
    )
```

```python
import functools

import jax
import jax.numpy as jnp
from jax import lax
from jax.experimental import pallas as pl
from jax.experimental.pallas import tpu as pltpu
from jax.sharding import PartitionSpec as P

HEAD_DIM = 64
LEN = 1024
BLOCK = 256
HALF = LEN // 2

norm_epsilon = 1e-05
count_scale = 10.0
masked_score = -1e30

f32 = jnp.float32
bf16 = jnp.bfloat16
MESH = pl.DeviceIdType.MESH
NT = (((1,), (1,)), ((), ()))
NN = (((1,), (0,)), ((), ()))
TN = (((0,), (0,)), ((), ()))


def dot(left, right, dims=NN):
    return lax.dot_general(left, right, dims, preferred_element_type=f32)


def mask_diagonal(scores, whole):
    first = lax.broadcasted_iota(jnp.int32, (BLOCK, BLOCK), 0)
    second = lax.broadcasted_iota(jnp.int32, (BLOCK, BLOCK), 1)
    last = jnp.where(first <= second, scores[whole * BLOCK :], masked_score)
    if not whole:
        return last
    return jnp.concatenate([scores[: whole * BLOCK], last], axis=0)


def remote(src, dst, send, recv, device):
    return pltpu.make_async_remote_copy(
        src_ref=src, dst_ref=dst, send_sem=send, recv_sem=recv, device_id=device, device_id_type=MESH
    )


def greet(devices):
    barrier = pltpu.get_barrier_semaphore()
    for device in devices:
        pl.semaphore_signal(barrier, inc=1, device_id=device, device_id_type=MESH)
    pl.semaphore_wait(barrier, len(devices))


def normalise(values):
    centre = values - jnp.mean(values, axis=-1, keepdims=True)
    inverse = lax.rsqrt(jnp.mean(centre * centre, axis=-1, keepdims=True) + norm_epsilon)
    return centre * inverse, inverse


def norm_pull(d_normed, scaled, inverse, gain):
    d_scaled = d_normed * gain
    return inverse * (
        d_scaled
        - jnp.mean(d_scaled, axis=-1, keepdims=True)
        - scaled * jnp.mean(d_scaled * scaled, axis=-1, keepdims=True)
    )


PAIRS = 3
PAIR = 2 * HEAD_DIM
STRIP = 256


def pick_sequence(positions, loss):
    domains, counts, weights, keep = loss
    value = jnp.zeros(positions.shape, f32)
    for index in range(domains.shape[0]):
        domain = domains[index]
        weight = jnp.full(positions.shape, keep[index].astype(f32) * weights[domain], f32)
        factor = weight * count_scale / jnp.full(positions.shape, counts[domain].astype(f32), f32)
        value = jnp.where(positions >= index * LEN, factor, value)
    return value


def forward_kernel(
    experts, slots, cap,
    domains_ref, counts_ref, weights_ref, keep_ref, x_ref, cot_ref, routes_ref, gain_one_ref, shift_one_ref, gain_two_ref, shift_two_ref,
    w_ref, proj_ref, w_in_ref,
    normed_out, qkv_out, ext_out, mixed_out, log_out, heads_out, proj_out, hidden_out, rows_out, cot_out,
    placing_t_out, w_in_far_out,
    normed, qkv, ext, mixed, logs, heads, proj, hidden, rows, placing, placing_t, cot_send, mixed_far, normed_two,
    keys, values,
    w_sems, pass_sems, proj_sems, w_in_sems, normed_sems, ext_sems, mixed_sems, row_send, row_recv, local_sems,
    save_sems,
):
    me, mp = lax.axis_index("dp"), lax.axis_index("mp")
    chip, core = mp // 2, mp % 2
    tok, width = x_ref.shape
    part = proj_ref.shape[0]
    total = experts * slots
    beside = {"mp": mp + 1 - 2 * core}
    across = {"mp": (mp + 2) % 4}
    side = me % 2
    partner = {"dp": me + 1 - 2 * side}
    second = chip == 1
    others = [(me + k) % experts for k in range(1, experts)]
    greet([{"dp": other} for other in others] + [beside, across])

    own_part = pl.ds(pl.multiple_of(chip * part, 16), part)
    other_part = pl.ds(pl.multiple_of((1 - chip) * part, 16), part)
    half = pl.ds(pl.multiple_of(side * (width // 2), 128), width // 2)

    def w_copy(index):
        if index == 3:
            source, target = proj_ref.at[:, half], proj.at[0, own_part, half]
        else:
            source, target = w_ref.at[index, :, half], heads.at[index, own_part, half]
        return remote(source, target, w_sems.at[0, index], w_sems.at[1, index], across)

    def w_pass(index):
        block = proj.at[0, other_part, half] if index == 3 else heads.at[index, other_part, half]
        return remote(block, block, pass_sems.at[0, index], pass_sems.at[1, index], partner)

    proj_pass = remote(proj.at[0], proj.at[1], proj_sems.at[0], proj_sems.at[1], beside)
    w_in_copy = remote(w_in_ref, w_in_far_out, w_in_sems.at[0], w_in_sems.at[1], across)
    for index in range(4):
        w_copy(index).start()
    w_local = pltpu.make_async_copy(w_ref, heads.at[:, own_part], local_sems.at[0])
    proj_local = pltpu.make_async_copy(proj_ref, proj.at[0, own_part], local_sems.at[1])
    w_local.start()
    proj_local.start()

    mine = pl.multiple_of(core * tok, tok)

    def first_norm(step, carry):
        at = pl.ds(pl.multiple_of(step * STRIP, STRIP), STRIP)
        scaled, _ = normalise(x_ref[at].astype(f32))
        normed[pl.ds(pl.multiple_of(HALF + mine + step * STRIP, STRIP), STRIP)] = (
            scaled * gain_one_ref[...][None, :] + shift_one_ref[...][None, :]
        ).astype(bf16)
        return carry

    lax.fori_loop(0, tok // STRIP, first_norm, 0)
    own_normed = normed.at[pl.ds(pl.multiple_of(HALF + mine, STRIP), tok)]
    normed_copy = remote(own_normed, own_normed, normed_sems.at[0], normed_sems.at[1], beside)
    normed_copy.start()

    wide = max(16, experts)
    own_routes = routes_ref[:, pl.ds(pl.multiple_of(mp * tok, tok), tok)]
    picked = own_routes == lax.broadcasted_iota(jnp.int32, (wide, tok), 0)
    earlier = lax.broadcasted_iota(jnp.int32, (tok, tok), 0) < lax.broadcasted_iota(jnp.int32, (tok, tok), 1)
    counts = dot(jnp.where(picked, 1.0, 0.0).astype(bf16), jnp.where(earlier, 1.0, 0.0).astype(bf16))
    rank = jnp.sum(jnp.where(picked, counts, 0.0), axis=0, keepdims=True)
    slot_of = own_routes.astype(f32) * slots + rank

    def place(step, carry):
        ids = lax.broadcasted_iota(jnp.int32, (STRIP, tok), 0) + step * STRIP
        at = pl.ds(pl.multiple_of(step * STRIP, STRIP), STRIP)
        placing[at] = jnp.where(ids.astype(f32) == slot_of, 1.0, 0.0).astype(bf16)
        return carry

    lax.fori_loop(0, total // STRIP, place, 0)

    positions = mp * tok + lax.broadcasted_iota(jnp.int32, (1, tok), 1)
    factors = pick_sequence(positions, (domains_ref, counts_ref, weights_ref, keep_ref))
    high = factors.astype(bf16)
    low = (factors - high.astype(f32)).astype(bf16)
    which = lax.broadcasted_iota(jnp.int32, (16, tok), 0)
    both = jnp.where(which == 0, high, jnp.where(which == 1, low, bf16(0)))
    spread = dot(both, placing[...], NT)

    def place_cot(step, carry):
        at = pl.ds(pl.multiple_of(step * STRIP, STRIP), STRIP)
        cot_send[at] = dot(placing[at], cot_ref[...]).astype(bf16)
        return carry

    lax.fori_loop(0, total // STRIP, place_cot, 0)
    spare = lax.broadcasted_iota(jnp.int32, (16, slots), 0) == cap - (slots - 16)
    for expert in range(experts):
        at = slice((expert + 1) * slots - 16, (expert + 1) * slots)
        here = slice(expert * slots, (expert + 1) * slots)
        for term, column in ((0, 0), (1, width // 2)):
            cot_send[at, column : column + slots] = jnp.where(
                spare, spread[term : term + 1, here], cot_send[at, column : column + slots].astype(f32)
            ).astype(bf16)

    def chunk(index):
        return pl.ds(pl.multiple_of(index * slots, 16), slots)

    def row_copy(target, source):
        return remote(
            cot_send.at[chunk(target)], cot_out.at[chunk(source)],
            row_send.at[target], row_recv.at[source], {"dp": target},
        )

    own_rows = pltpu.make_async_copy(cot_send.at[chunk(me)], cot_out.at[chunk(me)], local_sems.at[2])
    own_rows.start()
    same_side = [(me + k) % experts for k in range(2, experts, 2)]
    for other in same_side:
        row_copy(other, me).start()

    def turn(step, carry):
        at = pl.ds(pl.multiple_of(step * STRIP, STRIP), STRIP)
        placing_t[:, at] = placing[at].T
        return carry

    lax.fori_loop(0, total // STRIP, turn, 0)

    saves = []

    def save(source, target):
        copy = pltpu.make_async_copy(source, target, save_sems.at[len(saves)])
        copy.start()
        saves.append(copy)

    save(placing_t, placing_t_out)

    def pair_of(step):
        return (1 - chip) * step + chip * (PAIRS - 1 - step)

    def column(offset, pair):
        return pl.ds(pl.multiple_of((offset * PAIRS + pair) * PAIR, PAIR), PAIR)

    def project(step):
        pair = pair_of(step)
        weights = jnp.concatenate([heads[index, column(0, pair)] for index in range(3)])

        def strip_of(strip, carry):
            at = pl.ds(pl.multiple_of(strip * 512, 512), 512)
            value = dot(normed[pl.ds(pl.multiple_of(HALF + strip * 512, 512), 512)], weights, NT).astype(bf16)
            for index in range(3):
                qkv[at, column(index, pair)] = value[:, index * PAIR : (index + 1) * PAIR]
            return carry

        lax.fori_loop(0, 2 * tok // 512, strip_of, 0)

    lane = lax.broadcasted_iota(jnp.int32, (1, PAIR), 1)
    row = lax.broadcasted_iota(jnp.int32, (PAIR, 1), 0)

    def attend_blocks(pair, blocks):
        items = [(first, whole, head) for first, whole in blocks for head in range(2)]

        def start(first, whole, head):
            span = (whole + 1) * BLOCK
            near = pl.ds(pl.multiple_of(first + HALF - whole * BLOCK, BLOCK), span)
            queries = qkv[pl.ds(first, BLOCK), column(0, pair)] * bf16(0.125)
            own = jnp.where((lane // HEAD_DIM) == head, queries, bf16(0))
            return near, dot(keys[near], own, NT)

        waiting = start(*items[0])
        parts = []
        for index, (first, whole, head) in enumerate(items):
            near, scores = waiting
            if index + 1 < len(items):
                waiting = start(*items[index + 1])
            scores = mask_diagonal(scores, whole)
            largest = jnp.max(scores, axis=0, keepdims=True)
            expo = jnp.exp(scores - largest)
            summed = jnp.sum(expo, axis=0, keepdims=True)
            parts.append(dot(values[:, near], expo.astype(bf16)) / summed)
            at = pl.ds(first, BLOCK)
            logs[pair, head : head + 1, at] = largest + jnp.log(summed)
            if head:
                mixed[at, column(0, pair)] = jnp.where(row < HEAD_DIM, parts[-2], parts[-1]).T.astype(bf16)

    quarter = HALF // 2
    ext_rows = pl.ds(pl.multiple_of(core * quarter, quarter), quarter)
    ext_copy = remote(
        normed.at[pl.ds(pl.multiple_of(2 * tok + core * quarter, quarter), quarter)], normed.at[ext_rows],
        ext_sems.at[0, 0], ext_sems.at[1, 0], across,
    )
    ext_pass = remote(normed.at[ext_rows], normed.at[ext_rows], ext_sems.at[0, 1], ext_sems.at[1, 1], beside)
    w_local.wait()
    normed_copy.wait_recv()

    @pl.when(chip == 0)
    def _():
        ext_copy.start()

    w_in_copy.start()
    project(0)
    for index in range(4):
        w_copy(index).wait_recv()
        w_pass(index).start()

    def attention(step, carry):
        pair = pair_of(step)

        @pl.when(step == 1)
        def _():
            for index in range(3):
                w_pass(index).wait_recv()
            for other in [(me + k) % experts for k in range(1, experts, 2)]:
                row_copy(other, me).start()
            project(1)
            project(2)

        keys[HALF:] = qkv[:, column(1, pair)]
        values[:, HALF:] = qkv[:, column(2, pair)].T
        attend_blocks(pair, [(pl.multiple_of((2 * chip + whole) * BLOCK, BLOCK), whole) for whole in range(4)])

        @pl.when(chip == 0)
        def _():
            attend_blocks(pair, [(4 * BLOCK, 0), (5 * BLOCK, 1)])

        return carry

    lax.fori_loop(0, PAIRS, attention, 0)
    save(qkv, qkv_out)
    save(heads, heads_out)
    proj_local.wait()
    w_pass(3).wait_recv()
    proj_pass.start()
    save(proj.at[0], proj_out)

    @pl.when(second)
    def _():
        ext_copy.wait_recv()
        ext_pass.start()
        ext_pass.wait_recv()
        for index in range(2):
            ext[:, index * PAIRS * PAIR : (index + 1) * PAIRS * PAIR] = dot(
                normed[0:HALF], heads[1 + index], NT
            ).astype(bf16)

        def late(pair, carry):
            keys[0:HALF] = ext[:, column(0, pair)]
            keys[HALF : 2 * HALF] = qkv[0:HALF, column(1, pair)]
            values[:, 0:HALF] = ext[:, column(1, pair)].T
            values[:, HALF : 2 * HALF] = qkv[0:HALF, column(2, pair)].T
            attend_blocks(pair, [(0, 2), (BLOCK, 3)])
            return carry

        lax.fori_loop(0, PAIRS, late, 0)

    @pl.when(chip == 0)
    def _():
        ext_copy.wait_send()
        ext[...] = jnp.zeros_like(ext)
        normed[0:HALF] = jnp.zeros((HALF, width), bf16)

    @pl.when(second)
    def _():
        ext_pass.wait_send()

    save(normed, normed_out)
    save(ext, ext_out)
    save(mixed, mixed_out)
    save(logs, log_out)
    mixed_copy = remote(
        mixed.at[pl.ds(pl.multiple_of((1 - core) * tok, tok), tok)], mixed_far,
        mixed_sems.at[0], mixed_sems.at[1], beside,
    )
    mixed_copy.start()
    proj_pass.wait_recv()
    mixed_copy.wait_recv()

    def second_norm(step, carry):
        at = pl.ds(pl.multiple_of(step * STRIP, STRIP), STRIP)
        value = x_ref[at].astype(f32) + (
            dot(mixed[pl.ds(pl.multiple_of(mine + step * STRIP, STRIP), STRIP)], proj[0])
            + dot(mixed_far[at], proj[1])
        )
        hidden[at] = value
        scaled, _ = normalise(value)
        normed_two[at] = (scaled * gain_two_ref[...][None, :] + shift_two_ref[...][None, :]).astype(bf16)
        return carry

    lax.fori_loop(0, tok // STRIP, second_norm, 0)
    save(hidden, hidden_out)

    def place_rows(step, carry):
        at = pl.ds(pl.multiple_of(step * STRIP, STRIP), STRIP)
        rows[at] = dot(placing[at], normed_two[...]).astype(bf16)
        return carry

    lax.fori_loop(0, total // STRIP, place_rows, 0)
    save(rows, rows_out)
    own_rows.wait()
    for other in others:
        row_copy(me, other).wait_recv()
        row_copy(other, me).wait_send()
    for index in range(4):
        w_copy(index).wait_send()
        w_pass(index).wait_send()
    for copy in (proj_pass, normed_copy, mixed_copy):
        copy.wait_send()
    for copy in saves:
        copy.wait()
    w_in_copy.wait()


def run_forward(
    loss, x, cotangent, routes, gain_one, shift_one, gain_two, shift_two, w_heads, w_proj, w_in, experts, cap, slots
):
    tok, width = x.shape
    rows = 2 * tok
    total = experts * slots
    part = w_proj.shape[0]
    anyspace, vmem = pl.BlockSpec(memory_space=pl.ANY), pl.BlockSpec(memory_space=pltpu.VMEM)
    smem = pl.BlockSpec(memory_space=pltpu.SMEM)
    dma = pltpu.SemaphoreType.DMA
    kept = [
        ((HALF + rows, width), bf16),
        ((rows, 3 * PAIRS * PAIR), bf16),
        ((HALF, 2 * PAIRS * PAIR), bf16),
        ((rows, PAIRS * PAIR), bf16),
        ((PAIRS, 8, rows), f32),
        ((3, 2 * part, width), bf16),
    ]
    late = [((tok, width), f32), ((total, width), bf16)]
    return pl.pallas_call(
        functools.partial(forward_kernel, experts, slots, cap),
        in_specs=[smem] * 4 + [vmem] * 7 + [anyspace] * 3,
        out_specs=[anyspace] * 12,
        out_shape=[
            jax.ShapeDtypeStruct(*item)
            for item in kept
            + [((2 * part, width), bf16)]
            + late
            + [((total, width), bf16), ((tok, total), bf16), (w_in.shape, bf16)]
        ],
        scratch_shapes=[pltpu.VMEM(*item) for item in kept + [((2, 2 * part, width), bf16)] + late]
        + [
            pltpu.VMEM((total, tok), bf16),
            pltpu.VMEM((tok, total), bf16),
            pltpu.VMEM((total, width), bf16),
            pltpu.VMEM((tok, PAIRS * PAIR), bf16),
            pltpu.VMEM((tok, width), bf16),
            pltpu.VMEM((HALF + rows, PAIR), bf16),
            pltpu.VMEM((PAIR, HALF + rows), bf16),
            dma((2, 4)), dma((2, 4)), dma((2,)), dma((2,)), dma((2,)), dma((2, 2)), dma((2,)),
            dma((experts,)), dma((experts,)), dma((3,)), dma((10,)),
        ],
        compiler_params=pltpu.CompilerParams(
            collective_id=4, has_side_effects=True, vmem_limit_bytes=56 * 2**20
        ),
        cost_estimate=pl.CostEstimate(flops=30 * 10**9, bytes_accessed=30 * 10**6, transcendentals=8 * 10**6),
        name="forward",
    )(*loss, x, cotangent, routes, gain_one, shift_one, gain_two, shift_two, w_heads, w_proj, w_in)


def backward_kernel(
    experts, slots,
    domains_ref, counts_ref, weights_ref, keep_ref,
    hidden_ref, gain_one_ref, gain_two_ref, placing_ref, d_returned_ref, router_ref,
    cot_any, result_ref, there_in_ref, there_out_ref, mixed_any, proj_any, qkv_any, ext_any, log_any, normed_any, heads_any, x_any,
    output_ref, input_grad_ref, total_ref, small_ref, far_in_ref, far_out_ref,
    mixed_ref, proj_ref, qkv_ref, ext_ref, log_ref, normed_ref, heads_ref, x_ref, saved,
    summed, returned, d_hidden, d_branch, d_mixed, keys, values, d_keys, d_values, d_qkv, d_ext,
    grads_own, grads_send, grads_recv, d_norm, norm_recv, ext_recv,
    held, half_recv, piece_recv, small, first_slots, second_slots, last_slots,
    row_send, row_recv, branch_sems, norm_sems, ext_sems, far_sems, grad_sems,
    half_sems, piece_sems, gather_sems, back_sems, small_sems, load_sems, local_sems,
):
    me, mp = lax.axis_index("dp"), lax.axis_index("mp")
    chip, core = mp // 2, mp % 2
    tok, width = hidden_ref.shape
    rows = 2 * tok
    part = grads_own.shape[1]
    all_heads = PAIRS * PAIR
    beside = {"mp": mp + 1 - 2 * core}
    across = {"mp": (mp + 2) % 4}
    second = chip == 1
    others = [(me + k) % experts for k in range(1, experts)]
    diagonal = {"mp": 3 - mp}
    greet([{"dp": other} for other in others] + [beside, across, diagonal])

    def chunk(index):
        return pl.ds(pl.multiple_of(index * slots, 16), slots)

    def row_copy(target, source):
        return remote(
            result_ref.at[chunk(target)], returned.at[chunk(source)],
            row_send.at[target], row_recv.at[source], {"dp": target},
        )

    cot_copy = pltpu.make_async_copy(cot_any, grads_send, local_sems.at[1])
    cot_copy.start()
    loads = [
        pltpu.make_async_copy(source, target, load_sems.at[index])
        for index, (source, target) in enumerate(
            (
                (mixed_any, mixed_ref), (proj_any, proj_ref), (qkv_any, qkv_ref), (ext_any, ext_ref),
                (log_any, log_ref), (normed_any, normed_ref), (heads_any, heads_ref), (x_any, x_ref),
            )
        )
    ]
    for load in loads:
        load.start()
    far_half = there_in_ref.shape[0] // 2
    far_copies = [
        remote(
            there_out_ref.at[pl.ds(far_half, far_half)], far_out_ref, far_sems.at[0, 0], far_sems.at[1, 0], across
        )
    ] + [
        remote(
            there_in_ref.at[pl.ds(index * far_half, far_half)], far_in_ref.at[pl.ds(index * far_half, far_half)],
            far_sems.at[0, 1 + index], far_sems.at[1, 1 + index], across,
        )
        for index in range(2)
    ]
    far_copies[0].start()
    far_copies[1].start()
    own_rows = pltpu.make_async_copy(result_ref.at[chunk(me)], returned.at[chunk(me)], local_sems.at[0])
    own_rows.start()
    for other in others:
        row_copy(other, me).start()

    cot_copy.wait()
    small[...] = jnp.zeros_like(small)
    mine = pl.multiple_of(core * tok, tok)

    def second_norm(step, carry):
        at = pl.ds(pl.multiple_of(step * STRIP, STRIP), STRIP)
        scaled, inverse = normalise(hidden_ref[at])
        d_normed = dot(placing_ref[at], d_returned_ref[...])
        small[2:3] += jnp.sum(d_normed * scaled, axis=0, keepdims=True)
        small[3:4] += jnp.sum(d_normed, axis=0, keepdims=True)
        positions = mp * tok + step * STRIP + lax.broadcasted_iota(jnp.int32, (STRIP, 1), 0)
        total = grads_send[at].astype(f32) * pick_sequence(
            positions, (domains_ref, counts_ref, weights_ref, keep_ref)
        ) + norm_pull(
            d_normed, scaled, inverse, gain_two_ref[...][None, :]
        )
        d_hidden[at] = total
        d_branch[pl.ds(pl.multiple_of(mine + step * STRIP, STRIP), STRIP)] = total.astype(bf16)
        return carry

    lax.fori_loop(0, tok // STRIP, second_norm, 0)
    own_branch = d_branch.at[pl.ds(mine, tok)]
    branch_copy = remote(own_branch, own_branch, branch_sems.at[0], branch_sems.at[1], beside)
    branch_copy.start()

    for load in loads[:2]:
        load.wait()

    def push_branch(base):
        def push(step, carry):
            at = pl.ds(pl.multiple_of(base + step * STRIP, STRIP), STRIP)
            d_mixed[at] = dot(d_branch[at], proj_ref[...], NT).astype(bf16)
            return carry

        lax.fori_loop(0, tok // STRIP, push, 0)

    push_branch(mine)
    branch_copy.wait()
    push_branch((1 - core) * tok)

    side, line = me % 2, me // 2
    lines = experts // 2
    partner = {"dp": me + 1 - 2 * side}
    mates = [(line + k) % lines for k in range(1, lines)]
    piece_rows = held.shape[1] // lines
    own_columns = pl.ds(pl.multiple_of(side * (width // 2), 128), width // 2)
    other_columns = pl.ds(pl.multiple_of((1 - side) * (width // 2), 128), width // 2)

    def piece(index):
        return pl.ds(pl.multiple_of(index * piece_rows, 16), piece_rows)

    def sent(index):
        return slice(index * part, (index + 1) * part)

    def grad_copy(index):
        return remote(
            grads_send.at[sent(index)], grads_recv.at[index], grad_sems.at[0, index], grad_sems.at[1, index], across
        )

    def half_copy(index):
        return remote(
            held.at[index, :, other_columns], half_recv.at[index],
            half_sems.at[0, index], half_sems.at[1, index], partner,
        )

    def piece_copy(index, target, source):
        return remote(
            held.at[index, piece(target), own_columns], piece_recv.at[index, source],
            piece_sems.at[0, index, target], piece_sems.at[1, index, source], {"dp": 2 * target + side},
        )

    def gather_copy(index, target, source):
        block = total_ref.at[index, piece(source), own_columns]
        return remote(
            block, block,
            gather_sems.at[0, index, target], gather_sems.at[1, index, source], {"dp": 2 * target + side},
        )

    def back_copy(index):
        block = total_ref.at[index, :, own_columns]
        return remote(block, block, back_sems.at[0, index], back_sems.at[1, index], partner)

    def product(left, right, first):
        def block(step, carry):
            at = pl.ds(pl.multiple_of(first + step * PAIR, PAIR), PAIR)
            summed[pl.ds(pl.multiple_of(step * PAIR, PAIR), PAIR)] = dot(left[:, at], right[...], TN)
            return carry

        lax.fori_loop(0, PAIRS, block, 0)

    def send_grad(index):
        grads_own[index] = summed[pl.ds(pl.multiple_of(chip * part, 16), part)]
        grads_send[sent(index)] = summed[pl.ds(pl.multiple_of((1 - chip) * part, 16), part)].astype(bf16)

        grad_copy(index).start()

    chunks = held.shape[0]
    parts = 4 // chunks

    def stage_one(index):
        if index >= chunks:
            return
        for at in range(parts):
            number = index * parts + at
            grad_copy(number).wait_recv()
            held[index, at * part : (at + 1) * part] = (
                grads_own[number] + grads_recv[number].astype(f32)
            ).astype(bf16)
        if held.shape[1] > parts * part:
            held[index, parts * part :] = jnp.zeros((held.shape[1] - parts * part, width), bf16)
        half_copy(index).start()

    def stage_two(index):
        if index >= chunks:
            return
        half_copy(index).wait_recv()
        held[index, :, own_columns] = (
            held[index, :, own_columns].astype(f32) + half_recv[index].astype(f32)
        ).astype(bf16)
        for mate in mates:
            piece_copy(index, mate, line).start()

    def stage_three(index):
        if index >= chunks:
            return
        value = held[index, piece(line), own_columns].astype(f32)
        for mate in mates:
            piece_copy(index, line, mate).wait_recv()
            value += piece_recv[index, mate].astype(f32)
        total_ref[index, piece(line), own_columns] = value.astype(bf16)
        for mate in mates:
            gather_copy(index, mate, line).start()

    def stage_four(index):
        if index >= chunks:
            return
        for mate in mates:
            gather_copy(index, line, mate).wait_recv()
        back_copy(index).start()

    product(mixed_ref, d_branch, 0)
    send_grad(0)

    lane = lax.broadcasted_iota(jnp.int32, (1, PAIR), 1)

    def column(offset, pair):
        return pl.ds(pl.multiple_of((offset * PAIRS + pair) * PAIR, PAIR), PAIR)

    def attend_blocks(pair, blocks):
        for first, whole in blocks:
            span = (whole + 1) * BLOCK
            start = pl.multiple_of(first + HALF - whole * BLOCK, BLOCK)
            at = pl.ds(first, BLOCK)
            queries = qkv_ref[at, column(0, pair)] * bf16(0.125)
            d_out = d_mixed[at, column(0, pair)]
            near = keys[pl.ds(start, span)]
            near_values = values[pl.ds(start, span)]
            product = (d_out.astype(f32) * mixed_ref[at, column(0, pair)].astype(f32)).T
            dq = dk = dv = 0.0
            for head in range(2):
                here = (lane // HEAD_DIM) == head
                own = jnp.where(here, queries, bf16(0))
                d_own = jnp.where(here, d_out, bf16(0))
                delta = jnp.sum(product[HEAD_DIM * head : HEAD_DIM * (head + 1)], axis=0, keepdims=True)
                scores = mask_diagonal(dot(near, own, NT), whole)
                probs = jnp.exp(scores - log_ref[pair, head : head + 1, at])
                d_probs = dot(near_values, d_own, NT)
                d_scores = (probs * (d_probs - delta)).astype(bf16)
                dv = dv + dot(probs.astype(bf16), d_own)
                dk = dk + dot(d_scores, own)
                dq = dq + dot(d_scores, jnp.where(here, near, bf16(0)), TN)
            d_qkv[at, column(0, pair)] = (dq * 0.125).astype(bf16)
            d_keys[pl.ds(start, span)] += dk
            d_values[pl.ds(start, span)] += dv

    ext_part, norm_send = d_branch.at[tok : tok + HALF], d_branch.at[0:tok]
    ext_beside = remote(ext_part, ext_recv, ext_sems.at[0, 0], ext_sems.at[1, 0], beside)
    ext_across = remote(ext_part, ext_recv, ext_sems.at[0, 1], ext_sems.at[1, 1], across)
    for load in loads[2:5]:
        load.wait()

    @pl.when(second)
    def _():
        def early(pair, carry):
            keys[0:HALF] = ext_ref[:, column(0, pair)]
            keys[HALF : 2 * HALF] = qkv_ref[0:HALF, column(1, pair)]
            values[0:HALF] = ext_ref[:, column(1, pair)]
            values[HALF : 2 * HALF] = qkv_ref[0:HALF, column(2, pair)]
            d_keys[0 : 2 * HALF] = jnp.zeros((2 * HALF, PAIR), f32)
            d_values[0 : 2 * HALF] = jnp.zeros((2 * HALF, PAIR), f32)
            attend_blocks(pair, [(0, 2), (BLOCK, 3)])
            d_ext[:, column(0, pair)] = d_keys[0:HALF].astype(bf16)
            d_ext[:, column(1, pair)] = d_values[0:HALF].astype(bf16)
            saved[pair, :, 0:PAIR] = d_keys[HALF : 2 * HALF]
            saved[pair, :, PAIR:] = d_values[HALF : 2 * HALF]
            return carry

        lax.fori_loop(0, PAIRS, early, 0)

    for load in loads[5:7]:
        load.wait()

    @pl.when(second)
    def _():
        ext_part[...] = dot(d_ext[...], heads_ref[1:3].reshape(2 * all_heads, width)).astype(bf16)

    @pl.when(chip == 0)
    def _():
        d_ext[...] = jnp.zeros_like(d_ext)
        saved[...] = jnp.zeros_like(saved)

    @pl.when(mp == 2)
    def _():
        ext_beside.start()

    def attention(pair, carry):
        keys[HALF:] = qkv_ref[:, column(1, pair)]
        values[HALF:] = qkv_ref[:, column(2, pair)]
        d_keys[HALF : 2 * HALF] = saved[pair, :, 0:PAIR]
        d_keys[2 * HALF :] = jnp.zeros((rows - HALF, PAIR), f32)
        d_values[HALF : 2 * HALF] = saved[pair, :, PAIR:]
        d_values[2 * HALF :] = jnp.zeros((rows - HALF, PAIR), f32)
        attend_blocks(pair, [(pl.multiple_of((2 * chip + whole) * BLOCK, BLOCK), whole) for whole in range(4)])

        @pl.when(chip == 0)
        def _():
            attend_blocks(pair, [(4 * BLOCK, 0), (5 * BLOCK, 1)])

        @pl.when((mp == 3) & (pair == 0))
        def _():
            ext_beside.wait_recv()
            ext_part[...] = (ext_part[...].astype(f32) + ext_recv[...].astype(f32)).astype(bf16)
            ext_across.start()

        d_qkv[:, column(1, pair)] = d_keys[HALF:].astype(bf16)
        d_qkv[:, column(2, pair)] = d_values[HALF:].astype(bf16)
        return carry

    lax.fori_loop(0, PAIRS, attention, 0)

    product(d_qkv, normed_ref.at[HALF:], 0)
    send_grad(1)

    for index in (1, 2):
        product(d_qkv, normed_ref.at[HALF:], index * all_heads)

        @pl.when(second)
        def _():
            def block(step, carry):
                at = pl.ds(pl.multiple_of((index - 1) * all_heads + step * PAIR, PAIR), PAIR)
                summed[pl.ds(pl.multiple_of(step * PAIR, PAIR), PAIR)] += dot(d_ext[:, at], normed_ref[0:HALF], TN)
                return carry

            lax.fori_loop(0, PAIRS, block, 0)

        send_grad(1 + index)
    stage_one(0)

    weights = heads_ref[...].reshape(3 * all_heads, width)

    def push_norm(step, carry):
        at = pl.ds(pl.multiple_of((1 - core) * tok + step * STRIP, STRIP), STRIP)
        norm_send[pl.ds(pl.multiple_of(step * STRIP, STRIP), STRIP)] = dot(d_qkv[at], weights).astype(bf16)
        return carry

    def pull_norm(step, carry):
        at = pl.ds(pl.multiple_of(mine + step * STRIP, STRIP), STRIP)
        d_norm[pl.ds(pl.multiple_of(step * STRIP, STRIP), STRIP)] = dot(d_qkv[at], weights)
        return carry

    lax.fori_loop(0, tok // STRIP, push_norm, 0)
    norm_copy = remote(norm_send, norm_recv, norm_sems.at[0], norm_sems.at[1], beside)
    norm_copy.start()
    lax.fori_loop(0, tok // STRIP, pull_norm, 0)
    stage_two(0)
    stage_one(1)
    own_rows.wait()
    for other in others:
        row_copy(me, other).wait_recv()

    def finish(step, carry):
        at = pl.ds(pl.multiple_of(step * STRIP, STRIP), STRIP)
        output_ref[at] = (hidden_ref[at] + dot(placing_ref[at], returned[...])).astype(bf16)
        return carry

    lax.fori_loop(0, tok // STRIP, finish, 0)
    stage_three(0)
    stage_two(1)
    stage_one(2)
    norm_copy.wait_recv()
    loads[7].wait()

    @pl.when(mp == 1)
    def _():
        ext_across.wait_recv()
        d_norm[tok - HALF :] += ext_recv[...].astype(f32)

    def first_norm(step, carry):
        at = pl.ds(pl.multiple_of(step * STRIP, STRIP), STRIP)
        scaled, inverse = normalise(x_ref[at].astype(f32))
        d_normed = d_norm[at] + norm_recv[at].astype(f32)
        small[0:1] += jnp.sum(d_normed * scaled, axis=0, keepdims=True)
        small[1:2] += jnp.sum(d_normed, axis=0, keepdims=True)
        input_grad_ref[at] = (
            d_hidden[at] + norm_pull(d_normed, scaled, inverse, gain_one_ref[...][None, :])
        ).astype(bf16)
        return carry

    lax.fori_loop(0, tok // STRIP, first_norm, 0)

    small[4:5] = router_ref[...]
    rounds = [(first_slots, "dp", me, me - me % 8, 1, 8)]
    if experts > 8:
        rounds.append((second_slots, "dp", me, me % 8, 8, 8))
    rounds.append((last_slots, "mp", mp, mp - mp % 4, 1, 4))

    def small_copies(number, receiving):
        slots_of, axis, place, base, step, size = rounds[number]
        own = (place - base) // step
        copies = []
        for k in range(1, size):
            other = (own + k) % size
            source, target = (other, own) if receiving else (own, other)
            copies.append(
                remote(
                    slots_of.at[own], slots_of.at[source],
                    small_sems.at[0, number, target], small_sems.at[1, number, source],
                    {axis: base + other * step},
                )
            )
        return copies

    def small_start(number):
        for copy in small_copies(number, False):
            copy.start()

    def small_finish(number):
        for copy in small_copies(number, True):
            copy.wait_recv()
        slots_of, size = rounds[number][0], rounds[number][-1]
        value = slots_of[0]
        for index in range(1, size):
            value += slots_of[index]
        return value

    first_slots[me % 8] = small[...]
    small_start(0)
    stage_four(0)
    stage_three(1)
    stage_two(2)
    norms = small_finish(0)
    if experts > 8:
        second_slots[me // 8, 0:8] = norms
        for index in range(8):
            second_slots[me // 8, 8 + index : 9 + index] = first_slots[index, 4:5]
        small_start(1)
        norms = small_finish(1)
        for index in range(8):
            last_slots[mp % 4, 8 + 8 * index : 16 + 8 * index] = second_slots[index, 8:16]
    else:
        for index in range(8):
            last_slots[mp % 4, 8 + index : 9 + index] = first_slots[index, 4:5]
    last_slots[mp % 4, 0:8] = norms[0:8]
    small_start(len(rounds) - 1)
    far_copies[2].start()
    stage_one(3)
    stage_four(1)
    stage_three(2)
    stage_two(3)
    stage_four(2)
    stage_three(3)
    small_ref[...] = small_finish(len(rounds) - 1)
    stage_four(3)
    for index in range(chunks):
        other = total_ref.at[index, :, other_columns]
        remote(other, other, back_sems.at[0, index], back_sems.at[1, index], partner).wait_recv()

    for other in others:
        row_copy(other, me).wait_send()
    for mate in mates:
        for index in range(chunks):
            piece_copy(index, mate, line).wait_send()
            gather_copy(index, mate, line).wait_send()
    for index in range(4):
        grad_copy(index).wait_send()
    for index in range(chunks):
        half_copy(index).wait_send()
        back_copy(index).wait_send()
    for number in range(len(rounds)):
        for copy in small_copies(number, False):
            copy.wait_send()
    norm_copy.wait_send()

    @pl.when(mp == 2)
    def _():
        ext_beside.wait_send()

    @pl.when(mp == 3)
    def _():
        ext_across.wait_send()

    for copy in far_copies:
        copy.wait()


def run_backward(
    loss, x, cotangent, hidden, gain_one, gain_two, placing, d_returned, result, normed, qkv, ext,
    mixed, log_total, heads, proj, router_grad, there_in, there_out, experts,
):
    tok, width = x.shape
    rows = 2 * tok
    total = d_returned.shape[0]
    part = proj.shape[0] // 2
    lines = experts // 2
    steps = 2 if experts <= 8 else 3
    chunks = 4 if part % (16 * lines) == 0 else 2
    padded = (4 // chunks * part + 16 * lines - 1) // (16 * lines) * (16 * lines)
    small = (8 + max(8, experts), width)
    anyspace, vmem = pl.BlockSpec(memory_space=pl.ANY), pl.BlockSpec(memory_space=pltpu.VMEM)
    smem = pl.BlockSpec(memory_space=pltpu.SMEM)
    dma = pltpu.SemaphoreType.DMA
    return pl.pallas_call(
        functools.partial(backward_kernel, experts, total // experts),
        in_specs=[smem] * 4 + [vmem] * 6 + [anyspace] * 12,
        out_specs=[vmem] * 4 + [anyspace] * 2,
        out_shape=[
            jax.ShapeDtypeStruct((tok, width), bf16),
            jax.ShapeDtypeStruct((tok, width), bf16),
            jax.ShapeDtypeStruct((chunks, padded, width), bf16),
            jax.ShapeDtypeStruct(small, f32),
            jax.ShapeDtypeStruct(there_in.shape, bf16),
            jax.ShapeDtypeStruct((there_out.shape[0] // 2, width), bf16),
        ],
        scratch_shapes=[
            pltpu.VMEM(item.shape, item.dtype) for item in (mixed, proj, qkv, ext, log_total, normed, heads, x)
        ]
        + [
            pltpu.VMEM((PAIRS, HALF, 2 * PAIR), f32),
            pltpu.VMEM((PAIRS * PAIR, width), f32),
            pltpu.VMEM((total, width), bf16),
            pltpu.VMEM((tok, width), f32),
            pltpu.VMEM((rows, width), bf16),
            pltpu.VMEM((rows, PAIRS * PAIR), bf16),
            pltpu.VMEM((HALF + rows, PAIR), bf16),
            pltpu.VMEM((HALF + rows, PAIR), bf16),
            pltpu.VMEM((HALF + rows, PAIR), f32),
            pltpu.VMEM((HALF + rows, PAIR), f32),
            pltpu.VMEM((rows, 3 * PAIRS * PAIR), bf16),
            pltpu.VMEM((HALF, 2 * PAIRS * PAIR), bf16),
            pltpu.VMEM((4, part, width), f32),
            pltpu.VMEM((4 * part, width), bf16),
            pltpu.VMEM((4, part, width), bf16),
            pltpu.VMEM((tok, width), f32),
            pltpu.VMEM((tok, width), bf16),
            pltpu.VMEM((HALF, width), bf16),
            pltpu.VMEM((chunks, padded, width), bf16),
            pltpu.VMEM((chunks, padded, width // 2), bf16),
            pltpu.VMEM((chunks, lines, padded // lines, width // 2), bf16),
            pltpu.VMEM((8, width), f32),
            pltpu.VMEM((8, 8, width), f32),
            pltpu.VMEM((8, 16, width), f32),
            pltpu.VMEM((4,) + small, f32),
            dma((experts,)), dma((experts,)), dma((2,)), dma((2,)), dma((2, 2)), dma((2, 3)), dma((2, 4)),
            dma((2, chunks)), dma((2, chunks, lines)), dma((2, chunks, lines)), dma((2, chunks)),
            dma((2, steps, 8)), dma((8,)), dma((2,)),
        ],
        compiler_params=pltpu.CompilerParams(
            collective_id=2, has_side_effects=True, vmem_limit_bytes=62 * 2**20
        ),
        cost_estimate=pl.CostEstimate(flops=30 * 10**9, bytes_accessed=30 * 10**6, transcendentals=8 * 10**6),
        name="backward",
    )(
        *loss, hidden, gain_one, gain_two, placing, d_returned, router_grad,
        cotangent, result, there_in, there_out, mixed, proj, qkv, ext, log_total, normed, heads, x,
    )


def gelu_parts(pre):
    scale = 0.7978845608028654
    square = pre * pre
    inner = jnp.tanh(pre * (scale + (scale * 0.044715) * square))
    half = 0.5 * (1.0 + inner)
    slope = half + (0.5 * pre) * (1.0 - inner * inner) * (scale + (3.0 * scale * 0.044715) * square)
    return pre * half, slope

STAGES = 4

def expert_kernel(
    experts, slots, cap,
    rows_ref, cot_ref, router_ref, w_in_ref, w_out_ref, w_in_far_ref,
    back_ref, result_out, router_grad_ref, here_in_ref, here_out, there_in_ref, there_out_ref, far_grad_ref,
    result, here_out_held, router, factor, x, wi, wo, d_out, act, d_pre, total, d_x, give, g_send, g_recv,
    row_send, row_recv, back_send, back_recv, w_send, w_recv, g_send_sem, g_recv_sem, far_sems, save_sems, local_sem,
):
    me = lax.axis_index("dp")
    mp = lax.axis_index("mp")
    beside = {"mp": mp + 1 - 2 * (mp % 2)}
    across = {"mp": (mp + 2) % 4}
    members = experts // STAGES
    span = members * slots
    own_group, own_member = me // members, me % members

    def group_of(stage):
        return 2 * ((own_group // 2 + stage // 2) % 2) + (own_group % 2 + stage % 2) % 2

    def chunk(index):
        return pl.ds(pl.multiple_of(index * slots, 16), slots)

    def group_rows(group):
        return pl.ds(pl.multiple_of(group * span, 16), span)

    barrier = pltpu.get_barrier_semaphore()

    def greet(step, carry):
        pl.semaphore_signal(barrier, inc=1, device_id={"dp": (me + step) % experts}, device_id_type=MESH)
        return carry

    lax.fori_loop(1, experts, greet, 0)
    pl.semaphore_signal(barrier, inc=1, device_id=beside, device_id_type=MESH)
    pl.semaphore_signal(barrier, inc=1, device_id=across, device_id_type=MESH)
    pl.semaphore_wait(barrier, experts + 1)

    def remote(src, dst, send, recv, device):
        return pltpu.make_async_remote_copy(
            src_ref=src, dst_ref=dst, send_sem=send, recv_sem=recv, device_id=device, device_id_type=MESH
        )

    def row_copy(target, source):
        return remote(rows_ref.at[chunk(target)], x.at[chunk(source)], row_send.at[target], row_recv.at[source], {"dp": target})

    def back_copy(target, source):
        return remote(give.at[chunk(target)], back_ref.at[chunk(source)], back_send.at[target], back_recv.at[source], {"dp": target})

    def partners(stage):
        group = group_of(stage)
        if stage == 0:
            return [group * members + (own_member + k) % members for k in range(1, members)]
        return [group * members + (own_member + k) % members for k in range(members)]

    for stage in (3, 0, 1):
        for other in partners(stage):
            row_copy(other, me).start()
    own_rows = pltpu.make_async_copy(rows_ref.at[chunk(me)], x.at[chunk(me)], local_sem.at[0])
    own_in = pltpu.make_async_copy(w_in_ref, wi.at[0], local_sem.at[1])
    own_out = pltpu.make_async_copy(w_out_ref, wo.at[0], local_sem.at[2])
    far_in = pltpu.make_async_copy(w_in_far_ref, wi.at[2], local_sem.at[3])
    near_in = remote(w_in_ref, wi.at[1], w_send.at[0], w_recv.at[0], beside)
    near_out = remote(w_out_ref, wo.at[1], w_send.at[1], w_recv.at[1], beside)
    far_near_in = remote(w_in_far_ref, wi.at[3], w_send.at[2], w_recv.at[2], beside)
    far_out = remote(w_out_ref, wo.at[2], w_send.at[3], w_recv.at[3], across)
    far_near_out = remote(wo.at[2], wo.at[3], w_send.at[4], w_recv.at[4], beside)
    for copy in (own_rows, own_in, own_out, near_in, near_out, far_in, far_out, far_near_in):
        copy.start()
    router_grad_ref[...] = jnp.zeros_like(router_grad_ref)
    router[...] = router_ref[...].astype(f32)

    diagonal = lax.broadcasted_iota(jnp.int32, (slots, slots), 0) == lax.broadcasted_iota(
        jnp.int32, (slots, slots), 1
    )

    def prepare(stage, rows):
        for member in range(members):
            index = group_of(stage) * members + member
            spare = cot_ref[pl.ds(pl.multiple_of((index + 1) * slots - 16, 16), 16)].astype(f32)
            spare = spare[cap - slots + 16 : cap - slots + 17]
            value = spare[:, 0:slots] + spare[:, x.shape[1] // 2 : x.shape[1] // 2 + slots]
            factor[chunk(index)] = jnp.sum(jnp.where(diagonal, value, 0.0), axis=1, keepdims=True)
        features = x[rows].astype(f32)
        gate = jax.nn.sigmoid(jnp.sum(features * router[pl.ds(me, 1)], axis=1, keepdims=True))
        d_out[rows] = (gate * (cot_ref[rows].astype(f32) * factor[rows])).astype(bf16)
        total[rows] = jnp.zeros((span, x.shape[1]), f32)
        d_x[rows] = jnp.zeros((span, x.shape[1]), f32)

    def finish(stage, rows):
        features = x[rows].astype(f32)
        gate = jax.nn.sigmoid(jnp.sum(features * router[pl.ds(me, 1)], axis=1, keepdims=True))
        value = total[rows]
        d_gate = jnp.sum(cot_ref[rows].astype(f32) * factor[rows] * value, axis=1, keepdims=True)
        d_logit = (d_gate * gate * (1.0 - gate)).astype(bf16).astype(f32)
        give[rows] = (d_x[rows] + d_logit * router[pl.ds(me, 1)]).astype(bf16)
        result[rows] = (gate * value).astype(bf16)
        router_grad_ref[...] += jnp.sum(features * d_logit, axis=0, keepdims=True)

    def stage_of(step):
        near = jnp.where(step < 2, 0, jnp.where(step < 4, 1, 3))
        return jnp.where(step < 8, near, jnp.where(step < 12, 2, jnp.where(step < 14, 1, 0)))

    def step_body(step, carry):
        stage = stage_of(step)
        part = jnp.where(step < 6, step % 2, jnp.where((step < 8) | (step >= 12), 2 + step % 2, step - 8))
        rows = group_rows(group_of(stage))

        for static, at in enumerate((0, 2, 8, 4)):
            @pl.when(step == at)
            def _():
                if static == 0:
                    own_rows.wait()
                for other in partners(static):
                    row_copy(me, other).wait_recv()
        @pl.when((step == 0) | (step == 2) | (step == 4) | (step == 8))
        def _():
            prepare(stage, rows)

        @pl.when(step == 1)
        def _():
            for other in partners(2):
                row_copy(other, me).start()

        @pl.when(step == 0)
        def _():
            own_in.wait()
            own_out.wait()

        @pl.when(step == 1)
        def _():
            near_in.wait_recv()
            near_out.wait_recv()

        @pl.when(step == 6)
        def _():
            far_in.wait()
            far_out.wait_recv()
            far_near_out.start()

        @pl.when(step == 7)
        def _():
            far_near_in.wait_recv()
            far_near_out.wait_recv()

        pre = dot(x[rows], wi[part])
        value, slope = gelu_parts(pre)
        value = value.astype(bf16)
        act[part, rows] = value
        total[rows] += dot(value, wo[part])
        d_value = (dot(d_out[rows], wo[part], NT) * slope).astype(bf16)
        d_pre[part, rows] = d_value
        d_x[rows] += dot(d_value, wi[part], NT)

        @pl.when((step == 7) | (step == 11) | (step == 13) | (step == 15))
        def _():
            finish(stage, rows)

        for static, at in enumerate((15, 13, 11, 7)):
            @pl.when(step == at)
            def _():
                for other in partners(static):
                    back_copy(other, me).start()
        return carry

    lax.fori_loop(0, 16, step_body, 0)
    own_back = pltpu.make_async_copy(give.at[chunk(me)], back_ref.at[chunk(me)], local_sem.at[4])
    own_back.start()
    result_save = pltpu.make_async_copy(result, result_out, save_sems.at[0])
    result_save.start()

    kept = pl.ds(0, x.shape[1])
    outgoing = [g_send, act.at[3, kept], d_pre.at[3, kept], act.at[1, kept]]

    def product(left, right, store):
        def block(step, carry):
            at = pl.ds(pl.multiple_of(step * STRIP, STRIP), STRIP)
            store(at, dot(left[:, at], right[...], TN))
            return carry

        lax.fori_loop(0, x.shape[1] // STRIP, block, 0)

    def keep(target):
        def store(at, value):
            target[at] = value.astype(target.dtype)

        return store

    def grad_copy(index):
        return remote(outgoing[index], g_recv.at[index], g_send_sem.at[index], g_recv_sem.at[index], beside)

    product(act.at[3], d_out, keep(outgoing[0]))
    grad_copy(0).start()
    product(x, d_pre.at[3], keep(outgoing[1]))
    grad_copy(1).start()
    product(act.at[2], d_out, keep(total))
    product(act.at[1], d_out, keep(outgoing[2]))
    grad_copy(2).start()
    grad_copy(0).wait_recv()
    there_out_ref[...] = (total[kept] + g_recv[0].astype(f32)).astype(bf16)
    early = pl.ds(0, far_grad_ref.shape[0])
    far_grad = remote(there_out_ref.at[early], far_grad_ref, far_sems.at[0], far_sems.at[1], across)
    far_grad.start()
    product(x, d_pre.at[1], keep(outgoing[3]))
    grad_copy(3).start()
    product(x, d_pre.at[2], keep(d_x))
    product(act.at[0], d_out, keep(here_out_held))
    product(x, d_pre.at[0], keep(here_in_ref))
    grad_copy(1).wait_recv()
    there_in_ref[...] = (d_x[kept] + g_recv[1].astype(f32)).astype(bf16)
    grad_copy(2).wait_recv()
    here_out_held[...] += g_recv[2].astype(f32)
    here_save = pltpu.make_async_copy(here_out_held, here_out, save_sems.at[1])
    here_save.start()
    grad_copy(3).wait_recv()
    here_in_ref[...] += g_recv[3].astype(f32)

    result_save.wait()
    here_save.wait()
    own_back.wait()
    for stage in range(STAGES):
        for other in partners(stage):
            back_copy(me, other).wait_recv()
            back_copy(other, me).wait_send()
            row_copy(other, me).wait_send()
    for copy in (near_in, near_out, far_near_in, far_out, far_near_out):
        copy.wait_send()
    for index in range(4):
        grad_copy(index).wait_send()
    far_grad.wait()


def run_expert(rows, cot_rows, router, w_in, w_out, w_in_far, experts, cap):
    total, width = rows.shape
    slots = total // experts
    hidden = w_in.shape[1]
    anyspace, vmem = pl.BlockSpec(memory_space=pl.ANY), pl.BlockSpec(memory_space=pltpu.VMEM)
    dma = pltpu.SemaphoreType.DMA
    return pl.pallas_call(
        functools.partial(expert_kernel, experts, slots, cap),
        in_specs=[anyspace, vmem, vmem, anyspace, anyspace, anyspace],
        out_specs=[anyspace, anyspace, vmem, vmem, anyspace, vmem, vmem, anyspace],
        out_shape=[
            jax.ShapeDtypeStruct((total, width), bf16),
            jax.ShapeDtypeStruct((total, width), bf16),
            jax.ShapeDtypeStruct((1, width), f32),
            jax.ShapeDtypeStruct((width, hidden), f32),
            jax.ShapeDtypeStruct((hidden, width), f32),
            jax.ShapeDtypeStruct((width, hidden), bf16),
            jax.ShapeDtypeStruct((hidden, width), bf16),
            jax.ShapeDtypeStruct((hidden // 2, width), bf16),
        ],
        scratch_shapes=[
            pltpu.VMEM((total, width), bf16),
            pltpu.VMEM((hidden, width), f32),
            pltpu.VMEM(router.shape, f32),
            pltpu.VMEM((total, 1), f32),
            pltpu.VMEM((total, width), bf16),
            pltpu.VMEM((4, width, hidden), bf16),
            pltpu.VMEM((4, hidden, width), bf16),
            pltpu.VMEM((total, width), bf16),
            pltpu.VMEM((4, total, hidden), bf16),
            pltpu.VMEM((4, total, hidden), bf16),
            pltpu.VMEM((total, width), f32),
            pltpu.VMEM((total, width), f32),
            pltpu.VMEM((total, width), bf16),
            pltpu.VMEM((width, width), bf16),
            pltpu.VMEM((4, width, width), bf16),
            dma((experts,)), dma((experts,)), dma((experts,)), dma((experts,)),
            dma((5,)), dma((5,)), dma((4,)), dma((4,)), dma((2,)), dma((2,)), dma((5,)),
        ],
        compiler_params=pltpu.CompilerParams(
            collective_id=1, has_side_effects=True, vmem_limit_bytes=60 * 2**20
        ),
        cost_estimate=pl.CostEstimate(flops=30 * 10**9, bytes_accessed=40 * 10**6, transcendentals=3 * 10**6),
        name="expert",
    )(rows, cot_rows, router, w_in, w_out, w_in_far)


def shards(
    inputs, cotangent, routes, domains, domain_counts, domain_weights, keep_mask, gain_one, shift_one,
    w_qkv, w_proj, gain_two, shift_two, w_router, w_in, w_out,
):
    tok, width = inputs.shape
    experts = w_router.shape[1]
    cap = max(2, tok * 5 // (4 * experts))
    slots = (cap + 16) // 16 * 16
    loss = (domains, domain_counts, domain_weights, keep_mask)
    w_own = jnp.transpose(w_qkv, (1, 2, 0))
    normed, qkv, ext, mixed, log_total, heads, proj, hidden, rows, cot_rows, placing_t, w_in_far = run_forward(
        loss, inputs, cotangent, routes.reshape(1, -1), gain_one, shift_one, gain_two,
        shift_two, w_own, w_proj, w_in[0], experts, cap, slots,
    )
    d_returned, result, router_grad, here_in, here_out, there_in, there_out, far_early = run_expert(
        rows, cot_rows, w_router.T, w_in[0], w_out[0], w_in_far, experts, cap
    )
    output, input_grad, sums, small, far_in, far_out = run_backward(
        loss, inputs, cotangent, hidden, gain_one, gain_two, placing_t, d_returned, result,
        normed, qkv, ext, mixed, log_total, heads, proj, router_grad, there_in, there_out, experts,
    )
    part = w_proj.shape[0]
    sums = sums[:, : 4 * part // sums.shape[0]].reshape(4, part, -1)
    return (
        output,
        input_grad,
        small[0],
        small[1],
        jnp.transpose(sums[1:].astype(f32), (2, 0, 1)),
        sums[0].astype(f32),
        small[2],
        small[3],
        small[8 : 8 + experts].T,
        (here_in + far_in.astype(f32))[None],
        (here_out + jnp.concatenate([far_early, far_out]).astype(f32))[None],
    )


def solution(mesh):
    tokens, group = P(("dp", "mp"), None), P("dp")
    return jax.shard_map(
        shards,
        mesh=mesh,
        in_specs=(
            tokens, tokens, P("dp", None), group, P(), P(), group, P(), P(),
            P(None, None, "mp"), P("mp", None), P(), P(), P(),
            P("dp", None, "mp"), P("dp", "mp", None),
        ),
        out_specs=(
            tokens, tokens, P(), P(), P(None, None, "mp"), P("mp", None), P(), P(), P(),
            P("dp", None, "mp"), P("dp", "mp", None),
        ),
        check_vma=False,
    )
```

```python
import functools

import jax
import jax.numpy as jnp
from jax import lax
from jax.experimental import pallas as pl
from jax.experimental.pallas import tpu as pltpu
from jax.sharding import PartitionSpec as P

HEAD_DIM = 64
LEN = 1024
BLOCK = 256
HALF = LEN // 2

norm_epsilon = 1e-05
count_scale = 10.0
masked_score = -1e30

f32 = jnp.float32
bf16 = jnp.bfloat16
MESH = pl.DeviceIdType.MESH
NT = (((1,), (1,)), ((), ()))
NN = (((1,), (0,)), ((), ()))
TN = (((0,), (0,)), ((), ()))


def dot(left, right, dims=NN):
    return lax.dot_general(left, right, dims, preferred_element_type=f32)


def mask_diagonal(scores, whole):
    first = lax.broadcasted_iota(jnp.int32, (BLOCK, BLOCK), 0)
    second = lax.broadcasted_iota(jnp.int32, (BLOCK, BLOCK), 1)
    last = jnp.where(first <= second, scores[whole * BLOCK :], masked_score)
    if not whole:
        return last
    return jnp.concatenate([scores[: whole * BLOCK], last], axis=0)


def remote(src, dst, send, recv, device):
    return pltpu.make_async_remote_copy(
        src_ref=src, dst_ref=dst, send_sem=send, recv_sem=recv, device_id=device, device_id_type=MESH
    )


def greet(devices):
    barrier = pltpu.get_barrier_semaphore()
    for device in devices:
        pl.semaphore_signal(barrier, inc=1, device_id=device, device_id_type=MESH)
    pl.semaphore_wait(barrier, len(devices))


def normalise(values):
    centre = values - jnp.mean(values, axis=-1, keepdims=True)
    inverse = lax.rsqrt(jnp.mean(centre * centre, axis=-1, keepdims=True) + norm_epsilon)
    return centre * inverse, inverse


def norm_pull(d_normed, scaled, inverse, gain):
    d_scaled = d_normed * gain
    return inverse * (
        d_scaled
        - jnp.mean(d_scaled, axis=-1, keepdims=True)
        - scaled * jnp.mean(d_scaled * scaled, axis=-1, keepdims=True)
    )


PAIRS = 3
PAIR = 2 * HEAD_DIM
STRIP = 256


def pick_sequence(positions, loss):
    domains, counts, weights, keep = loss
    value = jnp.zeros(positions.shape, f32)
    for index in range(domains.shape[0]):
        domain = domains[index]
        weight = jnp.full(positions.shape, keep[index].astype(f32) * weights[domain], f32)
        factor = weight * count_scale / jnp.full(positions.shape, counts[domain].astype(f32), f32)
        value = jnp.where(positions >= index * LEN, factor, value)
    return value


def forward_kernel(
    experts, slots, cap,
    domains_ref, counts_ref, weights_ref, keep_ref, x_ref, cot_ref, routes_ref, gain_one_ref, shift_one_ref, gain_two_ref, shift_two_ref,
    w_ref, proj_ref, w_in_ref,
    normed_out, qkv_out, ext_out, mixed_out, log_out, heads_out, proj_out, hidden_out, rows_out, cot_out,
    placing_t_out, w_in_far_out,
    normed, qkv, ext, mixed, logs, heads, proj, hidden, rows, placing, placing_t, cot_send, mixed_far, normed_two,
    keys, values,
    w_sems, pass_sems, proj_sems, w_in_sems, normed_sems, ext_sems, mixed_sems, row_send, row_recv, local_sems,
    save_sems,
):
    me, mp = lax.axis_index("dp"), lax.axis_index("mp")
    chip, core = mp // 2, mp % 2
    tok, width = x_ref.shape
    part = proj_ref.shape[0]
    total = experts * slots
    beside = {"mp": mp + 1 - 2 * core}
    across = {"mp": (mp + 2) % 4}
    side = me % 2
    partner = {"dp": me + 1 - 2 * side}
    second = chip == 1
    others = [(me + k) % experts for k in range(1, experts)]
    greet([{"dp": other} for other in others] + [beside, across])

    own_part = pl.ds(pl.multiple_of(chip * part, 16), part)
    other_part = pl.ds(pl.multiple_of((1 - chip) * part, 16), part)
    half = pl.ds(pl.multiple_of(side * (width // 2), 128), width // 2)

    def w_copy(index):
        if index == 3:
            source, target = proj_ref.at[:, half], proj.at[0, own_part, half]
        else:
            source, target = w_ref.at[index, :, half], heads.at[index, own_part, half]
        return remote(source, target, w_sems.at[0, index], w_sems.at[1, index], across)

    def w_pass(index):
        block = proj.at[0, other_part, half] if index == 3 else heads.at[index, other_part, half]
        return remote(block, block, pass_sems.at[0, index], pass_sems.at[1, index], partner)

    proj_pass = remote(proj.at[0], proj.at[1], proj_sems.at[0], proj_sems.at[1], beside)
    w_in_copy = remote(w_in_ref, w_in_far_out, w_in_sems.at[0], w_in_sems.at[1], across)
    for index in range(4):
        w_copy(index).start()
    w_local = pltpu.make_async_copy(w_ref, heads.at[:, own_part], local_sems.at[0])
    proj_local = pltpu.make_async_copy(proj_ref, proj.at[0, own_part], local_sems.at[1])
    w_local.start()
    proj_local.start()

    mine = pl.multiple_of(core * tok, tok)

    def first_norm(step, carry):
        at = pl.ds(pl.multiple_of(step * STRIP, STRIP), STRIP)
        scaled, _ = normalise(x_ref[at].astype(f32))
        normed[pl.ds(pl.multiple_of(HALF + mine + step * STRIP, STRIP), STRIP)] = (
            scaled * gain_one_ref[...][None, :] + shift_one_ref[...][None, :]
        ).astype(bf16)
        return carry

    lax.fori_loop(0, tok // STRIP, first_norm, 0)
    own_normed = normed.at[pl.ds(pl.multiple_of(HALF + mine, STRIP), tok)]
    normed_copy = remote(own_normed, own_normed, normed_sems.at[0], normed_sems.at[1], beside)
    normed_copy.start()

    wide = max(16, experts)
    own_routes = routes_ref[:, pl.ds(pl.multiple_of(mp * tok, tok), tok)]
    picked = own_routes == lax.broadcasted_iota(jnp.int32, (wide, tok), 0)
    earlier = lax.broadcasted_iota(jnp.int32, (tok, tok), 0) < lax.broadcasted_iota(jnp.int32, (tok, tok), 1)
    counts = dot(jnp.where(picked, 1.0, 0.0).astype(bf16), jnp.where(earlier, 1.0, 0.0).astype(bf16))
    rank = jnp.sum(jnp.where(picked, counts, 0.0), axis=0, keepdims=True)
    slot_of = own_routes.astype(f32) * slots + rank

    def place(step, carry):
        ids = lax.broadcasted_iota(jnp.int32, (STRIP, tok), 0) + step * STRIP
        at = pl.ds(pl.multiple_of(step * STRIP, STRIP), STRIP)
        placing[at] = jnp.where(ids.astype(f32) == slot_of, 1.0, 0.0).astype(bf16)
        return carry

    lax.fori_loop(0, total // STRIP, place, 0)

    positions = mp * tok + lax.broadcasted_iota(jnp.int32, (1, tok), 1)
    factors = pick_sequence(positions, (domains_ref, counts_ref, weights_ref, keep_ref))
    high = factors.astype(bf16)
    low = (factors - high.astype(f32)).astype(bf16)
    which = lax.broadcasted_iota(jnp.int32, (16, tok), 0)
    both = jnp.where(which == 0, high, jnp.where(which == 1, low, bf16(0)))
    spread = dot(both, placing[...], NT)

    def place_cot(step, carry):
        at = pl.ds(pl.multiple_of(step * STRIP, STRIP), STRIP)
        cot_send[at] = dot(placing[at], cot_ref[...]).astype(bf16)
        return carry

    lax.fori_loop(0, total // STRIP, place_cot, 0)
    spare = lax.broadcasted_iota(jnp.int32, (16, slots), 0) == cap - (slots - 16)
    for expert in range(experts):
        at = slice((expert + 1) * slots - 16, (expert + 1) * slots)
        here = slice(expert * slots, (expert + 1) * slots)
        for term, column in ((0, 0), (1, width // 2)):
            cot_send[at, column : column + slots] = jnp.where(
                spare, spread[term : term + 1, here], cot_send[at, column : column + slots].astype(f32)
            ).astype(bf16)

    def chunk(index):
        return pl.ds(pl.multiple_of(index * slots, 16), slots)

    def row_copy(target, source):
        return remote(
            cot_send.at[chunk(target)], cot_out.at[chunk(source)],
            row_send.at[target], row_recv.at[source], {"dp": target},
        )

    own_rows = pltpu.make_async_copy(cot_send.at[chunk(me)], cot_out.at[chunk(me)], local_sems.at[2])
    own_rows.start()
    same_side = [(me + k) % experts for k in range(2, experts, 2)]
    for other in same_side:
        row_copy(other, me).start()

    def turn(step, carry):
        at = pl.ds(pl.multiple_of(step * STRIP, STRIP), STRIP)
        placing_t[:, at] = placing[at].T
        return carry

    lax.fori_loop(0, total // STRIP, turn, 0)

    saves = []

    def save(source, target):
        copy = pltpu.make_async_copy(source, target, save_sems.at[len(saves)])
        copy.start()
        saves.append(copy)

    save(placing_t, placing_t_out)

    def pair_of(step):
        return (1 - chip) * step + chip * (PAIRS - 1 - step)

    def column(offset, pair):
        return pl.ds(pl.multiple_of((offset * PAIRS + pair) * PAIR, PAIR), PAIR)

    def project(step):
        pair = pair_of(step)
        weights = jnp.concatenate([heads[index, column(0, pair)] for index in range(3)])

        def strip_of(strip, carry):
            at = pl.ds(pl.multiple_of(strip * 512, 512), 512)
            value = dot(normed[pl.ds(pl.multiple_of(HALF + strip * 512, 512), 512)], weights, NT).astype(bf16)
            for index in range(3):
                qkv[at, column(index, pair)] = value[:, index * PAIR : (index + 1) * PAIR]
            return carry

        lax.fori_loop(0, 2 * tok // 512, strip_of, 0)

    lane = lax.broadcasted_iota(jnp.int32, (1, PAIR), 1)
    row = lax.broadcasted_iota(jnp.int32, (PAIR, 1), 0)

    def attend_blocks(pair, blocks):
        items = [(first, whole, head) for first, whole in blocks for head in range(2)]

        def start(first, whole, head):
            span = (whole + 1) * BLOCK
            near = pl.ds(pl.multiple_of(first + HALF - whole * BLOCK, BLOCK), span)
            queries = qkv[pl.ds(first, BLOCK), column(0, pair)] * bf16(0.125)
            own = jnp.where((lane // HEAD_DIM) == head, queries, bf16(0))
            return near, dot(keys[near], own, NT)

        waiting = start(*items[0])
        parts = []
        for index, (first, whole, head) in enumerate(items):
            near, scores = waiting
            if index + 1 < len(items):
                waiting = start(*items[index + 1])
            scores = mask_diagonal(scores, whole)
            largest = jnp.max(scores, axis=0, keepdims=True)
            expo = jnp.exp(scores - largest)
            summed = jnp.sum(expo, axis=0, keepdims=True)
            parts.append(dot(values[:, near], expo.astype(bf16)) / summed)
            at = pl.ds(first, BLOCK)
            logs[pair, head : head + 1, at] = largest + jnp.log(summed)
            if head:
                mixed[at, column(0, pair)] = jnp.where(row < HEAD_DIM, parts[-2], parts[-1]).T.astype(bf16)

    quarter = HALF // 2
    ext_rows = pl.ds(pl.multiple_of(core * quarter, quarter), quarter)
    ext_copy = remote(
        normed.at[pl.ds(pl.multiple_of(2 * tok + core * quarter, quarter), quarter)], normed.at[ext_rows],
        ext_sems.at[0, 0], ext_sems.at[1, 0], across,
    )
    ext_pass = remote(normed.at[ext_rows], normed.at[ext_rows], ext_sems.at[0, 1], ext_sems.at[1, 1], beside)
    w_local.wait()
    normed_copy.wait_recv()

    @pl.when(chip == 0)
    def _():
        ext_copy.start()

    w_in_copy.start()
    project(0)
    for index in range(4):
        w_copy(index).wait_recv()
        w_pass(index).start()

    def attention(step, carry):
        pair = pair_of(step)

        @pl.when(step == 1)
        def _():
            for index in range(3):
                w_pass(index).wait_recv()
            for other in [(me + k) % experts for k in range(1, experts, 2)]:
                row_copy(other, me).start()
            project(1)
            project(2)

        keys[HALF:] = qkv[:, column(1, pair)]
        values[:, HALF:] = qkv[:, column(2, pair)].T
        attend_blocks(pair, [(pl.multiple_of((2 * chip + whole) * BLOCK, BLOCK), whole) for whole in range(4)])

        @pl.when(chip == 0)
        def _():
            attend_blocks(pair, [(4 * BLOCK, 0), (5 * BLOCK, 1)])

        return carry

    lax.fori_loop(0, PAIRS, attention, 0)
    save(qkv, qkv_out)
    save(heads, heads_out)
    proj_local.wait()
    w_pass(3).wait_recv()
    proj_pass.start()
    save(proj.at[0], proj_out)

    @pl.when(second)
    def _():
        ext_copy.wait_recv()
        ext_pass.start()
        ext_pass.wait_recv()
        for index in range(2):
            ext[:, index * PAIRS * PAIR : (index + 1) * PAIRS * PAIR] = dot(
                normed[0:HALF], heads[1 + index], NT
            ).astype(bf16)

        def late(pair, carry):
            keys[0:HALF] = ext[:, column(0, pair)]
            keys[HALF : 2 * HALF] = qkv[0:HALF, column(1, pair)]
            values[:, 0:HALF] = ext[:, column(1, pair)].T
            values[:, HALF : 2 * HALF] = qkv[0:HALF, column(2, pair)].T
            attend_blocks(pair, [(0, 2), (BLOCK, 3)])
            return carry

        lax.fori_loop(0, PAIRS, late, 0)

    @pl.when(chip == 0)
    def _():
        ext_copy.wait_send()
        ext[...] = jnp.zeros_like(ext)
        normed[0:HALF] = jnp.zeros((HALF, width), bf16)

    @pl.when(second)
    def _():
        ext_pass.wait_send()

    save(normed, normed_out)
    save(ext, ext_out)
    save(mixed, mixed_out)
    save(logs, log_out)
    mixed_copy = remote(
        mixed.at[pl.ds(pl.multiple_of((1 - core) * tok, tok), tok)], mixed_far,
        mixed_sems.at[0], mixed_sems.at[1], beside,
    )
    mixed_copy.start()
    proj_pass.wait_recv()
    mixed_copy.wait_recv()

    def second_norm(step, carry):
        at = pl.ds(pl.multiple_of(step * STRIP, STRIP), STRIP)
        value = x_ref[at].astype(f32) + (
            dot(mixed[pl.ds(pl.multiple_of(mine + step * STRIP, STRIP), STRIP)], proj[0])
            + dot(mixed_far[at], proj[1])
        )
        hidden[at] = value
        scaled, _ = normalise(value)
        normed_two[at] = (scaled * gain_two_ref[...][None, :] + shift_two_ref[...][None, :]).astype(bf16)
        return carry

    lax.fori_loop(0, tok // STRIP, second_norm, 0)
    save(hidden, hidden_out)

    def place_rows(step, carry):
        at = pl.ds(pl.multiple_of(step * STRIP, STRIP), STRIP)
        rows[at] = dot(placing[at], normed_two[...]).astype(bf16)
        return carry

    lax.fori_loop(0, total // STRIP, place_rows, 0)
    save(rows, rows_out)
    own_rows.wait()
    for other in others:
        row_copy(me, other).wait_recv()
        row_copy(other, me).wait_send()
    for index in range(4):
        w_copy(index).wait_send()
        w_pass(index).wait_send()
    for copy in (proj_pass, normed_copy, mixed_copy):
        copy.wait_send()
    for copy in saves:
        copy.wait()
    w_in_copy.wait()


def run_forward(
    loss, x, cotangent, routes, gain_one, shift_one, gain_two, shift_two, w_heads, w_proj, w_in, experts, cap, slots
):
    tok, width = x.shape
    rows = 2 * tok
    total = experts * slots
    part = w_proj.shape[0]
    anyspace, vmem = pl.BlockSpec(memory_space=pl.ANY), pl.BlockSpec(memory_space=pltpu.VMEM)
    smem = pl.BlockSpec(memory_space=pltpu.SMEM)
    dma = pltpu.SemaphoreType.DMA
    kept = [
        ((HALF + rows, width), bf16),
        ((rows, 3 * PAIRS * PAIR), bf16),
        ((HALF, 2 * PAIRS * PAIR), bf16),
        ((rows, PAIRS * PAIR), bf16),
        ((PAIRS, 8, rows), f32),
        ((3, 2 * part, width), bf16),
    ]
    late = [((tok, width), f32), ((total, width), bf16)]
    return pl.pallas_call(
        functools.partial(forward_kernel, experts, slots, cap),
        in_specs=[smem] * 4 + [vmem] * 7 + [anyspace] * 3,
        out_specs=[anyspace] * 12,
        out_shape=[
            jax.ShapeDtypeStruct(*item)
            for item in kept
            + [((2 * part, width), bf16)]
            + late
            + [((total, width), bf16), ((tok, total), bf16), (w_in.shape, bf16)]
        ],
        scratch_shapes=[pltpu.VMEM(*item) for item in kept + [((2, 2 * part, width), bf16)] + late]
        + [
            pltpu.VMEM((total, tok), bf16),
            pltpu.VMEM((tok, total), bf16),
            pltpu.VMEM((total, width), bf16),
            pltpu.VMEM((tok, PAIRS * PAIR), bf16),
            pltpu.VMEM((tok, width), bf16),
            pltpu.VMEM((HALF + rows, PAIR), bf16),
            pltpu.VMEM((PAIR, HALF + rows), bf16),
            dma((2, 4)), dma((2, 4)), dma((2,)), dma((2,)), dma((2,)), dma((2, 2)), dma((2,)),
            dma((experts,)), dma((experts,)), dma((3,)), dma((10,)),
        ],
        compiler_params=pltpu.CompilerParams(
            collective_id=4, has_side_effects=True, vmem_limit_bytes=56 * 2**20
        ),
        cost_estimate=pl.CostEstimate(flops=30 * 10**9, bytes_accessed=30 * 10**6, transcendentals=8 * 10**6),
        name="forward",
    )(*loss, x, cotangent, routes, gain_one, shift_one, gain_two, shift_two, w_heads, w_proj, w_in)


def backward_kernel(
    experts, slots,
    domains_ref, counts_ref, weights_ref, keep_ref,
    hidden_ref, gain_one_ref, gain_two_ref, placing_ref, d_returned_ref, router_ref,
    cot_any, result_ref, there_in_ref, there_out_ref, mixed_any, proj_any, qkv_any, ext_any, log_any, normed_any, heads_any, x_any,
    output_ref, input_grad_ref, total_ref, small_ref, far_in_ref, far_out_ref,
    mixed_ref, proj_ref, qkv_ref, ext_ref, log_ref, normed_ref, heads_ref, x_ref, saved,
    summed, returned, d_hidden, d_branch, d_mixed, keys, values, d_keys, d_values, d_qkv, d_ext,
    grads_own, grads_send, grads_recv, d_norm, norm_recv, ext_recv,
    held, half_recv, piece_recv, small, first_slots, second_slots, last_slots,
    row_send, row_recv, branch_sems, norm_sems, ext_sems, far_sems, grad_sems,
    half_sems, piece_sems, gather_sems, back_sems, small_sems, load_sems, local_sems,
):
    me, mp = lax.axis_index("dp"), lax.axis_index("mp")
    chip, core = mp // 2, mp % 2
    tok, width = hidden_ref.shape
    rows = 2 * tok
    part = grads_own.shape[1]
    all_heads = PAIRS * PAIR
    beside = {"mp": mp + 1 - 2 * core}
    across = {"mp": (mp + 2) % 4}
    second = chip == 1
    others = [(me + k) % experts for k in range(1, experts)]
    diagonal = {"mp": 3 - mp}
    greet([{"dp": other} for other in others] + [beside, across, diagonal])

    def chunk(index):
        return pl.ds(pl.multiple_of(index * slots, 16), slots)

    def row_copy(target, source):
        return remote(
            result_ref.at[chunk(target)], returned.at[chunk(source)],
            row_send.at[target], row_recv.at[source], {"dp": target},
        )

    cot_copy = pltpu.make_async_copy(cot_any, grads_send, local_sems.at[1])
    cot_copy.start()
    loads = [
        pltpu.make_async_copy(source, target, load_sems.at[index])
        for index, (source, target) in enumerate(
            (
                (mixed_any, mixed_ref), (proj_any, proj_ref), (qkv_any, qkv_ref), (ext_any, ext_ref),
                (log_any, log_ref), (normed_any, normed_ref), (heads_any, heads_ref), (x_any, x_ref),
            )
        )
    ]
    for load in loads:
        load.start()
    far_half = there_in_ref.shape[0] // 2
    far_copies = [
        remote(
            there_out_ref.at[pl.ds(far_half, far_half)], far_out_ref, far_sems.at[0, 0], far_sems.at[1, 0], across
        )
    ] + [
        remote(
            there_in_ref.at[pl.ds(index * far_half, far_half)], far_in_ref.at[pl.ds(index * far_half, far_half)],
            far_sems.at[0, 1 + index], far_sems.at[1, 1 + index], across,
        )
        for index in range(2)
    ]
    far_copies[0].start()
    far_copies[1].start()
    own_rows = pltpu.make_async_copy(result_ref.at[chunk(me)], returned.at[chunk(me)], local_sems.at[0])
    own_rows.start()
    for other in others:
        row_copy(other, me).start()

    cot_copy.wait()
    small[...] = jnp.zeros_like(small)
    mine = pl.multiple_of(core * tok, tok)

    def second_norm(step, carry):
        at = pl.ds(pl.multiple_of(step * STRIP, STRIP), STRIP)
        scaled, inverse = normalise(hidden_ref[at])
        d_normed = dot(placing_ref[at], d_returned_ref[...])
        small[2:3] += jnp.sum(d_normed * scaled, axis=0, keepdims=True)
        small[3:4] += jnp.sum(d_normed, axis=0, keepdims=True)
        positions = mp * tok + step * STRIP + lax.broadcasted_iota(jnp.int32, (STRIP, 1), 0)
        total = grads_send[at].astype(f32) * pick_sequence(
            positions, (domains_ref, counts_ref, weights_ref, keep_ref)
        ) + norm_pull(
            d_normed, scaled, inverse, gain_two_ref[...][None, :]
        )
        d_hidden[at] = total
        d_branch[pl.ds(pl.multiple_of(mine + step * STRIP, STRIP), STRIP)] = total.astype(bf16)
        return carry

    lax.fori_loop(0, tok // STRIP, second_norm, 0)
    own_branch = d_branch.at[pl.ds(mine, tok)]
    branch_copy = remote(own_branch, own_branch, branch_sems.at[0], branch_sems.at[1], beside)
    branch_copy.start()

    for load in loads[:2]:
        load.wait()

    def push_branch(base):
        def push(step, carry):
            at = pl.ds(pl.multiple_of(base + step * STRIP, STRIP), STRIP)
            d_mixed[at] = dot(d_branch[at], proj_ref[...], NT).astype(bf16)
            return carry

        lax.fori_loop(0, tok // STRIP, push, 0)

    push_branch(mine)
    branch_copy.wait()
    push_branch((1 - core) * tok)

    side, line = me % 2, me // 2
    lines = experts // 2
    partner = {"dp": me + 1 - 2 * side}
    mates = [(line + k) % lines for k in range(1, lines)]
    piece_rows = held.shape[1] // lines
    own_columns = pl.ds(pl.multiple_of(side * (width // 2), 128), width // 2)
    other_columns = pl.ds(pl.multiple_of((1 - side) * (width // 2), 128), width // 2)

    def piece(index):
        return pl.ds(pl.multiple_of(index * piece_rows, 16), piece_rows)

    def sent(index):
        return slice(index * part, (index + 1) * part)

    def grad_copy(index):
        return remote(
            grads_send.at[sent(index)], grads_recv.at[index], grad_sems.at[0, index], grad_sems.at[1, index], across
        )

    def half_copy(index):
        return remote(
            held.at[index, :, other_columns], half_recv.at[index],
            half_sems.at[0, index], half_sems.at[1, index], partner,
        )

    def piece_copy(index, target, source):
        return remote(
            held.at[index, piece(target), own_columns], piece_recv.at[index, source],
            piece_sems.at[0, index, target], piece_sems.at[1, index, source], {"dp": 2 * target + side},
        )

    def gather_copy(index, target, source):
        block = total_ref.at[index, piece(source), own_columns]
        return remote(
            block, block,
            gather_sems.at[0, index, target], gather_sems.at[1, index, source], {"dp": 2 * target + side},
        )

    def back_copy(index):
        block = total_ref.at[index, :, own_columns]
        return remote(block, block, back_sems.at[0, index], back_sems.at[1, index], partner)

    def product(left, right, first):
        def block(step, carry):
            at = pl.ds(pl.multiple_of(first + step * PAIR, PAIR), PAIR)
            summed[pl.ds(pl.multiple_of(step * PAIR, PAIR), PAIR)] = dot(left[:, at], right[...], TN)
            return carry

        lax.fori_loop(0, PAIRS, block, 0)

    def send_grad(index):
        grads_own[index] = summed[pl.ds(pl.multiple_of(chip * part, 16), part)]
        grads_send[sent(index)] = summed[pl.ds(pl.multiple_of((1 - chip) * part, 16), part)].astype(bf16)

        grad_copy(index).start()

    chunks = held.shape[0]
    parts = 4 // chunks

    def stage_one(index):
        if index >= chunks:
            return
        for at in range(parts):
            number = index * parts + at
            grad_copy(number).wait_recv()
            held[index, at * part : (at + 1) * part] = (
                grads_own[number] + grads_recv[number].astype(f32)
            ).astype(bf16)
        if held.shape[1] > parts * part:
            held[index, parts * part :] = jnp.zeros((held.shape[1] - parts * part, width), bf16)
        half_copy(index).start()

    def stage_two(index):
        if index >= chunks:
            return
        half_copy(index).wait_recv()
        held[index, :, own_columns] = (
            held[index, :, own_columns].astype(f32) + half_recv[index].astype(f32)
        ).astype(bf16)
        for mate in mates:
            piece_copy(index, mate, line).start()

    def stage_three(index):
        if index >= chunks:
            return
        value = held[index, piece(line), own_columns].astype(f32)
        for mate in mates:
            piece_copy(index, line, mate).wait_recv()
            value += piece_recv[index, mate].astype(f32)
        total_ref[index, piece(line), own_columns] = value.astype(bf16)
        for mate in mates:
            gather_copy(index, mate, line).start()

    def stage_four(index):
        if index >= chunks:
            return
        for mate in mates:
            gather_copy(index, line, mate).wait_recv()
        back_copy(index).start()

    product(mixed_ref, d_branch, 0)
    send_grad(0)

    lane = lax.broadcasted_iota(jnp.int32, (1, PAIR), 1)

    def column(offset, pair):
        return pl.ds(pl.multiple_of((offset * PAIRS + pair) * PAIR, PAIR), PAIR)

    def attend_blocks(pair, blocks):
        for first, whole in blocks:
            span = (whole + 1) * BLOCK
            start = pl.multiple_of(first + HALF - whole * BLOCK, BLOCK)
            at = pl.ds(first, BLOCK)
            queries = qkv_ref[at, column(0, pair)] * bf16(0.125)
            d_out = d_mixed[at, column(0, pair)]
            near = keys[pl.ds(start, span)]
            near_values = values[pl.ds(start, span)]
            product = (d_out.astype(f32) * mixed_ref[at, column(0, pair)].astype(f32)).T
            dq = dk = dv = 0.0
            for head in range(2):
                here = (lane // HEAD_DIM) == head
                own = jnp.where(here, queries, bf16(0))
                d_own = jnp.where(here, d_out, bf16(0))
                delta = jnp.sum(product[HEAD_DIM * head : HEAD_DIM * (head + 1)], axis=0, keepdims=True)
                scores = mask_diagonal(dot(near, own, NT), whole)
                probs = jnp.exp(scores - log_ref[pair, head : head + 1, at])
                d_probs = dot(near_values, d_own, NT)
                d_scores = (probs * (d_probs - delta)).astype(bf16)
                dv = dv + dot(probs.astype(bf16), d_own)
                dk = dk + dot(d_scores, own)
                dq = dq + dot(d_scores, jnp.where(here, near, bf16(0)), TN)
            d_qkv[at, column(0, pair)] = (dq * 0.125).astype(bf16)
            d_keys[pl.ds(start, span)] += dk
            d_values[pl.ds(start, span)] += dv

    ext_part, norm_send = d_branch.at[tok : tok + HALF], d_branch.at[0:tok]
    ext_beside = remote(ext_part, ext_recv, ext_sems.at[0, 0], ext_sems.at[1, 0], beside)
    ext_across = remote(ext_part, ext_recv, ext_sems.at[0, 1], ext_sems.at[1, 1], across)
    for load in loads[2:5]:
        load.wait()

    @pl.when(second)
    def _():
        def early(pair, carry):
            keys[0:HALF] = ext_ref[:, column(0, pair)]
            keys[HALF : 2 * HALF] = qkv_ref[0:HALF, column(1, pair)]
            values[0:HALF] = ext_ref[:, column(1, pair)]
            values[HALF : 2 * HALF] = qkv_ref[0:HALF, column(2, pair)]
            d_keys[0 : 2 * HALF] = jnp.zeros((2 * HALF, PAIR), f32)
            d_values[0 : 2 * HALF] = jnp.zeros((2 * HALF, PAIR), f32)
            attend_blocks(pair, [(0, 2), (BLOCK, 3)])
            d_ext[:, column(0, pair)] = d_keys[0:HALF].astype(bf16)
            d_ext[:, column(1, pair)] = d_values[0:HALF].astype(bf16)
            saved[pair, :, 0:PAIR] = d_keys[HALF : 2 * HALF]
            saved[pair, :, PAIR:] = d_values[HALF : 2 * HALF]
            return carry

        lax.fori_loop(0, PAIRS, early, 0)

    for load in loads[5:7]:
        load.wait()

    @pl.when(second)
    def _():
        ext_part[...] = dot(d_ext[...], heads_ref[1:3].reshape(2 * all_heads, width)).astype(bf16)

    @pl.when(chip == 0)
    def _():
        d_ext[...] = jnp.zeros_like(d_ext)
        saved[...] = jnp.zeros_like(saved)

    @pl.when(mp == 2)
    def _():
        ext_beside.start()

    def attention(pair, carry):
        keys[HALF:] = qkv_ref[:, column(1, pair)]
        values[HALF:] = qkv_ref[:, column(2, pair)]
        d_keys[HALF : 2 * HALF] = saved[pair, :, 0:PAIR]
        d_keys[2 * HALF :] = jnp.zeros((rows - HALF, PAIR), f32)
        d_values[HALF : 2 * HALF] = saved[pair, :, PAIR:]
        d_values[2 * HALF :] = jnp.zeros((rows - HALF, PAIR), f32)
        attend_blocks(pair, [(pl.multiple_of((2 * chip + whole) * BLOCK, BLOCK), whole) for whole in range(4)])

        @pl.when(chip == 0)
        def _():
            attend_blocks(pair, [(4 * BLOCK, 0), (5 * BLOCK, 1)])

        @pl.when((mp == 3) & (pair == 0))
        def _():
            ext_beside.wait_recv()
            ext_part[...] = (ext_part[...].astype(f32) + ext_recv[...].astype(f32)).astype(bf16)
            ext_across.start()

        d_qkv[:, column(1, pair)] = d_keys[HALF:].astype(bf16)
        d_qkv[:, column(2, pair)] = d_values[HALF:].astype(bf16)
        return carry

    lax.fori_loop(0, PAIRS, attention, 0)

    product(d_qkv, normed_ref.at[HALF:], 0)
    send_grad(1)

    for index in (1, 2):
        product(d_qkv, normed_ref.at[HALF:], index * all_heads)

        @pl.when(second)
        def _():
            def block(step, carry):
                at = pl.ds(pl.multiple_of((index - 1) * all_heads + step * PAIR, PAIR), PAIR)
                summed[pl.ds(pl.multiple_of(step * PAIR, PAIR), PAIR)] += dot(d_ext[:, at], normed_ref[0:HALF], TN)
                return carry

            lax.fori_loop(0, PAIRS, block, 0)

        send_grad(1 + index)
    stage_one(0)

    weights = heads_ref[...].reshape(3 * all_heads, width)

    def push_norm(step, carry):
        at = pl.ds(pl.multiple_of((1 - core) * tok + step * STRIP, STRIP), STRIP)
        norm_send[pl.ds(pl.multiple_of(step * STRIP, STRIP), STRIP)] = dot(d_qkv[at], weights).astype(bf16)
        return carry

    def pull_norm(step, carry):
        at = pl.ds(pl.multiple_of(mine + step * STRIP, STRIP), STRIP)
        d_norm[pl.ds(pl.multiple_of(step * STRIP, STRIP), STRIP)] = dot(d_qkv[at], weights)
        return carry

    lax.fori_loop(0, tok // STRIP, push_norm, 0)
    norm_copy = remote(norm_send, norm_recv, norm_sems.at[0], norm_sems.at[1], beside)
    norm_copy.start()
    lax.fori_loop(0, tok // STRIP, pull_norm, 0)
    stage_two(0)
    own_rows.wait()
    for other in others:
        row_copy(me, other).wait_recv()

    def finish(step, carry):
        at = pl.ds(pl.multiple_of(step * STRIP, STRIP), STRIP)
        output_ref[at] = (hidden_ref[at] + dot(placing_ref[at], returned[...])).astype(bf16)
        return carry

    lax.fori_loop(0, tok // STRIP, finish, 0)
    stage_three(0)
    stage_one(1)
    norm_copy.wait_recv()
    loads[7].wait()

    @pl.when(mp == 1)
    def _():
        ext_across.wait_recv()
        d_norm[tok - HALF :] += ext_recv[...].astype(f32)

    def first_norm(step, carry):
        at = pl.ds(pl.multiple_of(step * STRIP, STRIP), STRIP)
        scaled, inverse = normalise(x_ref[at].astype(f32))
        d_normed = d_norm[at] + norm_recv[at].astype(f32)
        small[0:1] += jnp.sum(d_normed * scaled, axis=0, keepdims=True)
        small[1:2] += jnp.sum(d_normed, axis=0, keepdims=True)
        input_grad_ref[at] = (
            d_hidden[at] + norm_pull(d_normed, scaled, inverse, gain_one_ref[...][None, :])
        ).astype(bf16)
        return carry

    lax.fori_loop(0, tok // STRIP, first_norm, 0)
    stage_two(1)
    stage_one(2)

    small[4:5] = router_ref[...]
    rounds = [(first_slots, "dp", me, me - me % 8, 1, 8)]
    if experts > 8:
        rounds.append((second_slots, "dp", me, me % 8, 8, 8))
    rounds.append((last_slots, "mp", mp, mp - mp % 4, 1, 4))

    def small_copies(number, receiving):
        slots_of, axis, place, base, step, size = rounds[number]
        own = (place - base) // step
        copies = []
        for k in range(1, size):
            other = (own + k) % size
            source, target = (other, own) if receiving else (own, other)
            copies.append(
                remote(
                    slots_of.at[own], slots_of.at[source],
                    small_sems.at[0, number, target], small_sems.at[1, number, source],
                    {axis: base + other * step},
                )
            )
        return copies

    def small_start(number):
        for copy in small_copies(number, False):
            copy.start()

    def small_finish(number):
        for copy in small_copies(number, True):
            copy.wait_recv()
        slots_of, size = rounds[number][0], rounds[number][-1]
        value = slots_of[0]
        for index in range(1, size):
            value += slots_of[index]
        return value

    first_slots[me % 8] = small[...]
    small_start(0)
    stage_four(0)
    stage_three(1)
    stage_two(2)
    norms = small_finish(0)
    if experts > 8:
        second_slots[me // 8, 0:8] = norms
        for index in range(8):
            second_slots[me // 8, 8 + index : 9 + index] = first_slots[index, 4:5]
        small_start(1)
        norms = small_finish(1)
        for index in range(8):
            last_slots[mp % 4, 8 + 8 * index : 16 + 8 * index] = second_slots[index, 8:16]
    else:
        for index in range(8):
            last_slots[mp % 4, 8 + index : 9 + index] = first_slots[index, 4:5]
    last_slots[mp % 4, 0:8] = norms[0:8]
    small_start(len(rounds) - 1)
    far_copies[2].start()
    stage_one(3)
    stage_four(1)
    stage_three(2)
    stage_two(3)
    stage_four(2)
    stage_three(3)
    small_ref[...] = small_finish(len(rounds) - 1)
    stage_four(3)
    for index in range(chunks):
        other = total_ref.at[index, :, other_columns]
        remote(other, other, back_sems.at[0, index], back_sems.at[1, index], partner).wait_recv()

    for other in others:
        row_copy(other, me).wait_send()
    for mate in mates:
        for index in range(chunks):
            piece_copy(index, mate, line).wait_send()
            gather_copy(index, mate, line).wait_send()
    for index in range(4):
        grad_copy(index).wait_send()
    for index in range(chunks):
        half_copy(index).wait_send()
        back_copy(index).wait_send()
    for number in range(len(rounds)):
        for copy in small_copies(number, False):
            copy.wait_send()
    norm_copy.wait_send()

    @pl.when(mp == 2)
    def _():
        ext_beside.wait_send()

    @pl.when(mp == 3)
    def _():
        ext_across.wait_send()

    for copy in far_copies:
        copy.wait()


def run_backward(
    loss, x, cotangent, hidden, gain_one, gain_two, placing, d_returned, result, normed, qkv, ext,
    mixed, log_total, heads, proj, router_grad, there_in, there_out, experts,
):
    tok, width = x.shape
    rows = 2 * tok
    total = d_returned.shape[0]
    part = proj.shape[0] // 2
    lines = experts // 2
    steps = 2 if experts <= 8 else 3
    chunks = 4 if part % (16 * lines) == 0 else 2
    padded = (4 // chunks * part + 16 * lines - 1) // (16 * lines) * (16 * lines)
    small = (8 + max(8, experts), width)
    anyspace, vmem = pl.BlockSpec(memory_space=pl.ANY), pl.BlockSpec(memory_space=pltpu.VMEM)
    smem = pl.BlockSpec(memory_space=pltpu.SMEM)
    dma = pltpu.SemaphoreType.DMA
    return pl.pallas_call(
        functools.partial(backward_kernel, experts, total // experts),
        in_specs=[smem] * 4 + [vmem] * 6 + [anyspace] * 12,
        out_specs=[vmem] * 4 + [anyspace] * 2,
        out_shape=[
            jax.ShapeDtypeStruct((tok, width), bf16),
            jax.ShapeDtypeStruct((tok, width), bf16),
            jax.ShapeDtypeStruct((chunks, padded, width), bf16),
            jax.ShapeDtypeStruct(small, f32),
            jax.ShapeDtypeStruct(there_in.shape, bf16),
            jax.ShapeDtypeStruct((there_out.shape[0] // 2, width), bf16),
        ],
        scratch_shapes=[
            pltpu.VMEM(item.shape, item.dtype) for item in (mixed, proj, qkv, ext, log_total, normed, heads, x)
        ]
        + [
            pltpu.VMEM((PAIRS, HALF, 2 * PAIR), f32),
            pltpu.VMEM((PAIRS * PAIR, width), f32),
            pltpu.VMEM((total, width), bf16),
            pltpu.VMEM((tok, width), f32),
            pltpu.VMEM((rows, width), bf16),
            pltpu.VMEM((rows, PAIRS * PAIR), bf16),
            pltpu.VMEM((HALF + rows, PAIR), bf16),
            pltpu.VMEM((HALF + rows, PAIR), bf16),
            pltpu.VMEM((HALF + rows, PAIR), f32),
            pltpu.VMEM((HALF + rows, PAIR), f32),
            pltpu.VMEM((rows, 3 * PAIRS * PAIR), bf16),
            pltpu.VMEM((HALF, 2 * PAIRS * PAIR), bf16),
            pltpu.VMEM((4, part, width), f32),
            pltpu.VMEM((4 * part, width), bf16),
            pltpu.VMEM((4, part, width), bf16),
            pltpu.VMEM((tok, width), f32),
            pltpu.VMEM((tok, width), bf16),
            pltpu.VMEM((HALF, width), bf16),
            pltpu.VMEM((chunks, padded, width), bf16),
            pltpu.VMEM((chunks, padded, width // 2), bf16),
            pltpu.VMEM((chunks, lines, padded // lines, width // 2), bf16),
            pltpu.VMEM((8, width), f32),
            pltpu.VMEM((8, 8, width), f32),
            pltpu.VMEM((8, 16, width), f32),
            pltpu.VMEM((4,) + small, f32),
            dma((experts,)), dma((experts,)), dma((2,)), dma((2,)), dma((2, 2)), dma((2, 3)), dma((2, 4)),
            dma((2, chunks)), dma((2, chunks, lines)), dma((2, chunks, lines)), dma((2, chunks)),
            dma((2, steps, 8)), dma((8,)), dma((2,)),
        ],
        compiler_params=pltpu.CompilerParams(
            collective_id=2, has_side_effects=True, vmem_limit_bytes=62 * 2**20
        ),
        cost_estimate=pl.CostEstimate(flops=30 * 10**9, bytes_accessed=30 * 10**6, transcendentals=8 * 10**6),
        name="backward",
    )(
        *loss, hidden, gain_one, gain_two, placing, d_returned, router_grad,
        cotangent, result, there_in, there_out, mixed, proj, qkv, ext, log_total, normed, heads, x,
    )


def gelu_parts(pre):
    scale = 0.7978845608028654
    square = pre * pre
    inner = jnp.tanh(pre * (scale + (scale * 0.044715) * square))
    half = 0.5 * (1.0 + inner)
    slope = half + (0.5 * pre) * (1.0 - inner * inner) * (scale + (3.0 * scale * 0.044715) * square)
    return pre * half, slope

STAGES = 4

def expert_kernel(
    experts, slots, cap,
    rows_ref, cot_ref, router_ref, w_in_ref, w_out_ref, w_in_far_ref,
    back_ref, result_out, router_grad_ref, here_in_ref, here_out, there_in_ref, there_out_ref, far_grad_ref,
    result, here_out_held, router, factor, x, wi, wo, d_out, act, d_pre, total, d_x, give, g_send, g_recv,
    row_send, row_recv, back_send, back_recv, w_send, w_recv, g_send_sem, g_recv_sem, far_sems, save_sems, local_sem,
):
    me = lax.axis_index("dp")
    mp = lax.axis_index("mp")
    beside = {"mp": mp + 1 - 2 * (mp % 2)}
    across = {"mp": (mp + 2) % 4}
    members = experts // STAGES
    span = members * slots
    own_group, own_member = me // members, me % members

    def group_of(stage):
        return 2 * ((own_group // 2 + stage // 2) % 2) + (own_group % 2 + stage % 2) % 2

    def chunk(index):
        return pl.ds(pl.multiple_of(index * slots, 16), slots)

    def group_rows(group):
        return pl.ds(pl.multiple_of(group * span, 16), span)

    barrier = pltpu.get_barrier_semaphore()

    def greet(step, carry):
        pl.semaphore_signal(barrier, inc=1, device_id={"dp": (me + step) % experts}, device_id_type=MESH)
        return carry

    lax.fori_loop(1, experts, greet, 0)
    pl.semaphore_signal(barrier, inc=1, device_id=beside, device_id_type=MESH)
    pl.semaphore_signal(barrier, inc=1, device_id=across, device_id_type=MESH)
    pl.semaphore_wait(barrier, experts + 1)

    def remote(src, dst, send, recv, device):
        return pltpu.make_async_remote_copy(
            src_ref=src, dst_ref=dst, send_sem=send, recv_sem=recv, device_id=device, device_id_type=MESH
        )

    def row_copy(target, source):
        return remote(rows_ref.at[chunk(target)], x.at[chunk(source)], row_send.at[target], row_recv.at[source], {"dp": target})

    def back_copy(target, source):
        return remote(give.at[chunk(target)], back_ref.at[chunk(source)], back_send.at[target], back_recv.at[source], {"dp": target})

    def partners(stage):
        group = group_of(stage)
        if stage == 0:
            return [group * members + (own_member + k) % members for k in range(1, members)]
        return [group * members + (own_member + k) % members for k in range(members)]

    for stage in (3, 0, 1):
        for other in partners(stage):
            row_copy(other, me).start()
    own_rows = pltpu.make_async_copy(rows_ref.at[chunk(me)], x.at[chunk(me)], local_sem.at[0])
    own_in = pltpu.make_async_copy(w_in_ref, wi.at[0], local_sem.at[1])
    own_out = pltpu.make_async_copy(w_out_ref, wo.at[0], local_sem.at[2])
    far_in = pltpu.make_async_copy(w_in_far_ref, wi.at[2], local_sem.at[3])
    near_in = remote(w_in_ref, wi.at[1], w_send.at[0], w_recv.at[0], beside)
    near_out = remote(w_out_ref, wo.at[1], w_send.at[1], w_recv.at[1], beside)
    far_near_in = remote(w_in_far_ref, wi.at[3], w_send.at[2], w_recv.at[2], beside)
    far_out = remote(w_out_ref, wo.at[2], w_send.at[3], w_recv.at[3], across)
    far_near_out = remote(wo.at[2], wo.at[3], w_send.at[4], w_recv.at[4], beside)
    for copy in (own_rows, own_in, own_out, near_in, near_out, far_in, far_out, far_near_in):
        copy.start()
    router_grad_ref[...] = jnp.zeros_like(router_grad_ref)
    router[...] = router_ref[...].astype(f32)

    diagonal = lax.broadcasted_iota(jnp.int32, (slots, slots), 0) == lax.broadcasted_iota(
        jnp.int32, (slots, slots), 1
    )

    def prepare(stage, rows):
        for member in range(members):
            index = group_of(stage) * members + member
            spare = cot_ref[pl.ds(pl.multiple_of((index + 1) * slots - 16, 16), 16)].astype(f32)
            spare = spare[cap - slots + 16 : cap - slots + 17]
            value = spare[:, 0:slots] + spare[:, x.shape[1] // 2 : x.shape[1] // 2 + slots]
            factor[chunk(index)] = jnp.sum(jnp.where(diagonal, value, 0.0), axis=1, keepdims=True)
        features = x[rows].astype(f32)
        gate = jax.nn.sigmoid(jnp.sum(features * router[pl.ds(me, 1)], axis=1, keepdims=True))
        d_out[rows] = (gate * (cot_ref[rows].astype(f32) * factor[rows])).astype(bf16)
        total[rows] = jnp.zeros((span, x.shape[1]), f32)
        d_x[rows] = jnp.zeros((span, x.shape[1]), f32)

    def finish(stage, rows):
        features = x[rows].astype(f32)
        gate = jax.nn.sigmoid(jnp.sum(features * router[pl.ds(me, 1)], axis=1, keepdims=True))
        value = total[rows]
        d_gate = jnp.sum(cot_ref[rows].astype(f32) * factor[rows] * value, axis=1, keepdims=True)
        d_logit = (d_gate * gate * (1.0 - gate)).astype(bf16).astype(f32)
        give[rows] = (d_x[rows] + d_logit * router[pl.ds(me, 1)]).astype(bf16)
        result[rows] = (gate * value).astype(bf16)
        router_grad_ref[...] += jnp.sum(features * d_logit, axis=0, keepdims=True)

    def stage_of(step):
        near = jnp.where(step < 2, 0, jnp.where(step < 4, 1, 3))
        return jnp.where(step < 8, near, jnp.where(step < 12, 2, jnp.where(step < 14, 1, 0)))

    def step_body(step, carry):
        stage = stage_of(step)
        part = jnp.where(step < 6, step % 2, jnp.where((step < 8) | (step >= 12), 2 + step % 2, step - 8))
        rows = group_rows(group_of(stage))

        for static, at in enumerate((0, 2, 8, 4)):
            @pl.when(step == at)
            def _():
                if static == 0:
                    own_rows.wait()
                for other in partners(static):
                    row_copy(me, other).wait_recv()
        @pl.when((step == 0) | (step == 2) | (step == 4) | (step == 8))
        def _():
            prepare(stage, rows)

        @pl.when(step == 1)
        def _():
            for other in partners(2):
                row_copy(other, me).start()

        @pl.when(step == 0)
        def _():
            own_in.wait()
            own_out.wait()

        @pl.when(step == 1)
        def _():
            near_in.wait_recv()
            near_out.wait_recv()

        @pl.when(step == 6)
        def _():
            far_in.wait()
            far_out.wait_recv()
            far_near_out.start()

        @pl.when(step == 7)
        def _():
            far_near_in.wait_recv()
            far_near_out.wait_recv()

        pre = dot(x[rows], wi[part])
        value, slope = gelu_parts(pre)
        value = value.astype(bf16)
        act[part, rows] = value
        total[rows] += dot(value, wo[part])
        d_value = (dot(d_out[rows], wo[part], NT) * slope).astype(bf16)
        d_pre[part, rows] = d_value
        d_x[rows] += dot(d_value, wi[part], NT)

        @pl.when((step == 7) | (step == 11) | (step == 13) | (step == 15))
        def _():
            finish(stage, rows)

        for static, at in enumerate((15, 13, 11, 7)):
            @pl.when(step == at)
            def _():
                for other in partners(static):
                    back_copy(other, me).start()
        return carry

    lax.fori_loop(0, 16, step_body, 0)
    own_back = pltpu.make_async_copy(give.at[chunk(me)], back_ref.at[chunk(me)], local_sem.at[4])
    own_back.start()
    result_save = pltpu.make_async_copy(result, result_out, save_sems.at[0])
    result_save.start()

    kept = pl.ds(0, x.shape[1])
    outgoing = [g_send, act.at[3, kept], d_pre.at[3, kept], act.at[1, kept]]

    def product(left, right, store):
        def block(step, carry):
            at = pl.ds(pl.multiple_of(step * STRIP, STRIP), STRIP)
            store(at, dot(left[:, at], right[...], TN))
            return carry

        lax.fori_loop(0, x.shape[1] // STRIP, block, 0)

    def keep(target):
        def store(at, value):
            target[at] = value.astype(target.dtype)

        return store

    def grad_copy(index):
        return remote(outgoing[index], g_recv.at[index], g_send_sem.at[index], g_recv_sem.at[index], beside)

    product(act.at[3], d_out, keep(outgoing[0]))
    grad_copy(0).start()
    product(act.at[2], d_out, keep(total))
    product(x, d_pre.at[3], keep(outgoing[1]))
    grad_copy(1).start()
    grad_copy(0).wait_recv()
    there_out_ref[...] = (total[kept] + g_recv[0].astype(f32)).astype(bf16)
    early = pl.ds(0, far_grad_ref.shape[0])
    far_grad = remote(there_out_ref.at[early], far_grad_ref, far_sems.at[0], far_sems.at[1], across)
    far_grad.start()
    product(act.at[1], d_out, keep(outgoing[2]))
    grad_copy(2).start()
    product(x, d_pre.at[1], keep(outgoing[3]))
    grad_copy(3).start()
    product(x, d_pre.at[2], keep(d_x))
    product(act.at[0], d_out, keep(here_out_held))
    product(x, d_pre.at[0], keep(here_in_ref))
    grad_copy(1).wait_recv()
    there_in_ref[...] = (d_x[kept] + g_recv[1].astype(f32)).astype(bf16)
    grad_copy(2).wait_recv()
    here_out_held[...] += g_recv[2].astype(f32)
    here_save = pltpu.make_async_copy(here_out_held, here_out, save_sems.at[1])
    here_save.start()
    grad_copy(3).wait_recv()
    here_in_ref[...] += g_recv[3].astype(f32)

    result_save.wait()
    here_save.wait()
    own_back.wait()
    for stage in range(STAGES):
        for other in partners(stage):
            back_copy(me, other).wait_recv()
            back_copy(other, me).wait_send()
            row_copy(other, me).wait_send()
    for copy in (near_in, near_out, far_near_in, far_out, far_near_out):
        copy.wait_send()
    for index in range(4):
        grad_copy(index).wait_send()
    far_grad.wait()


def run_expert(rows, cot_rows, router, w_in, w_out, w_in_far, experts, cap):
    total, width = rows.shape
    slots = total // experts
    hidden = w_in.shape[1]
    anyspace, vmem = pl.BlockSpec(memory_space=pl.ANY), pl.BlockSpec(memory_space=pltpu.VMEM)
    dma = pltpu.SemaphoreType.DMA
    return pl.pallas_call(
        functools.partial(expert_kernel, experts, slots, cap),
        in_specs=[anyspace, vmem, vmem, anyspace, anyspace, anyspace],
        out_specs=[anyspace, anyspace, vmem, vmem, anyspace, vmem, vmem, anyspace],
        out_shape=[
            jax.ShapeDtypeStruct((total, width), bf16),
            jax.ShapeDtypeStruct((total, width), bf16),
            jax.ShapeDtypeStruct((1, width), f32),
            jax.ShapeDtypeStruct((width, hidden), f32),
            jax.ShapeDtypeStruct((hidden, width), f32),
            jax.ShapeDtypeStruct((width, hidden), bf16),
            jax.ShapeDtypeStruct((hidden, width), bf16),
            jax.ShapeDtypeStruct((hidden // 2, width), bf16),
        ],
        scratch_shapes=[
            pltpu.VMEM((total, width), bf16),
            pltpu.VMEM((hidden, width), f32),
            pltpu.VMEM(router.shape, f32),
            pltpu.VMEM((total, 1), f32),
            pltpu.VMEM((total, width), bf16),
            pltpu.VMEM((4, width, hidden), bf16),
            pltpu.VMEM((4, hidden, width), bf16),
            pltpu.VMEM((total, width), bf16),
            pltpu.VMEM((4, total, hidden), bf16),
            pltpu.VMEM((4, total, hidden), bf16),
            pltpu.VMEM((total, width), f32),
            pltpu.VMEM((total, width), f32),
            pltpu.VMEM((total, width), bf16),
            pltpu.VMEM((width, width), bf16),
            pltpu.VMEM((4, width, width), bf16),
            dma((experts,)), dma((experts,)), dma((experts,)), dma((experts,)),
            dma((5,)), dma((5,)), dma((4,)), dma((4,)), dma((2,)), dma((2,)), dma((5,)),
        ],
        compiler_params=pltpu.CompilerParams(
            collective_id=1, has_side_effects=True, vmem_limit_bytes=60 * 2**20
        ),
        cost_estimate=pl.CostEstimate(flops=30 * 10**9, bytes_accessed=40 * 10**6, transcendentals=3 * 10**6),
        name="expert",
    )(rows, cot_rows, router, w_in, w_out, w_in_far)


def shards(
    inputs, cotangent, routes, domains, domain_counts, domain_weights, keep_mask, gain_one, shift_one,
    w_qkv, w_proj, gain_two, shift_two, w_router, w_in, w_out,
):
    tok, width = inputs.shape
    experts = w_router.shape[1]
    cap = max(2, tok * 5 // (4 * experts))
    slots = (cap + 16) // 16 * 16
    loss = (domains, domain_counts, domain_weights, keep_mask)
    w_own = jnp.transpose(w_qkv, (1, 2, 0))
    normed, qkv, ext, mixed, log_total, heads, proj, hidden, rows, cot_rows, placing_t, w_in_far = run_forward(
        loss, inputs, cotangent, routes.reshape(1, -1), gain_one, shift_one, gain_two,
        shift_two, w_own, w_proj, w_in[0], experts, cap, slots,
    )
    d_returned, result, router_grad, here_in, here_out, there_in, there_out, far_early = run_expert(
        rows, cot_rows, w_router.T, w_in[0], w_out[0], w_in_far, experts, cap
    )
    output, input_grad, sums, small, far_in, far_out = run_backward(
        loss, inputs, cotangent, hidden, gain_one, gain_two, placing_t, d_returned, result,
        normed, qkv, ext, mixed, log_total, heads, proj, router_grad, there_in, there_out, experts,
    )
    part = w_proj.shape[0]
    sums = sums[:, : 4 * part // sums.shape[0]].reshape(4, part, -1)
    return (
        output,
        input_grad,
        small[0],
        small[1],
        jnp.transpose(sums[1:].astype(f32), (2, 0, 1)),
        sums[0].astype(f32),
        small[2],
        small[3],
        small[8 : 8 + experts].T,
        (here_in + far_in.astype(f32))[None],
        (here_out + jnp.concatenate([far_early, far_out]).astype(f32))[None],
    )


def solution(mesh):
    tokens, group = P(("dp", "mp"), None), P("dp")
    return jax.shard_map(
        shards,
        mesh=mesh,
        in_specs=(
            tokens, tokens, P("dp", None), group, P(), P(), group, P(), P(),
            P(None, None, "mp"), P("mp", None), P(), P(), P(),
            P("dp", None, "mp"), P("dp", "mp", None),
        ),
        out_specs=(
            tokens, tokens, P(), P(), P(None, None, "mp"), P("mp", None), P(), P(), P(),
            P("dp", None, "mp"), P("dp", "mp", None),
        ),
        check_vma=False,
    )
```
